256 devices in a mesh: blk: 64 (over y_lo, z, x), row: 4 (over y_hi, core).
Axes of the slice: x: 4, y: 4 (y_hi: 2, y_lo: 2; y = y_hi * 2 + y_lo), z: 8, core: 2. Of those that a mesh axis runs over, the one named last changes fastest.
Arguments:
- transmission: float32 [16384, 2, 8192], P(('blk', 'row')), may hold values from -64 to 64, as said below
- assignment: int32 [256], replicated, may hold values from 0 to 255, each once
- pairing: int32 [2, 64], replicated, may hold values from 0 to 2
Outputs:
- rotated: float32 [16384, 2, 8192], P(('blk', 'row'))
The draws below stay inside these ranges and needn't reach their ends.
Inputs may be any that keep to these rules, and one draw needn't show every extreme that they name: `transmission`: entries are real and imaginary parts of a measured speckle field; columns and rows have differing gains. `assignment`: A permutation of the block numbers.
All inputs are finite; a program needn't handle non-finite values.
Results may differ from the reference program's by a relative error of at most 0.00016.
Values sent between devices are 32-bit elements; how exact they have to be, the bound alone decides.
A program may use at most 128 MiB of HBM per device.

```python
import math
import jax
import jax.numpy as jnp
from jax import lax

ROWS = 16384
BLOCK = 32
SLOTS = 4
ROUNDS = 2
NS_STEPS = 6
BLK_DEVS = 64
BLOCKS = 256
COLS = 8192


def draw_transmission(key, part):
    key = jax.random.fold_in(key, 11)
    first, second, third = jax.random.split(key, 3)
    field = jnp.clip(jax.random.normal(first, (ROWS, 2, COLS), jnp.float32), -5.0, 5.0)
    low_gain, high_gain = (0.3, 3.0)
    row_gain = jnp.exp(jax.random.uniform(second, (ROWS, 1, 1), jnp.float32, math.log(low_gain), math.log(high_gain)))
    col_gain = jnp.exp(jax.random.uniform(third, (1, 1, COLS), jnp.float32, math.log(low_gain), math.log(high_gain)))
    return field * row_gain * col_gain


def place_ends(entries, own_key, low, largest):
    longest = entries.shape.index(max(entries.shape))
    spots = []
    for shift in (0, 1):
        where = [jax.random.randint(jax.random.fold_in(own_key, axis), (), 0, length) for axis, length in enumerate(entries.shape)]
        where[longest] = (where[longest] + shift) % entries.shape[longest]
        spots.append(tuple(where))
    return entries.at[spots[0]].set(low).at[spots[1]].set(largest)


def setup_inputs(seed: int = 0) -> dict:
    splits = jax.random.split(jax.random.key(seed), 4)
    transmission = draw_transmission(jax.random.fold_in(splits[3], 71), 0)
    assignment = jax.random.permutation(splits[1], BLOCKS).astype(jnp.int32)
    pairing = place_ends(jax.random.randint(splits[2], (ROUNDS, BLK_DEVS), 0, 3), jax.random.fold_in(splits[2], 1), 0, 2).astype(jnp.int32)
    return {"transmission": transmission, "assignment": assignment, "pairing": pairing}


def pair_rotation(gram):
    half = gram.shape[0] // 2
    real_part = gram[:half, :half] + gram[half:, half:]
    imag_part = gram[:half, half:] - gram[half:, :half]
    kernel = jnp.concatenate([jnp.concatenate([real_part, imag_part], axis=1), jnp.concatenate([-imag_part, real_part], axis=1)], axis=0)
    scale = jnp.sqrt(jnp.sum(kernel * kernel))
    eye = jnp.eye(kernel.shape[0], dtype=jnp.float32)
    upper = kernel / scale
    lower = eye
    for step in range(NS_STEPS):
        middle = 1.5 * eye - 0.5 * jnp.dot(lower, upper, precision=lax.Precision.HIGHEST)
        upper = jnp.dot(upper, middle, precision=lax.Precision.HIGHEST)
        lower = jnp.dot(middle, lower, precision=lax.Precision.HIGHEST)
    return lower * jnp.sqrt(ROWS / scale)

def reference(transmission, assignment, pairing):
    orders = jnp.array([[0, 1, 2, 3], [0, 2, 1, 3], [0, 3, 1, 2]], dtype=jnp.int32)
    blocks = transmission.reshape(ROWS, 2, BLOCKS, BLOCK).transpose(2, 0, 1, 3)
    held = assignment.reshape(BLK_DEVS, SLOTS)
    for rnd in range(ROUNDS):
        order = orders[pairing[rnd]]
        ids = jnp.take_along_axis(held, order, axis=1)
        first_ids = ids[:, jnp.array([0, 2])].reshape(-1)
        second_ids = ids[:, jnp.array([1, 3])].reshape(-1)
        start = blocks

        def one_pair(index, current):
            left = start[first_ids[index]]
            right = start[second_ids[index]]
            joined = jnp.concatenate([left[:, 0], right[:, 0], left[:, 1], right[:, 1]], axis=1)
            gram = jnp.dot(joined.T, joined, precision=lax.Precision.HIGHEST)
            turned = jnp.dot(joined, pair_rotation(gram), precision=lax.Precision.HIGHEST)
            new_left = jnp.stack([turned[:, :BLOCK], turned[:, 2 * BLOCK:3 * BLOCK]], axis=1)
            new_right = jnp.stack([turned[:, BLOCK:2 * BLOCK], turned[:, 3 * BLOCK:]], axis=1)
            current = current.at[first_ids[index]].set(new_left)
            return current.at[second_ids[index]].set(new_right)
        blocks = lax.fori_loop(0, first_ids.shape[0], one_pair, blocks)
        if rnd < ROUNDS - 1:
            held = jnp.stack([held[:, 0], jnp.roll(held[:, 1], 1), jnp.roll(held[:, 2], -1), held[:, 3]], axis=1)
    return blocks.transpose(1, 2, 0, 3).reshape(ROWS, 2, COLS)
```

```python
import functools

import jax
import jax.numpy as jnp
from jax import lax
from jax.experimental import pallas as pl
from jax.experimental.pallas import tpu as pltpu
from jax.sharding import PartitionSpec as P

ROWS = 16384
BLOCK = 32
SLOTS = 4
NS_STEPS = 6
UNITS = 64
BLOCKS = 256
MESH = pl.DeviceIdType.MESH
F32 = jnp.float32
BF16 = jnp.bfloat16
NX, NY, NZ = 4, 4, 8
NXY = NX * NY
CHUNK = UNITS // 2 // NXY
SLICE = 64 // NZ
PARAMS = functools.partial(pltpu.CompilerParams, vmem_limit_bytes=56 * 1024 * 1024)


def pair_blocks(assign, pairing, rnd, d, h):
    pick = pairing[rnd, d]
    if h == 0:
        slots = (0, 1 + pick)
    else:
        slots = (jnp.where(pick == 0, 2, 1), jnp.where(pick == 2, 2, 3))

    def block(slot):
        index = d
        if rnd == 1:
            turn = jnp.where(slot == 1, -1, jnp.where(slot == 2, 1, 0))
            index = lax.rem(d + turn + UNITS, UNITS)
        return assign[index * SLOTS + slot]

    return block(slots[0]), block(slots[1])


def lanes_of(shape):
    return lax.broadcasted_iota(jnp.int32, shape, 1)


def rows_of(shape):
    return lax.broadcasted_iota(jnp.int32, shape, 0)


def split(value):
    high = value.astype(BF16)
    return high, (value - high.astype(F32)).astype(BF16)


def turned(pair):
    rolled = pltpu.roll(pair, 64, 1)
    return jnp.where(lanes_of(pair.shape) < 64, rolled, -rolled)


def unpack(unit):
    lane, row = lanes_of(unit.shape), rows_of(unit.shape)
    left = lane < 64
    column = jnp.where(left, lane, lane - 64)
    flipped = jnp.concatenate([unit, unit], axis=0).T
    rolled = pltpu.roll(unit, 64, 1)
    tops = []
    for h in range(2):
        here = jnp.where(left, unit, rolled) if h == 0 else jnp.where(left, rolled, unit)
        there = flipped[64 * h : 64 * h + 64]
        real = jnp.where(row <= column, here, there)
        imag = jnp.where(row > column, here, jnp.where(row < column, -there, 0.0))
        tops.append(jnp.where(left, real, imag))
    return tops


def pack(first, second):
    lane, row = lanes_of(first.shape), rows_of(first.shape)
    left = lane < 64
    packed_first = jnp.where(row <= lane, first, pltpu.roll(first, 64, 1))
    packed_second = jnp.where(row <= lane - 64, pltpu.roll(second, 64, 1), second)
    return jnp.where(left, packed_first, packed_second)


def both(pair):
    return jnp.concatenate([pair, turned(pair)], axis=0)


def nt_dot(a, b):
    return lax.dot_general(a, b, (((1,), (1,)), ((), ())), preferred_element_type=F32)


def gram_top(pair):
    high, low = split(both(pair))
    lhs = jnp.concatenate([high[:64], low[:64]], axis=1)
    rhs = jnp.concatenate([high, high], axis=1)
    return nt_dot(lhs, rhs) + nt_dot(high[:64], low)


def applied(top, pair):
    high, low = split(both(pair))
    whigh, wlow = split(top)
    lhs = jnp.concatenate([whigh, wlow], axis=1)
    rhs = jnp.concatenate([high, high], axis=0)
    return jnp.dot(lhs, rhs, preferred_element_type=F32) + jnp.dot(
        whigh, low, preferred_element_type=F32
    )


def load_pair(table, a, b):
    return jnp.concatenate([table[a], table[b]], axis=0)


def grams(assign, pairing, rnd, table, packed):
    def unit(d, carry):
        tops = []
        for h in range(2):
            a, b = pair_blocks(assign, pairing, rnd, d, h)
            tops.append(gram_top(load_pair(table, a, b)))
        packed[d] = pack(*tops)
        return carry

    lax.fori_loop(0, UNITS, unit, 0, unroll=2)


def apply_all(assign, pairing, rnd, weights, source, target):
    def unit(d, carry):
        tops = unpack(weights[d])
        for h in range(2):
            a, b = pair_blocks(assign, pairing, rnd, d, h)
            new = applied(tops[h], load_pair(source, a, b))
            target[a] = new[:BLOCK]
            target[b] = new[BLOCK:]
        return carry

    lax.fori_loop(0, UNITS, unit, 0, unroll=2)


def first_kernel(assign, pairing, x, table, packed):
    def tile(ct, carry):
        real = x[pl.ds(2 * ct, 64, stride=128), :]
        imag = x[pl.ds(2 * ct + 1, 64, stride=128), :]
        flipped = jnp.concatenate([real, imag], axis=0).T
        table[pl.ds(4 * ct, 4)] = flipped.reshape(4, BLOCK, 128)
        return carry

    lax.fori_loop(0, 64, tile, 0, unroll=2)
    grams(assign, pairing, 0, table, packed)


def middle_kernel(assign, pairing, weights, source, table, packed):
    apply_all(assign, pairing, 0, weights, source, table)
    grams(assign, pairing, 1, table, packed)


def last_kernel(assign, pairing, weights, source, out, table):
    apply_all(assign, pairing, 1, weights, source, table)

    def tile(ct, carry):
        flipped = table[pl.ds(4 * ct, 4)].reshape(128, 128).T
        out[pl.ds(2 * ct, 64, stride=128), :] = flipped[:64]
        out[pl.ds(2 * ct + 1, 64, stride=128), :] = flipped[64:]
        return carry

    lax.fori_loop(0, 64, tile, 0, unroll=2)


def full(top):
    rolled = pltpu.roll(top, 64, 1)
    return jnp.concatenate([top, jnp.where(lanes_of(top.shape) < 64, -rolled, rolled)], axis=0)


def split3(value):
    first, second = split(value)
    rest = value - first.astype(F32) - second.astype(F32)
    return first, second, rest.astype(BF16)


def fdot(a, b):
    a1, a2, a3 = split3(a)
    b1, b2, b3 = split3(b)
    wide = jnp.concatenate([b1, b2], axis=1)
    main = jnp.dot(
        jnp.concatenate([a1, a2], axis=1),
        jnp.concatenate([wide, wide], axis=0),
        preferred_element_type=F32,
    )
    rest = jnp.dot(
        jnp.concatenate([a1, a3], axis=1),
        jnp.concatenate([b3, b1], axis=0),
        preferred_element_type=F32,
    )
    return main[:, :128] + (main[:, 128:] + rest)


def inverse_roots(tops):
    shape = tops[0].shape
    eye = jnp.where(lanes_of(shape) == rows_of(shape), 1.0, 0.0).astype(F32)
    scales = [jnp.sqrt(2.0 * jnp.sum(t * t, axis=(0, 1), keepdims=True)) for t in tops]
    upper = [t / s for t, s in zip(tops, scales)]
    lower = [1.5 * eye - 0.5 * u for u in upper]
    upper = [fdot(u, full(m)) for u, m in zip(upper, lower)]

    def step(_, carry):
        up, low = carry
        middle = [1.5 * eye - 0.5 * fdot(z, full(y)) for y, z in zip(up, low)]
        return (
            [fdot(y, full(m)) for y, m in zip(up, middle)],
            [fdot(m, full(z)) for z, m in zip(low, middle)],
        )

    upper, lower = lax.fori_loop(0, NS_STEPS - 2, step, (upper, lower))
    middle = [1.5 * eye - 0.5 * fdot(z, full(y)) for y, z in zip(upper, lower)]
    lower = [fdot(m, full(z)) for z, m in zip(lower, middle)]
    return [z * jnp.sqrt(ROWS / s) for z, s in zip(lower, scales)]


def reduce_kernel(
    packed, weights, from_core, from_xy, total, slices, from_z, mine_z, gathered,
    core_send, core_recv, xy_send, xy_recv, zr_send, zr_recv, zg_send, zg_recv,
    wxy_send, wxy_recv, wcore_send, wcore_recv,
):
    blk, row = lax.axis_index("blk"), lax.axis_index("row")
    y_lo, z, x = blk // (NZ * NX), lax.rem(blk // NX, NZ), lax.rem(blk, NX)
    y_hi, core = row // 2, lax.rem(row, 2)
    y = y_hi * 2 + y_lo
    me = y * NX + x
    half = UNITS // 2

    def device(yy, zz, xx, cc):
        return (lax.rem(yy, 2) * (NZ * NX) + zz * NX + xx, (yy // 2) * 2 + cc)

    def plane(step):
        return lax.rem(y + step // NX, NY), lax.rem(x + lax.rem(step, NX), NX)

    def plane_back(step):
        return lax.rem(y - step // NX + NY, NY), lax.rem(x - lax.rem(step, NX) + NX, NX)

    partner = device(y, z, x, 1 - core)

    def plane_device(step):
        yy, xx = plane(step)
        return device(yy, z, xx, core)

    def ring_device(step):
        return device(y, lax.rem(z + step, NZ), x, core)

    barrier = pltpu.get_barrier_semaphore()
    pl.semaphore_signal(barrier, inc=1, device_id=partner, device_id_type=MESH)

    def greet_plane(step, carry):
        pl.semaphore_signal(barrier, inc=1, device_id=plane_device(step), device_id_type=MESH)
        return carry

    def greet_ring(step, carry):
        pl.semaphore_signal(barrier, inc=1, device_id=ring_device(step), device_id_type=MESH)
        return carry

    lax.fori_loop(1, NXY, greet_plane, 0)
    lax.fori_loop(1, NZ, greet_ring, 0)
    pl.semaphore_wait(barrier, NXY + NZ - 1)

    def core_copy():
        return pltpu.make_async_remote_copy(
            src_ref=packed.at[pl.ds((1 - core) * half, half)],
            dst_ref=from_core,
            send_sem=core_send,
            recv_sem=core_recv,
            device_id=partner,
            device_id_type=MESH,
        )

    core_copy().start()
    core_copy().wait_recv()

    def xy_copy(step):
        yy, xx = plane(step)
        return pltpu.make_async_remote_copy(
            src_ref=from_core.at[pl.ds((yy * NX + xx) * CHUNK, CHUNK)],
            dst_ref=from_xy.at[step],
            send_sem=xy_send.at[step],
            recv_sem=xy_recv.at[step],
            device_id=device(yy, z, xx, core),
            device_id_type=MESH,
        )

    def chunk_sum(step):
        yy, xx = plane(step)
        place = pl.ds((yy * NX + xx) * CHUNK, CHUNK)
        return from_core[place] + packed[pl.ds(core * half + (yy * NX + xx) * CHUNK, CHUNK)]

    def send_xy(step, carry):
        yy, xx = plane(step)
        from_core[pl.ds((yy * NX + xx) * CHUNK, CHUNK)] = chunk_sum(step)
        xy_copy(step).start()
        return carry

    lax.fori_loop(1, NXY, send_xy, 0)
    total[...] = chunk_sum(0)

    def add_xy(step, carry):
        xy_copy(step).wait_recv()
        total[...] += from_xy[step]
        return carry

    lax.fori_loop(1, NXY, add_xy, 0)

    for k in range(NZ):
        slices[k] = total[:, k * SLICE : (k + 1) * SLICE, :]

    def zr_copy(step):
        return pltpu.make_async_remote_copy(
            src_ref=slices.at[lax.rem(z + step, NZ)],
            dst_ref=from_z.at[step],
            send_sem=zr_send.at[step],
            recv_sem=zr_recv.at[step],
            device_id=ring_device(step),
            device_id_type=MESH,
        )

    def send_zr(step, carry):
        zr_copy(step).start()
        return carry

    def add_zr(step, acc):
        zr_copy(step).wait_recv()
        return acc + from_z[step]

    lax.fori_loop(1, NZ, send_zr, 0)
    mine_z[...] = lax.fori_loop(1, NZ, add_zr, slices[z])
    gathered[z] = mine_z[...]

    def zg_copy(step):
        return pltpu.make_async_remote_copy(
            src_ref=mine_z,
            dst_ref=gathered.at[z],
            send_sem=zg_send.at[step],
            recv_sem=zg_recv.at[step],
            device_id=ring_device(step),
            device_id_type=MESH,
        )

    def send_zg(step, carry):
        zg_copy(step).start()
        return carry

    def recv_zg(step, carry):
        zg_copy(step).wait_recv()
        return carry

    lax.fori_loop(1, NZ, send_zg, 0)
    lax.fori_loop(1, NZ, recv_zg, 0)

    tops = []
    for u in range(CHUNK):
        tops.extend(unpack(gathered[:, u].reshape(64, 128)))
    roots = inverse_roots(tops)
    first = core * half + me * CHUNK
    for u in range(CHUNK):
        weights[first + u] = pack(roots[2 * u], roots[2 * u + 1])

    def wxy_copy(step):
        return pltpu.make_async_remote_copy(
            src_ref=weights.at[pl.ds(first, CHUNK)],
            dst_ref=weights.at[pl.ds(first, CHUNK)],
            send_sem=wxy_send.at[step],
            recv_sem=wxy_recv.at[step],
            device_id=plane_device(step),
            device_id_type=MESH,
        )

    def wcore_copy(step):
        yy, xx = plane_back(step)
        place = pl.ds(core * half + (yy * NX + xx) * CHUNK, CHUNK)
        return pltpu.make_async_remote_copy(
            src_ref=weights.at[place],
            dst_ref=weights.at[place],
            send_sem=wcore_send.at[step],
            recv_sem=wcore_recv.at[step],
            device_id=partner,
            device_id_type=MESH,
        )

    def send_wxy(step, carry):
        wxy_copy(step).start()
        return carry

    lax.fori_loop(1, NXY, send_wxy, 0)
    wcore_copy(0).start()

    def forward(step, carry):
        wxy_copy(step).wait_recv()
        wcore_copy(step).start()
        return carry

    lax.fori_loop(1, NXY, forward, 0)

    def finish(step, carry):
        wcore_copy(step).wait_recv()
        wcore_copy(step).wait_send()
        return carry

    lax.fori_loop(0, NXY, finish, 0)
    core_copy().wait_send()

    def drain_xy(step, carry):
        xy_copy(step).wait_send()
        wxy_copy(step).wait_send()
        return carry

    def drain_z(step, carry):
        zr_copy(step).wait_send()
        zg_copy(step).wait_send()
        return carry

    lax.fori_loop(1, NXY, drain_xy, 0)
    lax.fori_loop(1, NZ, drain_z, 0)


SMEM = pl.BlockSpec(memory_space=pltpu.SMEM)
VMEM = pl.BlockSpec(memory_space=pltpu.VMEM)
PACKED = jax.ShapeDtypeStruct((UNITS, 64, 128), F32)
TABLE = jax.ShapeDtypeStruct((BLOCKS, BLOCK, 128), F32)


def reduced_roots(packed):
    dma = pltpu.SemaphoreType.DMA
    return pl.pallas_call(
        reduce_kernel,
        out_shape=PACKED,
        in_specs=[VMEM],
        out_specs=VMEM,
        scratch_shapes=[
            pltpu.VMEM((UNITS // 2, 64, 128), F32),
            pltpu.VMEM((NXY, CHUNK, 64, 128), F32),
            pltpu.VMEM((CHUNK, 64, 128), F32),
            pltpu.VMEM((NZ, CHUNK, SLICE, 128), F32),
            pltpu.VMEM((NZ, CHUNK, SLICE, 128), F32),
            pltpu.VMEM((CHUNK, SLICE, 128), F32),
            pltpu.VMEM((NZ, CHUNK, SLICE, 128), F32),
            dma, dma,
            dma((NXY,)), dma((NXY,)), dma((NZ,)), dma((NZ,)), dma((NZ,)), dma((NZ,)),
            dma((NXY,)), dma((NXY,)), dma((NXY,)), dma((NXY,)),
        ],
        compiler_params=PARAMS(collective_id=0, has_side_effects=True),
        name="reduce_roots",
    )(packed)


def on_device(transmission, assignment, pairing):
    rows, _, cols = transmission.shape
    x = transmission.reshape(rows, 2, cols // 128, 128).transpose(0, 2, 1, 3).reshape(-1, 128)
    table, packed = pl.pallas_call(
        first_kernel,
        out_shape=(TABLE, PACKED),
        in_specs=[SMEM, SMEM, VMEM],
        out_specs=(VMEM, VMEM),
        compiler_params=PARAMS(),
        name="first_grams",
    )(assignment, pairing, x)
    weights = reduced_roots(packed)
    table, packed = pl.pallas_call(
        middle_kernel,
        out_shape=(TABLE, PACKED),
        in_specs=[SMEM, SMEM, VMEM, VMEM],
        out_specs=(VMEM, VMEM),
        compiler_params=PARAMS(),
        name="apply_grams",
    )(assignment, pairing, weights, table)
    weights = reduced_roots(packed)
    out = pl.pallas_call(
        last_kernel,
        out_shape=jax.ShapeDtypeStruct(x.shape, F32),
        in_specs=[SMEM, SMEM, VMEM, VMEM],
        out_specs=VMEM,
        scratch_shapes=[pltpu.VMEM((BLOCKS, BLOCK, 128), F32)],
        compiler_params=PARAMS(),
        name="apply_last",
    )(assignment, pairing, weights, table)
    out = out.reshape(rows, cols // 128, 2, 128).transpose(0, 2, 1, 3)
    return out.reshape(rows, 2, cols)


def solution(mesh):
    placed = (P(("blk", "row"), None, None), P(), P())
    return jax.shard_map(
        on_device,
        mesh=mesh,
        in_specs=placed,
        out_specs=P(("blk", "row"), None, None),
        check_vma=False,
    )
```

```python
import functools

import jax
import jax.numpy as jnp
from jax import lax
from jax.experimental import pallas as pl
from jax.experimental.pallas import tpu as pltpu
from jax.sharding import PartitionSpec as P

ROWS = 16384
BLOCK = 32
SLOTS = 4
NS_STEPS = 6
UNITS = 64
BLOCKS = 256
MESH = pl.DeviceIdType.MESH
F32 = jnp.float32
BF16 = jnp.bfloat16
NX, NY, NZ = 4, 4, 8
NXY = NX * NY
CHUNK = UNITS // 2 // NXY
SLICE = 64 // NZ
PARAMS = functools.partial(pltpu.CompilerParams, vmem_limit_bytes=56 * 1024 * 1024)


def position(pick, slot):
    if_two = jnp.where(slot == 0, 0, jnp.where(slot == 3, 1, slot + 1))
    if_one = jnp.where(slot == 1, 2, jnp.where(slot == 2, 1, slot))
    return jnp.where(pick == 0, slot, jnp.where(pick == 1, if_one, if_two))


def slot_at(pick, h):
    if h == 0:
        return 0, 1 + pick
    return jnp.where(pick == 0, 2, 1), jnp.where(pick == 2, 2, 3)


def turn_of(slot):
    return jnp.where(slot == 1, -1, jnp.where(slot == 2, 1, 0))


def pair_places(assign, pairing, rnd, d, h):
    slots = slot_at(pairing[rnd, d], h)
    if rnd == 0:
        return [assign[d * SLOTS + slot] for slot in slots]
    places = []
    for slot in slots:
        home = lax.rem(d + turn_of(slot) + UNITS, UNITS)
        places.append(home * SLOTS + position(pairing[0, home], slot))
    return places


def lanes_of(shape):
    return lax.broadcasted_iota(jnp.int32, shape, 1)


def rows_of(shape):
    return lax.broadcasted_iota(jnp.int32, shape, 0)


def split(value):
    high = value.astype(BF16)
    return high, (value - high.astype(F32)).astype(BF16)


def turned(pair):
    rolled = pltpu.roll(pair, 64, 1)
    return jnp.where(lanes_of(pair.shape) < 64, rolled, -rolled)


def unpack(unit):
    lane, row = lanes_of(unit.shape), rows_of(unit.shape)
    left = lane < 64
    column = jnp.where(left, lane, lane - 64)
    flipped = jnp.concatenate([unit, unit], axis=0).T
    rolled = pltpu.roll(unit, 64, 1)
    tops = []
    for h in range(2):
        here = jnp.where(left, unit, rolled) if h == 0 else jnp.where(left, rolled, unit)
        there = flipped[64 * h : 64 * h + 64]
        real = jnp.where(row <= column, here, there)
        imag = jnp.where(row > column, here, jnp.where(row < column, -there, 0.0))
        tops.append(jnp.where(left, real, imag))
    return tops


def pack(first, second):
    lane, row = lanes_of(first.shape), rows_of(first.shape)
    left = lane < 64
    packed_first = jnp.where(row <= lane, first, pltpu.roll(first, 64, 1))
    packed_second = jnp.where(row <= lane - 64, pltpu.roll(second, 64, 1), second)
    return jnp.where(left, packed_first, packed_second)


def both(pair):
    return jnp.concatenate([pair, turned(pair)], axis=0)


def nt_dot(a, b):
    return lax.dot_general(a, b, (((1,), (1,)), ((), ())), preferred_element_type=F32)


def gram_top(pair):
    high, low = split(both(pair))
    lhs = jnp.concatenate([high[:64], low[:64]], axis=1)
    rhs = jnp.concatenate([high, high], axis=1)
    return nt_dot(lhs, rhs) + nt_dot(high[:64], low)


def applied(top, pair):
    high, low = split(both(pair))
    whigh, wlow = split(top)
    lhs = jnp.concatenate([whigh, wlow], axis=1)
    rhs = jnp.concatenate([high, high], axis=0)
    return jnp.dot(lhs, rhs, preferred_element_type=F32) + jnp.dot(
        whigh, low, preferred_element_type=F32
    )


def load_pair(table, a, b):
    return jnp.concatenate([table[a], table[b]], axis=0)


def full(top):
    rolled = pltpu.roll(top, 64, 1)
    return jnp.concatenate([top, jnp.where(lanes_of(top.shape) < 64, -rolled, rolled)], axis=0)


def split3(value):
    first, second = split(value)
    rest = value - first.astype(F32) - second.astype(F32)
    return first, second, rest.astype(BF16)


def fdot(a, b):
    a1, a2, a3 = split3(a)
    b1, b2, b3 = split3(b)
    wide = jnp.concatenate([b1, b2], axis=1)
    main = jnp.dot(
        jnp.concatenate([a1, a2], axis=1),
        jnp.concatenate([wide, wide], axis=0),
        preferred_element_type=F32,
    )
    rest = jnp.dot(
        jnp.concatenate([a1, a3], axis=1),
        jnp.concatenate([b3, b1], axis=0),
        preferred_element_type=F32,
    )
    return main[:, :128] + (main[:, 128:] + rest)


def inverse_roots(tops):
    shape = tops[0].shape
    eye = jnp.where(lanes_of(shape) == rows_of(shape), 1.0, 0.0).astype(F32)
    scales = [jnp.sqrt(2.0 * jnp.sum(t * t, axis=(0, 1), keepdims=True)) for t in tops]
    upper = [t / s for t, s in zip(tops, scales)]
    lower = [1.5 * eye - 0.5 * u for u in upper]
    upper = [fdot(u, full(m)) for u, m in zip(upper, lower)]

    def step(_, carry):
        up, low = carry
        middle = [1.5 * eye - 0.5 * fdot(z, full(y)) for y, z in zip(up, low)]
        return (
            [fdot(y, full(m)) for y, m in zip(up, middle)],
            [fdot(m, full(z)) for z, m in zip(low, middle)],
        )

    upper, lower = lax.fori_loop(0, NS_STEPS - 2, step, (upper, lower))
    middle = [1.5 * eye - 0.5 * fdot(z, full(y)) for y, z in zip(upper, lower)]
    lower = [fdot(m, full(z)) for z, m in zip(lower, middle)]
    return [z * jnp.sqrt(ROWS / s) for z, s in zip(lower, scales)]


def fused_kernel(
    assign, pairing, x_in, out, table, rotated, packed, from_core, from_xy, total, slices, from_z,
    mine_z, gathered, weights,
    core_send, core_recv, xy_send, xy_recv, zr_send, zr_recv, zg_send, zg_recv,
    wxy_send, wxy_recv, wcore_send, wcore_recv,
):
    blk, row = lax.axis_index("blk"), lax.axis_index("row")
    y_lo, z, x = blk // (NZ * NX), lax.rem(blk // NX, NZ), lax.rem(blk, NX)
    y_hi, core = row // 2, lax.rem(row, 2)
    y = y_hi * 2 + y_lo
    half = UNITS // 2

    def device(yy, zz, xx, cc):
        return (lax.rem(yy, 2) * (NZ * NX) + zz * NX + xx, (yy // 2) * 2 + cc)

    def plane(step):
        return lax.rem(y + step // NX, NY), lax.rem(x + lax.rem(step, NX), NX)

    def chunk_to(step):
        yy, xx = plane(step)
        return (yy * NX + xx) * CHUNK

    def chunk_from(step):
        yy, xx = lax.rem(y - step // NX + NY, NY), lax.rem(x - lax.rem(step, NX) + NX, NX)
        return (yy * NX + xx) * CHUNK

    partner = device(y, z, x, 1 - core)

    def plane_device(step):
        yy, xx = plane(step)
        return device(yy, z, xx, core)

    def ring_device(step):
        return device(y, lax.rem(z + step, NZ), x, core)

    def each(first, last, body):
        def run(step, carry):
            body(step)
            return carry

        lax.fori_loop(first, last, run, 0)

    def remote(src, dst, send, recv, to):
        return pltpu.make_async_remote_copy(
            src_ref=src, dst_ref=dst, send_sem=send, recv_sem=recv, device_id=to, device_id_type=MESH
        )

    barrier = pltpu.get_barrier_semaphore()

    def greet(to):
        pl.semaphore_signal(barrier, inc=1, device_id=to, device_id_type=MESH)

    greet(partner)
    each(1, NXY, lambda step: greet(plane_device(step)))
    each(1, NZ, lambda step: greet(ring_device(step)))

    def tile(ct, carry):
        real = x_in[pl.ds(2 * ct, 64, stride=128), :]
        imag = x_in[pl.ds(2 * ct + 1, 64, stride=128), :]
        flipped = jnp.concatenate([real, imag], axis=0).T
        table[pl.ds(4 * ct, 4)] = flipped.reshape(4, BLOCK, 128)
        return carry

    lax.fori_loop(0, BLOCKS // 4, tile, 0, unroll=2)
    pl.semaphore_wait(barrier, NXY + NZ - 1)

    def one_round(rnd, source, target):
        def core_copy(step):
            place = chunk_to(step)
            return remote(
                packed.at[pl.ds((1 - core) * half + place, CHUNK)],
                from_core.at[rnd, pl.ds(place, CHUNK)],
                core_send.at[rnd, step], core_recv.at[rnd, step], partner,
            )

        def xy_copy(step):
            return remote(
                from_core.at[rnd, pl.ds(chunk_to(step), CHUNK)], from_xy.at[rnd, step],
                xy_send.at[rnd, step], xy_recv.at[rnd, step], plane_device(step),
            )

        def gram_units(first):
            for u in range(CHUNK):
                tops = []
                for h in range(2):
                    a, b = pair_places(assign, pairing, rnd, first + u, h)
                    tops.append(gram_top(load_pair(source, a, b)))
                packed[first + u] = pack(*tops)

        def compute(step):
            place = chunk_to(step)
            gram_units((1 - core) * half + place)
            core_copy(step).start()
            gram_units(core * half + place)

        def chunk_sum(step):
            place = chunk_to(step)
            core_copy(step).wait_recv()
            return from_core[rnd, pl.ds(place, CHUNK)] + packed[pl.ds(core * half + place, CHUNK)]

        def ship(step):
            from_core[rnd, pl.ds(chunk_to(step), CHUNK)] = chunk_sum(step)
            xy_copy(step).start()

        def advance(step):
            compute(lax.rem(step, NXY))
            ship(step - 1)

        compute(1)
        each(2, NXY + 1, advance)
        total[...] = chunk_sum(0)

        def add_xy(step):
            xy_copy(step).wait_recv()
            total[...] += from_xy[rnd, step]

        each(1, NXY, add_xy)

        for k in range(NZ):
            slices[k] = total[:, k * SLICE : (k + 1) * SLICE, :]

        def zr_copy(step):
            return remote(
                slices.at[lax.rem(z + step, NZ)], from_z.at[rnd, step],
                zr_send.at[rnd, step], zr_recv.at[rnd, step], ring_device(step),
            )

        def zg_copy(step):
            return remote(
                mine_z, gathered.at[rnd, z], zg_send.at[rnd, step], zg_recv.at[rnd, step],
                ring_device(step),
            )

        def add_zr(step, acc):
            zr_copy(step).wait_recv()
            return acc + from_z[rnd, step]

        each(1, NZ, lambda step: zr_copy(step).start())
        mine_z[...] = lax.fori_loop(1, NZ, add_zr, slices[z])
        gathered[rnd, z] = mine_z[...]
        each(1, NZ, lambda step: zg_copy(step).start())
        each(1, NZ, lambda step: zg_copy(step).wait_recv())

        tops = []
        for u in range(CHUNK):
            tops.extend(unpack(gathered[rnd, :, u].reshape(64, 128)))
        roots = inverse_roots(tops)
        mine = core * half + chunk_to(0)
        for u in range(CHUNK):
            weights[rnd, mine + u] = pack(roots[2 * u], roots[2 * u + 1])

        def wxy_copy(step):
            place = weights.at[rnd, pl.ds(mine, CHUNK)]
            return remote(
                place, place, wxy_send.at[rnd, step], wxy_recv.at[rnd, step], plane_device(step)
            )

        def wcore_copy(step):
            place = weights.at[rnd, pl.ds(core * half + chunk_from(step), CHUNK)]
            return remote(
                place, place, wcore_send.at[rnd, step], wcore_recv.at[rnd, step], partner
            )

        def apply_units(first):
            for u in range(CHUNK):
                d = first + u
                tops = unpack(weights[rnd, d])
                for h in range(2):
                    a, b = pair_places(assign, pairing, rnd, d, h)
                    new = applied(tops[h], load_pair(source, a, b))
                    target[pl.ds(SLOTS * d + 2 * h, 2)] = new.reshape(2, BLOCK, 128)

        def apply_other(step):
            wcore_copy(step).wait_recv()
            apply_units((1 - core) * half + chunk_from(step))

        def take(step):
            wxy_copy(step).wait_recv()
            wcore_copy(step).start()
            apply_units(core * half + chunk_from(step))
            apply_other(step - 1)

        each(1, NXY, lambda step: wxy_copy(step).start())
        wcore_copy(0).start()
        apply_units(mine)
        each(1, NXY, take)
        apply_other(NXY - 1)

        def drain_core(step):
            core_copy(step).wait_send()
            wcore_copy(step).wait_send()

        def drain_xy(step):
            xy_copy(step).wait_send()
            wxy_copy(step).wait_send()

        def drain_z(step):
            zr_copy(step).wait_send()
            zg_copy(step).wait_send()

        each(0, NXY, drain_core)
        each(1, NXY, drain_xy)
        each(1, NZ, drain_z)

    one_round(0, table, rotated)
    one_round(1, rotated, out)


def last_kernel(assign, pairing, source, out, places):
    def place(slot, carry):
        q = lax.rem(slot, SLOTS)
        home = lax.rem(slot // SLOTS - turn_of(q) + UNITS, UNITS)
        places[assign[slot]] = home * SLOTS + position(pairing[1, home], q)
        return carry

    lax.fori_loop(0, BLOCKS, place, 0, unroll=8)

    def tile(ct, carry):
        parts = [source[places[4 * ct + k]] for k in range(4)]
        flipped = jnp.concatenate(parts, axis=0).T
        out[pl.ds(2 * ct, 64, stride=128), :] = flipped[:64]
        out[pl.ds(2 * ct + 1, 64, stride=128), :] = flipped[64:]
        return carry

    lax.fori_loop(0, BLOCKS // 4, tile, 0, unroll=2)


SMEM = pl.BlockSpec(memory_space=pltpu.SMEM)
VMEM = pl.BlockSpec(memory_space=pltpu.VMEM)
TABLE = (BLOCKS, BLOCK, 128)


def rounds(assignment, pairing, x):
    dma = pltpu.SemaphoreType.DMA
    plane, ring = dma((2, NXY)), dma((2, NZ))
    return pl.pallas_call(
        fused_kernel,
        out_shape=jax.ShapeDtypeStruct(TABLE, F32),
        in_specs=[SMEM, SMEM, VMEM],
        out_specs=VMEM,
        scratch_shapes=[
            pltpu.VMEM(TABLE, F32),
            pltpu.VMEM(TABLE, F32),
            pltpu.VMEM((UNITS, 64, 128), F32),
            pltpu.VMEM((2, UNITS // 2, 64, 128), F32),
            pltpu.VMEM((2, NXY, CHUNK, 64, 128), F32),
            pltpu.VMEM((CHUNK, 64, 128), F32),
            pltpu.VMEM((NZ, CHUNK, SLICE, 128), F32),
            pltpu.VMEM((2, NZ, CHUNK, SLICE, 128), F32),
            pltpu.VMEM((CHUNK, SLICE, 128), F32),
            pltpu.VMEM((2, NZ, CHUNK, SLICE, 128), F32),
            pltpu.VMEM((2, UNITS, 64, 128), F32),
            plane, plane, plane, plane, ring, ring, ring, ring, plane, plane, plane, plane,
        ],
        compiler_params=PARAMS(collective_id=0, has_side_effects=True),
        name="rounds",
    )(assignment, pairing, x)


def on_device(transmission, assignment, pairing):
    rows, _, cols = transmission.shape
    x = transmission.reshape(rows, 2, cols // 128, 128).transpose(0, 2, 1, 3).reshape(-1, 128)
    turned_blocks = rounds(assignment, pairing, x)
    out = pl.pallas_call(
        last_kernel,
        out_shape=jax.ShapeDtypeStruct(x.shape, F32),
        in_specs=[SMEM, SMEM, VMEM],
        out_specs=VMEM,
        scratch_shapes=[pltpu.SMEM((BLOCKS,), jnp.int32)],
        compiler_params=PARAMS(),
        name="unturn",
    )(assignment, pairing, turned_blocks)
    out = out.reshape(rows, cols // 128, 2, 128).transpose(0, 2, 1, 3)
    return out.reshape(rows, 2, cols)


def solution(mesh):
    placed = (P(("blk", "row"), None, None), P(), P())
    return jax.shard_map(
        on_device,
        mesh=mesh,
        in_specs=placed,
        out_specs=P(("blk", "row"), None, None),
        check_vma=False,
    )
```

```python
import functools

import jax
import jax.numpy as jnp
from jax import lax
from jax.experimental import pallas as pl
from jax.experimental.pallas import tpu as pltpu
from jax.sharding import PartitionSpec as P

ROWS = 16384
BLOCK = 32
SLOTS = 4
NS_STEPS = 6
UNITS = 64
BLOCKS = 256
MESH = pl.DeviceIdType.MESH
F32 = jnp.float32
BF16 = jnp.bfloat16
NX, NY, NZ = 4, 4, 8
NXY = NX * NY
CHUNK = UNITS // 2 // NXY
SLICE = 64 // NZ
PARAMS = functools.partial(pltpu.CompilerParams, vmem_limit_bytes=56 * 1024 * 1024)


def position(pick, slot):
    if_two = jnp.where(slot == 0, 0, jnp.where(slot == 3, 1, slot + 1))
    if_one = jnp.where(slot == 1, 2, jnp.where(slot == 2, 1, slot))
    return jnp.where(pick == 0, slot, jnp.where(pick == 1, if_one, if_two))


def slot_at(pick, h):
    if h == 0:
        return 0, 1 + pick
    return jnp.where(pick == 0, 2, 1), jnp.where(pick == 2, 2, 3)


def turn_of(slot):
    return jnp.where(slot == 1, -1, jnp.where(slot == 2, 1, 0))


def pair_places(assign, pairing, rnd, d, h):
    slots = slot_at(pairing[rnd, d], h)
    if rnd == 0:
        return [assign[d * SLOTS + slot] for slot in slots]
    places = []
    for slot in slots:
        home = lax.rem(d + turn_of(slot) + UNITS, UNITS)
        places.append(home * SLOTS + position(pairing[0, home], slot))
    return places


def lanes_of(shape):
    return lax.broadcasted_iota(jnp.int32, shape, 1)


def rows_of(shape):
    return lax.broadcasted_iota(jnp.int32, shape, 0)


def split(value):
    high = value.astype(BF16)
    return high, (value - high.astype(F32)).astype(BF16)


def turned(pair):
    rolled = pltpu.roll(pair, 64, 1)
    return jnp.where(lanes_of(pair.shape) < 64, rolled, -rolled)


def unpack(unit):
    lane, row = lanes_of(unit.shape), rows_of(unit.shape)
    left = lane < 64
    column = jnp.where(left, lane, lane - 64)
    flipped = jnp.concatenate([unit, unit], axis=0).T
    rolled = pltpu.roll(unit, 64, 1)
    tops = []
    for h in range(2):
        here = jnp.where(left, unit, rolled) if h == 0 else jnp.where(left, rolled, unit)
        there = flipped[64 * h : 64 * h + 64]
        real = jnp.where(row <= column, here, there)
        imag = jnp.where(row > column, here, jnp.where(row < column, -there, 0.0))
        tops.append(jnp.where(left, real, imag))
    return tops


def pack(first, second):
    lane, row = lanes_of(first.shape), rows_of(first.shape)
    left = lane < 64
    packed_first = jnp.where(row <= lane, first, pltpu.roll(first, 64, 1))
    packed_second = jnp.where(row <= lane - 64, pltpu.roll(second, 64, 1), second)
    return jnp.where(left, packed_first, packed_second)


def both(pair):
    return jnp.concatenate([pair, turned(pair)], axis=0)


def nt_dot(a, b):
    return lax.dot_general(a, b, (((1,), (1,)), ((), ())), preferred_element_type=F32)


def gram_top(pair):
    high, low = split(both(pair))
    lhs = jnp.concatenate([high[:64], low[:64]], axis=1)
    rhs = jnp.concatenate([high, high], axis=1)
    return nt_dot(lhs, rhs) + nt_dot(high[:64], low)


def applied(top, pair):
    high, low = split(both(pair))
    whigh, wlow = split(top)
    lhs = jnp.concatenate([whigh, wlow], axis=1)
    rhs = jnp.concatenate([high, high], axis=0)
    return jnp.dot(lhs, rhs, preferred_element_type=F32) + jnp.dot(
        whigh, low, preferred_element_type=F32
    )


def load_pair(table, a, b):
    return jnp.concatenate([table[a], table[b]], axis=0)


def full(top):
    rolled = pltpu.roll(top, 64, 1)
    return jnp.concatenate([top, jnp.where(lanes_of(top.shape) < 64, -rolled, rolled)], axis=0)


def split3(value):
    first, second = split(value)
    rest = value - first.astype(F32) - second.astype(F32)
    return first, second, rest.astype(BF16)


def fdot(a, b):
    a1, a2, a3 = split3(a)
    b1, b2, b3 = split3(b)
    wide = jnp.concatenate([b1, b2], axis=1)
    main = jnp.dot(
        jnp.concatenate([a1, a2], axis=1),
        jnp.concatenate([wide, wide], axis=0),
        preferred_element_type=F32,
    )
    rest = jnp.dot(
        jnp.concatenate([a1, a3], axis=1),
        jnp.concatenate([b3, b1], axis=0),
        preferred_element_type=F32,
    )
    return main[:, :128] + (main[:, 128:] + rest)


def inverse_roots(tops):
    shape = tops[0].shape
    eye = jnp.where(lanes_of(shape) == rows_of(shape), 1.0, 0.0).astype(F32)
    scales = [jnp.sqrt(2.0 * jnp.sum(t * t, axis=(0, 1), keepdims=True)) for t in tops]
    upper = [t / s for t, s in zip(tops, scales)]
    lower = [1.5 * eye - 0.5 * u for u in upper]
    upper = [fdot(u, full(m)) for u, m in zip(upper, lower)]

    def step(_, carry):
        up, low = carry
        middle = [1.5 * eye - 0.5 * fdot(z, full(y)) for y, z in zip(up, low)]
        return (
            [fdot(y, full(m)) for y, m in zip(up, middle)],
            [fdot(m, full(z)) for z, m in zip(low, middle)],
        )

    upper, lower = lax.fori_loop(0, NS_STEPS - 2, step, (upper, lower))
    middle = [1.5 * eye - 0.5 * fdot(z, full(y)) for y, z in zip(upper, lower)]
    lower = [fdot(m, full(z)) for z, m in zip(lower, middle)]
    return [z * jnp.sqrt(ROWS / s) for z, s in zip(lower, scales)]


def order_in(i):
    return lax.rem(2 + 3 * i + 3 * (i * (i - 1) // 2), 4)


def order_out(i):
    return lax.rem(3 * i + 3 * (i * (i - 1) // 2), 4)


def fused_kernel(
    assign, pairing, x_in, out, table, rotated, packed, from_core, relay, inbox, total, slices, from_z,
    mine_z, gathered, weights,
    core_send, core_recv, relay_send, relay_recv, inbox_send, inbox_recv, zr_send, zr_recv, zg_send,
    zg_recv, wfull_send, wfull_recv, whalf_send, whalf_recv, wcore_send, wcore_recv,
):
    blk, row = lax.axis_index("blk"), lax.axis_index("row")
    y_lo, z, x = blk // (NZ * NX), lax.rem(blk // NX, NZ), lax.rem(blk, NX)
    y_hi, core = row // 2, lax.rem(row, 2)
    y = y_hi * 2 + y_lo
    half = UNITS // 2
    p, q = x + core * (y - x), y + core * (x - y)

    def device(yy, zz, xx, cc):
        return (lax.rem(yy, 2) * (NZ * NX) + zz * NX + xx, (yy // 2) * 2 + cc)

    def beside(direction, second):
        move = 1 + 2 * direction
        pp = lax.rem(p + move * (1 - second), 4)
        qq = lax.rem(q + move * second, 4)
        return device(qq + core * (pp - qq), z, pp + core * (qq - pp), core)

    partner = device(y, z, x, 1 - core)

    def ring_device(step):
        return device(y, lax.rem(z + step, NZ), x, core)

    def my_chunk(da, db):
        return (lax.rem(p + da, 4) * 4 + lax.rem(q + db, 4)) * CHUNK

    def other_chunk(da, db):
        return (lax.rem(q + da, 4) * 4 + lax.rem(p + db, 4)) * CHUNK

    def each(first, last, body):
        def run(step, carry):
            body(step)
            return carry

        lax.fori_loop(first, last, run, 0)

    def remote(src, dst, send, recv, to):
        return pltpu.make_async_remote_copy(
            src_ref=src, dst_ref=dst, send_sem=send, recv_sem=recv, device_id=to, device_id_type=MESH
        )

    barrier = pltpu.get_barrier_semaphore()

    def greet(to):
        pl.semaphore_signal(barrier, inc=1, device_id=to, device_id_type=MESH)

    greet(partner)
    for direction in range(2):
        for second in range(2):
            greet(beside(direction, second))
    each(1, NZ, lambda step: greet(ring_device(step)))

    def tile(ct, carry):
        real = x_in[pl.ds(2 * ct, 64, stride=128), :]
        imag = x_in[pl.ds(2 * ct + 1, 64, stride=128), :]
        flipped = jnp.concatenate([real, imag], axis=0).T
        table[pl.ds(4 * ct, 4)] = flipped.reshape(4, BLOCK, 128)
        return carry

    lax.fori_loop(0, BLOCKS // 4, tile, 0, unroll=2)
    pl.semaphore_wait(barrier, 4 + NZ)

    def one_round(rnd, source, target):
        def core_copy(step):
            place = other_chunk(order_in(step // 4), order_in(lax.rem(step, 4)))
            return remote(
                packed.at[pl.ds((1 - core) * half + place, CHUNK)],
                from_core.at[rnd, pl.ds(place, CHUNK)],
                core_send.at[rnd, step], core_recv.at[rnd, step], partner,
            )

        def relay_copy(direction, slot, place, second):
            return remote(
                from_core.at[rnd, place + direction], relay.at[rnd, direction, slot],
                relay_send.at[rnd, direction, slot], relay_recv.at[rnd, direction, slot],
                beside(direction, second),
            )

        def inbox_copy(direction, slot, place, second):
            return remote(
                from_core.at[rnd, pl.ds(place, CHUNK)], inbox.at[rnd, direction, slot],
                inbox_send.at[rnd, direction, slot], inbox_recv.at[rnd, direction, slot],
                beside(direction, second),
            )

        def gram_units(first):
            for u in range(CHUNK):
                tops = []
                for h in range(2):
                    a, b = pair_places(assign, pairing, rnd, first + u, h)
                    tops.append(gram_top(load_pair(source, a, b)))
                packed[first + u] = pack(*tops)

        def compute(step):
            da, db = order_in(step // 4), order_in(lax.rem(step, 4))
            gram_units((1 - core) * half + other_chunk(da, db))
            core_copy(step).start()
            gram_units(core * half + my_chunk(da, db))

        def inbox_sum(slot):
            for direction in range(2):
                inbox_copy(direction, slot, 0, 0).wait_recv()
            return inbox[rnd, 0, slot] + inbox[rnd, 1, slot]

        def ship(step):
            ia, ib = step // 4, lax.rem(step, 4)
            second = step // 12
            kind, slot = ia + second * (ib - ia), ib + second * (4 - ib)
            place = my_chunk(order_in(ia), order_in(ib))
            chunk = pl.ds(place, CHUNK)
            core_copy(step).wait_recv()
            from_core[rnd, chunk] += packed[pl.ds(core * half + place, CHUNK)]

            @pl.when(second == 1)
            def _():
                from_core[rnd, chunk] += inbox_sum(ib)

            @pl.when(kind == 0)
            def _():
                for direction in range(2):
                    relay_copy(direction, slot, place, second).start()

            for direction in range(2):

                @pl.when(kind == 1 + direction)
                def _(direction=direction):
                    relay_copy(direction, slot, place, second).wait_recv()
                    from_core[rnd, place + direction] += relay[rnd, direction, slot]
                    inbox_copy(direction, slot, place, second).start()

        def advance(step):
            compute(step)
            ship(step - 1)

        compute(0)
        each(1, 16, advance)
        core_copy(15).wait_recv()
        place = my_chunk(0, 0)
        total[...] = (
            from_core[rnd, pl.ds(place, CHUNK)]
            + packed[pl.ds(core * half + place, CHUNK)]
            + inbox_sum(3)
            + inbox_sum(4)
        )

        for k in range(NZ):
            slices[k] = total[:, k * SLICE : (k + 1) * SLICE, :]

        def zr_copy(step):
            return remote(
                slices.at[lax.rem(z + step, NZ)], from_z.at[rnd, step],
                zr_send.at[rnd, step], zr_recv.at[rnd, step], ring_device(step),
            )

        def zg_copy(step):
            return remote(
                mine_z, gathered.at[rnd, z], zg_send.at[rnd, step], zg_recv.at[rnd, step],
                ring_device(step),
            )

        far_first = (4, 3, 5, 2, 6, 1, 7)
        for step in far_first:
            zr_copy(step).start()
        acc = slices[z]
        for step in reversed(far_first):
            zr_copy(step).wait_recv()
            acc = acc + from_z[rnd, step]
        mine_z[...] = acc
        for step in far_first:
            zg_copy(step).start()
        gathered[rnd, z] = acc
        for step in reversed(far_first):
            zg_copy(step).wait_recv()

        tops = []
        for u in range(CHUNK):
            tops.extend(unpack(gathered[rnd, :, u].reshape(64, 128)))
        roots = inverse_roots(tops)
        mine = core * half + place
        for u in range(CHUNK):
            weights[rnd, mine + u] = pack(roots[2 * u], roots[2 * u + 1])

        def wfull_copy(direction, slot, first, second):
            part = weights.at[rnd, pl.ds(first, CHUNK)]
            return remote(
                part, part, wfull_send.at[rnd, direction, slot], wfull_recv.at[rnd, direction, slot],
                beside(direction, second),
            )

        def whalf_copy(direction, slot, first, second):
            part = weights.at[rnd, first + direction]
            return remote(
                part, part, whalf_send.at[rnd, direction, slot], whalf_recv.at[rnd, direction, slot],
                beside(direction, second),
            )

        def my_units(step):
            return core * half + my_chunk(order_out(step // 4), order_out(lax.rem(step, 4)))

        def other_units(step):
            return (1 - core) * half + other_chunk(order_out(step // 4), order_out(lax.rem(step, 4)))

        def wcore_copy(step):
            part = weights.at[rnd, pl.ds(my_units(step), CHUNK)]
            return remote(
                part, part, wcore_send.at[rnd, step], wcore_recv.at[rnd, step], partner
            )

        def apply_units(first):
            for u in range(CHUNK):
                d = first + u
                tops = unpack(weights[rnd, d])
                for h in range(2):
                    a, b = pair_places(assign, pairing, rnd, d, h)
                    new = applied(tops[h], load_pair(source, a, b))
                    target[pl.ds(SLOTS * d + 2 * h, 2)] = new.reshape(2, BLOCK, 128)

        def apply_other(step):
            wcore_copy(step).wait_recv()
            apply_units(other_units(step))

        def take(step):
            ia, ib = step // 4, lax.rem(step, 4)
            second = (15 - step) // 12
            kind, slot = ia + second * (ib - ia), ib + second * (4 - ib)
            first = my_units(step)
            for direction in range(2):

                @pl.when(kind == 1 + direction)
                def _(direction=direction):
                    wfull_copy(direction, slot, first, second).wait_recv()
                    whalf_copy(direction, slot, first, second).start()

            @pl.when(kind == 3)
            def _():
                for direction in range(2):
                    whalf_copy(direction, slot, first, second).wait_recv()

            @pl.when(second == 1)
            def _():
                for direction in range(2):
                    wfull_copy(direction, ib, first, 0).start()

            wcore_copy(step).start()
            apply_units(first)
            apply_other(step - 1)

        for direction in range(2):
            wfull_copy(direction, 4, mine, 1).start()
        for direction in range(2):
            wfull_copy(direction, 0, mine, 0).start()
        wcore_copy(0).start()
        apply_units(mine)
        each(1, 16, take)
        apply_other(15)

        def drain_core(step):
            core_copy(step).wait_send()
            wcore_copy(step).wait_send()

        def drain_plane(slot):
            for direction in range(2):
                relay_copy(direction, slot, 0, 0).wait_send()
                inbox_copy(direction, slot, 0, 0).wait_send()
                wfull_copy(direction, slot, 0, 0).wait_send()
                whalf_copy(direction, slot, 0, 0).wait_send()

        def drain_z(step):
            zr_copy(step).wait_send()
            zg_copy(step).wait_send()

        each(0, 16, drain_core)
        each(0, 5, drain_plane)
        each(1, NZ, drain_z)

    one_round(0, table, rotated)
    one_round(1, rotated, out)


STEP = 8


def last_kernel(assign, pairing, source, out, places):
    @pl.when(pl.program_id(0) == 0)
    def _():
        def unit(d, carry):
            up = jnp.where(d == UNITS - 1, 0, d + 1)
            down = jnp.where(d == 0, UNITS - 1, d - 1)
            here, above, below = pairing[1, d], pairing[1, up], pairing[1, down]
            places[assign[SLOTS * d]] = SLOTS * d
            places[assign[SLOTS * d + 1]] = SLOTS * up + jnp.where(above == 0, 1, 2)
            places[assign[SLOTS * d + 2]] = SLOTS * down + jnp.where(
                below == 0, 2, jnp.where(below == 1, 1, 3)
            )
            places[assign[SLOTS * d + 3]] = SLOTS * d + jnp.where(here == 2, 1, 3)
            return carry

        lax.fori_loop(0, UNITS, unit, 0, unroll=4)

    flat = out.reshape(64 * 2 * STEP, 128)
    for k in range(STEP):
        ct = pl.program_id(0) * STEP + k
        parts = [source[places[4 * ct + j]] for j in range(4)]
        flipped = jnp.concatenate(parts, axis=0).T
        flat[pl.ds(2 * k, 64, stride=2 * STEP), :] = flipped[:64]
        flat[pl.ds(2 * k + 1, 64, stride=2 * STEP), :] = flipped[64:]


SMEM = pl.BlockSpec(memory_space=pltpu.SMEM)
VMEM = pl.BlockSpec(memory_space=pltpu.VMEM)
TABLE = (BLOCKS, BLOCK, 128)


def rounds(assignment, pairing, x):
    dma = pltpu.SemaphoreType.DMA
    chunks, plane, ring = dma((2, 16)), dma((2, 2, 5)), dma((2, NZ))
    return pl.pallas_call(
        fused_kernel,
        out_shape=jax.ShapeDtypeStruct(TABLE, F32),
        in_specs=[SMEM, SMEM, VMEM],
        out_specs=VMEM,
        scratch_shapes=[
            pltpu.VMEM(TABLE, F32),
            pltpu.VMEM(TABLE, F32),
            pltpu.VMEM((UNITS, 64, 128), F32),
            pltpu.VMEM((2, UNITS // 2, 64, 128), F32),
            pltpu.VMEM((2, 2, 5, 64, 128), F32),
            pltpu.VMEM((2, 2, 5, CHUNK, 64, 128), F32),
            pltpu.VMEM((CHUNK, 64, 128), F32),
            pltpu.VMEM((NZ, CHUNK, SLICE, 128), F32),
            pltpu.VMEM((2, NZ, CHUNK, SLICE, 128), F32),
            pltpu.VMEM((CHUNK, SLICE, 128), F32),
            pltpu.VMEM((2, NZ, CHUNK, SLICE, 128), F32),
            pltpu.VMEM((2, UNITS, 64, 128), F32),
            chunks, chunks, plane, plane, plane, plane, ring, ring, ring, ring,
            plane, plane, plane, plane, chunks, chunks,
        ],
        compiler_params=PARAMS(collective_id=0, has_side_effects=True),
        name="rounds",
    )(assignment, pairing, x)


def unturned(assignment, pairing, source):
    shape = (64, BLOCKS // 2, 128)
    return pl.pallas_call(
        last_kernel,
        out_shape=jax.ShapeDtypeStruct(shape, F32),
        grid=(BLOCKS // 4 // STEP,),
        in_specs=[SMEM, SMEM, VMEM],
        out_specs=pl.BlockSpec((64, 2 * STEP, 128), lambda i: (0, i, 0)),
        scratch_shapes=[pltpu.SMEM((BLOCKS,), jnp.int32)],
        compiler_params=PARAMS(),
        name="unturn",
    )(assignment, pairing, source)


def on_device(transmission, assignment, pairing):
    rows, _, cols = transmission.shape
    x = transmission.reshape(rows, 2, cols // 128, 128).transpose(0, 2, 1, 3).reshape(-1, 128)
    turned_blocks = rounds(assignment, pairing, x)
    out = unturned(assignment, pairing, turned_blocks)
    out = out.reshape(rows, cols // 128, 2, 128).transpose(0, 2, 1, 3)
    return out.reshape(rows, 2, cols)


def solution(mesh):
    placed = (P(("blk", "row"), None, None), P(), P())
    return jax.shard_map(
        on_device,
        mesh=mesh,
        in_specs=placed,
        out_specs=P(("blk", "row"), None, None),
        check_vma=False,
    )
```

```python
import functools

import jax
import jax.numpy as jnp
from jax import lax
from jax.experimental import pallas as pl
from jax.experimental.pallas import tpu as pltpu
from jax.sharding import PartitionSpec as P

ROWS = 16384
BLOCK = 32
SLOTS = 4
NS_STEPS = 6
UNITS = 64
BLOCKS = 256
MESH = pl.DeviceIdType.MESH
F32 = jnp.float32
BF16 = jnp.bfloat16
NX, NY, NZ = 4, 4, 8
NXY = NX * NY
CHUNK = UNITS // 2 // NXY
SLICE = 64 // NZ
STEP = 8
GROUPS = BLOCKS // 4 // STEP
PARAMS = functools.partial(pltpu.CompilerParams, vmem_limit_bytes=60 * 1024 * 1024)


def position(pick, slot):
    if_two = jnp.where(slot == 0, 0, jnp.where(slot == 3, 1, slot + 1))
    if_one = jnp.where(slot == 1, 2, jnp.where(slot == 2, 1, slot))
    return jnp.where(pick == 0, slot, jnp.where(pick == 1, if_one, if_two))


def slot_at(pick, h):
    if h == 0:
        return 0, 1 + pick
    return jnp.where(pick == 0, 2, 1), jnp.where(pick == 2, 2, 3)


def turn_of(slot):
    return jnp.where(slot == 1, -1, jnp.where(slot == 2, 1, 0))


def pair_places(assign, pairing, rnd, d, h):
    slots = slot_at(pairing[rnd, d], h)
    if rnd == 0:
        return [assign[d * SLOTS + slot] for slot in slots]
    places = []
    for slot in slots:
        home = lax.rem(d + turn_of(slot) + UNITS, UNITS)
        places.append(home * SLOTS + position(pairing[0, home], slot))
    return places


def lanes_of(shape):
    return lax.broadcasted_iota(jnp.int32, shape, 1)


def rows_of(shape):
    return lax.broadcasted_iota(jnp.int32, shape, 0)


def split(value):
    high = value.astype(BF16)
    return high, (value - high.astype(F32)).astype(BF16)


def turned(pair):
    rolled = pltpu.roll(pair, 64, 1)
    return jnp.where(lanes_of(pair.shape) < 64, rolled, -rolled)


def unpack(unit):
    lane, row = lanes_of(unit.shape), rows_of(unit.shape)
    left = lane < 64
    column = jnp.where(left, lane, lane - 64)
    flipped = jnp.concatenate([unit, unit], axis=0).T
    rolled = pltpu.roll(unit, 64, 1)
    tops = []
    for h in range(2):
        here = jnp.where(left, unit, rolled) if h == 0 else jnp.where(left, rolled, unit)
        there = flipped[64 * h : 64 * h + 64]
        real = jnp.where(row <= column, here, there)
        imag = jnp.where(row > column, here, jnp.where(row < column, -there, 0.0))
        tops.append(jnp.where(left, real, imag))
    return tops


def pack(first, second):
    lane, row = lanes_of(first.shape), rows_of(first.shape)
    left = lane < 64
    real = jnp.where(left, first, second)
    imag = pltpu.roll(jnp.where(left, second, first), 64, 1)
    return jnp.where(row <= jnp.where(left, lane, lane - 64), real, imag)


def nt_dot(a, b):
    return lax.dot_general(a, b, (((1,), (1,)), ((), ())), preferred_element_type=F32)


def parts_of(table, a, b, swapped=False):
    order = (1, 0) if swapped else (0, 1)
    return jnp.concatenate([table[k, half] for half in order for k in (a, b)], axis=0)


def gram_top(tables, a, b, swapped):
    high = parts_of(tables[0], a, b, swapped)
    low = parts_of(tables[1], a, b, swapped)
    pair = slice(64, 128) if swapped else slice(0, 64)
    lhs = jnp.concatenate([high[pair], low[pair]], axis=1)
    rhs = jnp.concatenate([high, high], axis=1)
    return nt_dot(lhs, rhs) + nt_dot(high[pair], low)


def applied(top, tables, a, b):
    high, low = parts_of(tables[0], a, b), parts_of(tables[1], a, b)
    whigh, wlow = split(top)
    lhs = jnp.concatenate([whigh, wlow], axis=1)
    rhs = jnp.concatenate([high, high], axis=0)
    return jnp.dot(lhs, rhs, preferred_element_type=F32) + jnp.dot(
        whigh, low, preferred_element_type=F32
    )


def keep(tables, first, count, value):
    for index, whole in enumerate((value, turned(value))):
        for table, part in zip(tables, split(whole)):
            table[pl.ds(first, count), index] = part.reshape(count, BLOCK, 128)


def full(top):
    rolled = pltpu.roll(top, 64, 1)
    return jnp.concatenate([top, jnp.where(lanes_of(top.shape) < 64, -rolled, rolled)], axis=0)


def split3(value):
    first, second = split(value)
    rest = value - first.astype(F32) - second.astype(F32)
    return first, second, rest.astype(BF16)


def fdot(a, b):
    a1, a2, a3 = split3(a)
    b1, b2, b3 = split3(b)
    wide = jnp.concatenate([b1, b2], axis=1)
    main = jnp.dot(
        jnp.concatenate([a1, a2], axis=1),
        jnp.concatenate([wide, wide], axis=0),
        preferred_element_type=F32,
    )
    rest = jnp.dot(
        jnp.concatenate([a1, a3], axis=1),
        jnp.concatenate([b3, b1], axis=0),
        preferred_element_type=F32,
    )
    return main[:, :128] + (main[:, 128:] + rest)


def inverse_roots(tops):
    shape = tops[0].shape
    eye = jnp.where(lanes_of(shape) == rows_of(shape), 1.0, 0.0).astype(F32)
    scales = [jnp.sqrt(2.0 * jnp.sum(t * t, axis=(0, 1), keepdims=True)) for t in tops]
    upper = [t / s for t, s in zip(tops, scales)]
    lower = [1.5 * eye - 0.5 * u for u in upper]
    upper = [fdot(u, full(m)) for u, m in zip(upper, lower)]

    def step(_, carry):
        up, low = carry
        middle = [1.5 * eye - 0.5 * fdot(z, full(y)) for y, z in zip(up, low)]
        return (
            [fdot(y, full(m)) for y, m in zip(up, middle)],
            [fdot(m, full(z)) for z, m in zip(low, middle)],
        )

    upper, lower = lax.fori_loop(0, NS_STEPS - 2, step, (upper, lower))
    middle = [1.5 * eye - 0.5 * fdot(z, full(y)) for y, z in zip(upper, lower)]
    lower = [fdot(m, full(z)) for z, m in zip(lower, middle)]
    return [z * jnp.sqrt(ROWS / s) for z, s in zip(lower, scales)]


def order_in(i):
    return lax.rem(2 + 3 * i + 3 * (i * (i - 1) // 2), 4)


def order_out(i):
    return lax.rem(3 * i + 3 * (i * (i - 1) // 2), 4)


def fused_kernel(
    assign, pairing, x_in, out, x_held, results, high0, low0, high1, low1, packed, from_core, relay,
    inbox, second_in, total, slices, from_z, mine_z, gathered, weights, x_sem, out_sem,
    core_send, core_recv, relay_send, relay_recv, inbox_send, inbox_recv, second_send, second_recv, zr_send,
    zr_recv, zg_send, zg_recv, wfull_send, wfull_recv, whalf_send, whalf_recv, wsecond_send,
    wsecond_recv, wcore_send, wcore_recv,
):
    blk, row = lax.axis_index("blk"), lax.axis_index("row")
    y_lo, z, x = blk // (NZ * NX), lax.rem(blk // NX, NZ), lax.rem(blk, NX)
    y_hi, core = row // 2, lax.rem(row, 2)
    y = y_hi * 2 + y_lo
    half = UNITS // 2
    p, q = x + core * (y - x), y + core * (x - y)

    def device(yy, zz, xx, cc):
        return (lax.rem(yy, 2) * (NZ * NX) + zz * NX + xx, (yy // 2) * 2 + cc)

    def placed(pp, qq):
        return device(qq + core * (pp - qq), z, pp + core * (qq - pp), core)

    def beside(direction):
        return placed(lax.rem(p + 1 + 2 * direction, 4), q)

    def across(distance):
        return placed(p, lax.rem(q + distance, 4))

    partner = device(y, z, x, 1 - core)

    def ring_device(step):
        return device(y, lax.rem(z + step, NZ), x, core)

    def my_chunk(da, db):
        return (lax.rem(p + da, 4) * 4 + lax.rem(q + db, 4)) * CHUNK

    def other_chunk(da, db):
        return (lax.rem(q + da, 4) * 4 + lax.rem(p + db, 4)) * CHUNK

    def each(first, last, body):
        def run(step, carry):
            body(step)
            return carry

        lax.fori_loop(first, last, run, 0)

    def remote(src, dst, send, recv, to):
        return pltpu.make_async_remote_copy(
            src_ref=src, dst_ref=dst, send_sem=send, recv_sem=recv, device_id=to, device_id_type=MESH
        )

    barrier = pltpu.get_barrier_semaphore()

    def greet(to):
        pl.semaphore_signal(barrier, inc=1, device_id=to, device_id_type=MESH)

    greet(partner)
    for direction in range(2):
        greet(beside(direction))
    for distance in range(1, 4):
        greet(across(distance))
    for step in range(1, NZ):
        greet(ring_device(step))

    def x_copy(group):
        return pltpu.make_async_copy(
            x_in.at[:, pl.ds(group * 2 * STEP, 2 * STEP)], x_held.at[group], x_sem.at[group]
        )

    def load_group(group):
        x_copy(group).wait()
        flat = x_held.at[group].reshape(64 * 2 * STEP, 128)
        for k in range(STEP):
            real = flat[pl.ds(2 * k, 64, stride=2 * STEP), :]
            imag = flat[pl.ds(2 * k + 1, 64, stride=2 * STEP), :]
            flipped = jnp.concatenate([real, imag], axis=0).T
            keep((high0, low0), 4 * (group * STEP + k), 4, flipped)

    each(0, GROUPS, lambda group: x_copy(group).start())
    each(0, GROUPS, load_group)
    pl.semaphore_wait(barrier, 6 + NZ - 1)

    def one_round(rnd, source):
        def core_copy(step):
            place = other_chunk(order_in(step // 4), order_in(lax.rem(step, 4)))
            return remote(
                packed.at[pl.ds((1 - core) * half + place, CHUNK)],
                from_core.at[rnd, pl.ds(place, CHUNK)],
                core_send.at[rnd, step], core_recv.at[rnd, step], partner,
            )

        def relay_copy(direction, slot, place):
            return remote(
                from_core.at[rnd, place + direction], relay.at[rnd, direction, slot],
                relay_send.at[rnd, direction, slot], relay_recv.at[rnd, direction, slot],
                beside(direction),
            )

        def inbox_copy(direction, slot, place):
            return remote(
                from_core.at[rnd, pl.ds(place, CHUNK)], inbox.at[rnd, direction, slot],
                inbox_send.at[rnd, direction, slot], inbox_recv.at[rnd, direction, slot],
                beside(direction),
            )

        def second_copy(ib, place):
            return remote(
                from_core.at[rnd, pl.ds(place, CHUNK)], second_in.at[rnd, ib],
                second_send.at[rnd, ib], second_recv.at[rnd, ib], across(order_in(ib)),
            )

        def gram_units(first):
            for u in range(CHUNK):
                tops = []
                for h in range(2):
                    a, b = pair_places(assign, pairing, rnd, first + u, h)
                    tops.append(gram_top(source, a, b, h == 1))
                packed[first + u] = pack(*tops)

        def compute(step):
            da, db = order_in(step // 4), order_in(lax.rem(step, 4))
            gram_units((1 - core) * half + other_chunk(da, db))
            core_copy(step).start()
            gram_units(core * half + my_chunk(da, db))

        def inbox_sum(slot):
            for direction in range(2):
                inbox_copy(direction, slot, 0).wait_recv()
            return inbox[rnd, 0, slot] + inbox[rnd, 1, slot]

        def ship(step):
            ia, ib = step // 4, lax.rem(step, 4)
            place = my_chunk(order_in(ia), order_in(ib))
            chunk = pl.ds(place, CHUNK)
            core_copy(step).wait_recv()
            from_core[rnd, chunk] += packed[pl.ds(core * half + place, CHUNK)]

            @pl.when(ia == 0)
            def _():
                for direction in range(2):
                    relay_copy(direction, ib, place).start()

            for direction in range(2):

                @pl.when(ia == 1 + direction)
                def _(direction=direction):
                    relay_copy(direction, ib, place).wait_recv()
                    from_core[rnd, place + direction] += relay[rnd, direction, ib]
                    inbox_copy(direction, ib, place).start()

            @pl.when(ia == 3)
            def _():
                from_core[rnd, chunk] += inbox_sum(ib)
                second_copy(ib, place).start()

        def advance(step):
            compute(step)
            ship(step - 1)

        compute(0)
        each(1, 16, advance)
        core_copy(15).wait_recv()
        place = my_chunk(0, 0)
        total[...] = (
            from_core[rnd, pl.ds(place, CHUNK)]
            + packed[pl.ds(core * half + place, CHUNK)]
            + inbox_sum(3)
        )
        for ib in range(3):
            second_copy(ib, 0).wait_recv()
            total[...] += second_in[rnd, ib]

        for k in range(NZ):
            slices[k] = total[:, k * SLICE : (k + 1) * SLICE, :]

        def zr_copy(step):
            return remote(
                slices.at[lax.rem(z + step, NZ)], from_z.at[rnd, step],
                zr_send.at[rnd, step], zr_recv.at[rnd, step], ring_device(step),
            )

        def zg_copy(step):
            return remote(
                mine_z, gathered.at[rnd, z], zg_send.at[rnd, step], zg_recv.at[rnd, step],
                ring_device(step),
            )

        far_first = (4, 3, 5, 2, 6, 1, 7)
        for step in far_first:
            zr_copy(step).start()
        acc = slices[z]
        for step in reversed(far_first):
            zr_copy(step).wait_recv()
            acc = acc + from_z[rnd, step]
        mine_z[...] = acc
        for step in far_first:
            zg_copy(step).start()
        gathered[rnd, z] = acc
        for step in reversed(far_first):
            zg_copy(step).wait_recv()

        tops = []
        for u in range(CHUNK):
            tops.extend(unpack(gathered[rnd, :, u].reshape(64, 128)))
        roots = inverse_roots(tops)
        mine = core * half + place
        for u in range(CHUNK):
            weights[rnd, mine + u] = pack(roots[2 * u], pltpu.roll(roots[2 * u + 1], 64, 1))

        def wfull_copy(direction, slot, first):
            part = weights.at[rnd, pl.ds(first, CHUNK)]
            return remote(
                part, part, wfull_send.at[rnd, direction, slot], wfull_recv.at[rnd, direction, slot],
                beside(direction),
            )

        def whalf_copy(direction, slot, first):
            part = weights.at[rnd, first + direction]
            return remote(
                part, part, whalf_send.at[rnd, direction, slot], whalf_recv.at[rnd, direction, slot],
                beside(direction),
            )

        def wsecond_copy(ib, first):
            part = weights.at[rnd, pl.ds(first, CHUNK)]
            return remote(
                part, part, wsecond_send.at[rnd, ib], wsecond_recv.at[rnd, ib],
                across(4 - order_out(ib)),
            )

        def my_units(step):
            return core * half + my_chunk(order_out(step // 4), order_out(lax.rem(step, 4)))

        def other_units(step):
            return (1 - core) * half + other_chunk(order_out(step // 4), order_out(lax.rem(step, 4)))

        def wcore_copy(step):
            part = weights.at[rnd, pl.ds(my_units(step), CHUNK)]
            return remote(
                part, part, wcore_send.at[rnd, step], wcore_recv.at[rnd, step], partner
            )

        def out_copy(first, which):
            place = pl.ds(SLOTS * first, SLOTS * CHUNK)
            return pltpu.make_async_copy(results.at[place], out.at[place], out_sem.at[which])

        def apply_units(first, which):
            for u in range(CHUNK):
                d = first + u
                tops = unpack(weights[rnd, d])
                for h in range(2):
                    a, b = pair_places(assign, pairing, rnd, d, h)
                    new = applied(tops[h], source, a, b)
                    place = SLOTS * d + 2 * h
                    if rnd == 0:
                        keep((high1, low1), place, 2, new)
                    else:
                        results[pl.ds(place, 2)] = new.reshape(2, BLOCK, 128)
            if rnd == 1:
                out_copy(first, which).start()

        def apply_other(step):
            wcore_copy(step).wait_recv()
            apply_units(other_units(step), 16 + step)

        def take(step):
            ia, ib = step // 4, lax.rem(step, 4)
            first = my_units(step)

            @pl.when(ia == 0)
            def _():
                wsecond_copy(ib, first).wait_recv()
                for direction in range(2):
                    wfull_copy(direction, ib, first).start()

            for direction in range(2):

                @pl.when(ia == 1 + direction)
                def _(direction=direction):
                    wfull_copy(direction, ib, first).wait_recv()
                    whalf_copy(direction, ib, first).start()

            @pl.when(ia == 3)
            def _():
                for direction in range(2):
                    whalf_copy(direction, ib, first).wait_recv()

            wcore_copy(step).start()
            apply_units(first, step)
            apply_other(step - 1)

        for ib in (3, 2, 1):
            wsecond_copy(ib, mine).start()
        for direction in range(2):
            wfull_copy(direction, 0, mine).start()
        wcore_copy(0).start()
        apply_units(mine, 0)
        each(1, 16, take)
        apply_other(15)

        def drain_core(step):
            core_copy(step).wait_send()
            wcore_copy(step).wait_send()
            if rnd == 1:
                out_copy(0, step).wait()
                out_copy(0, 16 + step).wait()

        def drain_plane(slot):
            for direction in range(2):
                relay_copy(direction, slot, 0).wait_send()
                inbox_copy(direction, slot, 0).wait_send()
                wfull_copy(direction, slot, 0).wait_send()
                whalf_copy(direction, slot, 0).wait_send()

        def drain_second(ib):
            second_copy(ib, 0).wait_send()
            wsecond_copy(ib + 1, 0).wait_send()

        def drain_z(step):
            zr_copy(step).wait_send()
            zg_copy(step).wait_send()

        each(0, 16, drain_core)
        each(0, 4, drain_plane)
        each(0, 3, drain_second)
        each(1, NZ, drain_z)

    one_round(0, (high0, low0))
    one_round(1, (high1, low1))


def last_kernel(assign, pairing, source, out, places):
    @pl.when(pl.program_id(0) == 0)
    def _():
        def unit(d, carry):
            up = jnp.where(d == UNITS - 1, 0, d + 1)
            down = jnp.where(d == 0, UNITS - 1, d - 1)
            here, above, below = pairing[1, d], pairing[1, up], pairing[1, down]
            places[assign[SLOTS * d]] = SLOTS * d
            places[assign[SLOTS * d + 1]] = SLOTS * up + jnp.where(above == 0, 1, 2)
            places[assign[SLOTS * d + 2]] = SLOTS * down + jnp.where(
                below == 0, 2, jnp.where(below == 1, 1, 3)
            )
            places[assign[SLOTS * d + 3]] = SLOTS * d + jnp.where(here == 2, 1, 3)
            return carry

        lax.fori_loop(0, UNITS, unit, 0, unroll=4)

    flat = out.reshape(64 * 2 * STEP, 128)
    for k in range(STEP):
        ct = pl.program_id(0) * STEP + k
        parts = [source[places[4 * ct + j]] for j in range(4)]
        flipped = jnp.concatenate(parts, axis=0).T
        flat[pl.ds(2 * k, 64, stride=2 * STEP), :] = flipped[:64]
        flat[pl.ds(2 * k + 1, 64, stride=2 * STEP), :] = flipped[64:]


SMEM = pl.BlockSpec(memory_space=pltpu.SMEM)
VMEM = pl.BlockSpec(memory_space=pltpu.VMEM)
TABLE = (BLOCKS, BLOCK, 128)


def rounds(assignment, pairing, x):
    dma = pltpu.SemaphoreType.DMA
    chunks, plane, second, ring = dma((2, 16)), dma((2, 2, 4)), dma((2, 4)), dma((2, NZ))
    part = pltpu.VMEM((BLOCKS, 2, BLOCK, 128), BF16)
    return pl.pallas_call(
        fused_kernel,
        out_shape=jax.ShapeDtypeStruct(TABLE, F32),
        in_specs=[SMEM, SMEM, pl.BlockSpec(memory_space=pl.ANY)],
        out_specs=pl.BlockSpec(memory_space=pl.ANY),
        scratch_shapes=[
            pltpu.VMEM((GROUPS, 64, 2 * STEP, 128), F32),
            pltpu.VMEM(TABLE, F32),
            part, part, part, part,
            pltpu.VMEM((UNITS, 64, 128), F32),
            pltpu.VMEM((2, UNITS // 2, 64, 128), F32),
            pltpu.VMEM((2, 2, 4, 64, 128), F32),
            pltpu.VMEM((2, 2, 4, CHUNK, 64, 128), F32),
            pltpu.VMEM((2, 3, CHUNK, 64, 128), F32),
            pltpu.VMEM((CHUNK, 64, 128), F32),
            pltpu.VMEM((NZ, CHUNK, SLICE, 128), F32),
            pltpu.VMEM((2, NZ, CHUNK, SLICE, 128), F32),
            pltpu.VMEM((CHUNK, SLICE, 128), F32),
            pltpu.VMEM((2, NZ, CHUNK, SLICE, 128), F32),
            pltpu.VMEM((2, UNITS, 64, 128), F32),
            dma((GROUPS,)), dma((32,)),
            chunks, chunks, plane, plane, plane, plane, second, second, ring, ring, ring, ring,
            plane, plane, plane, plane, second, second, chunks, chunks,
        ],
        compiler_params=PARAMS(collective_id=0, has_side_effects=True),
        name="rounds",
    )(assignment, pairing, x)


def unturned(assignment, pairing, source):
    shape = (64, BLOCKS // 2, 128)
    return pl.pallas_call(
        last_kernel,
        out_shape=jax.ShapeDtypeStruct(shape, F32),
        grid=(BLOCKS // 4 // STEP,),
        in_specs=[SMEM, SMEM, VMEM],
        out_specs=pl.BlockSpec((64, 2 * STEP, 128), lambda i: (0, i, 0)),
        scratch_shapes=[pltpu.SMEM((BLOCKS,), jnp.int32)],
        compiler_params=PARAMS(),
        name="unturn",
    )(assignment, pairing, source)


def on_device(transmission, assignment, pairing):
    rows, _, cols = transmission.shape
    x = transmission.reshape(rows, 2, cols // 128, 128).transpose(0, 2, 1, 3).reshape(rows, -1, 128)
    turned_blocks = rounds(assignment, pairing, x)
    out = unturned(assignment, pairing, turned_blocks)
    out = out.reshape(rows, cols // 128, 2, 128).transpose(0, 2, 1, 3)
    return out.reshape(rows, 2, cols)


def solution(mesh):
    placed = (P(("blk", "row"), None, None), P(), P())
    return jax.shard_map(
        on_device,
        mesh=mesh,
        in_specs=placed,
        out_specs=P(("blk", "row"), None, None),
        check_vma=False,
    )
```

```python
import functools

import jax
import jax.numpy as jnp
from jax import lax
from jax.experimental import pallas as pl
from jax.experimental.pallas import tpu as pltpu
from jax.sharding import PartitionSpec as P

ROWS = 16384
BLOCK = 32
SLOTS = 4
NS_STEPS = 6
UNITS = 64
BLOCKS = 256
MESH = pl.DeviceIdType.MESH
F32 = jnp.float32
BF16 = jnp.bfloat16
NX, NY, NZ = 4, 4, 8
NXY = NX * NY
CHUNK = UNITS // 2 // NXY
DEPTH = 3 * 64
SLICE = DEPTH // NZ
STEP = 8
GROUPS = BLOCKS // 4 // STEP
PARAMS = functools.partial(pltpu.CompilerParams, vmem_limit_bytes=60 * 1024 * 1024)


def position(pick, slot):
    if_two = jnp.where(slot == 0, 0, jnp.where(slot == 3, 1, slot + 1))
    if_one = jnp.where(slot == 1, 2, jnp.where(slot == 2, 1, slot))
    return jnp.where(pick == 0, slot, jnp.where(pick == 1, if_one, if_two))


def slot_at(pick, h):
    if h == 0:
        return 0, 1 + pick
    return jnp.where(pick == 0, 2, 1), jnp.where(pick == 2, 2, 3)


def turn_of(slot):
    return jnp.where(slot == 1, -1, jnp.where(slot == 2, 1, 0))


def home_of(pairing, d, slot):
    home = lax.rem(d + turn_of(slot) + UNITS, UNITS)
    return home, position(pairing[0, home], slot)


def pair_places(assign, pairing, rnd, d, h):
    slots = slot_at(pairing[rnd, d], h)
    if rnd == 0:
        return [assign[d * SLOTS + slot] for slot in slots]
    places = []
    for slot in slots:
        home, place = home_of(pairing, d, slot)
        places.append(home * SLOTS + place)
    return places


def pair_around(assign, pairing, home, place):
    pick = pairing[0, home]
    in_first = place < 2
    first = jnp.where(in_first, 0, jnp.where(pick == 0, 2, 1))
    second = jnp.where(in_first, 1 + pick, jnp.where(pick == 2, 2, 3))
    return assign[home * SLOTS + first], assign[home * SLOTS + second]


def lanes_of(shape):
    return lax.broadcasted_iota(jnp.int32, shape, 1)


def rows_of(shape):
    return lax.broadcasted_iota(jnp.int32, shape, 0)


def split(value):
    high = value.astype(BF16)
    return high, (value - high.astype(F32)).astype(BF16)


def turned(pair):
    rolled = pltpu.roll(pair, 64, 1)
    return jnp.where(lanes_of(pair.shape) < 64, rolled, -rolled)


def unpack(unit):
    lane, row = lanes_of(unit.shape), rows_of(unit.shape)
    left = lane < 64
    column = jnp.where(left, lane, lane - 64)
    flipped = jnp.concatenate([unit, unit], axis=0).T
    rolled = pltpu.roll(unit, 64, 1)
    tops = []
    for h in range(2):
        here = jnp.where(left, unit, rolled) if h == 0 else jnp.where(left, rolled, unit)
        there = flipped[64 * h : 64 * h + 64]
        real = jnp.where(row <= column, here, there)
        imag = jnp.where(row > column, here, jnp.where(row < column, -there, 0.0))
        tops.append(jnp.where(left, real, imag))
    return tops


def pack(first, second):
    lane, row = lanes_of(first.shape), rows_of(first.shape)
    left = lane < 64
    real = jnp.where(left, first, second)
    imag = pltpu.roll(jnp.where(left, second, first), 64, 1)
    return jnp.where(row <= jnp.where(left, lane, lane - 64), real, imag)


def nt_dot(a, b):
    return lax.dot_general(a, b, (((1,), (1,)), ((), ())), preferred_element_type=F32)


def parts_of(table, a, b, swapped=False):
    order = (1, 0) if swapped else (0, 1)
    return jnp.concatenate([table[k, half] for half in order for k in (a, b)], axis=0)


def gram_top(tables, a, b, swapped):
    high = parts_of(tables[0], a, b, swapped)
    low = parts_of(tables[1], a, b, swapped)
    pair = slice(64, 128) if swapped else slice(0, 64)
    lhs = jnp.concatenate([high[pair], low[pair]], axis=1)
    rhs = jnp.concatenate([high, high], axis=1)
    return nt_dot(lhs, rhs) + nt_dot(high[pair], low)


def cross_top(tables, left, right):
    lhigh = jnp.concatenate([tables[0][k, 0] for k in left], axis=0)
    llow = jnp.concatenate([tables[1][k, 0] for k in left], axis=0)
    high, low = parts_of(tables[0], *right), parts_of(tables[1], *right)
    lhs = jnp.concatenate([lhigh, llow], axis=1)
    rhs = jnp.concatenate([high, high], axis=1)
    return nt_dot(lhs, rhs) + nt_dot(lhigh, low)


def applied(top, tables, a, b):
    high, low = parts_of(tables[0], a, b), parts_of(tables[1], a, b)
    whigh, wlow = split(top)
    lhs = jnp.concatenate([whigh, wlow], axis=1)
    rhs = jnp.concatenate([high, high], axis=0)
    return jnp.dot(lhs, rhs, preferred_element_type=F32) + jnp.dot(
        whigh, low, preferred_element_type=F32
    )


def keep(tables, first, count, value):
    for index, whole in enumerate((value, turned(value))):
        for table, part in zip(tables, split(whole)):
            table[pl.ds(first, count), index] = part.reshape(count, BLOCK, 128)


def full(top):
    rolled = pltpu.roll(top, 64, 1)
    return jnp.concatenate([top, jnp.where(lanes_of(top.shape) < 64, -rolled, rolled)], axis=0)


def split3(value):
    first, second = split(value)
    rest = value - first.astype(F32) - second.astype(F32)
    return first, second, rest.astype(BF16)


def fdot(a, b):
    a1, a2, a3 = split3(a)
    b1, b2, b3 = split3(b)
    wide = jnp.concatenate([b1, b2], axis=1)
    main = jnp.dot(
        jnp.concatenate([a1, a2], axis=1),
        jnp.concatenate([wide, wide], axis=0),
        preferred_element_type=F32,
    )
    rest = jnp.dot(
        jnp.concatenate([a1, a3], axis=1),
        jnp.concatenate([b3, b1], axis=0),
        preferred_element_type=F32,
    )
    return main[:, :128] + (main[:, 128:] + rest)


def inverse_roots(tops):
    shape = tops[0].shape
    eye = jnp.where(lanes_of(shape) == rows_of(shape), 1.0, 0.0).astype(F32)
    scales = [jnp.sqrt(2.0 * jnp.sum(t * t, axis=(0, 1), keepdims=True)) for t in tops]
    upper = [t / s for t, s in zip(tops, scales)]
    lower = [1.5 * eye - 0.5 * u for u in upper]
    upper = [fdot(u, full(m)) for u, m in zip(upper, lower)]

    def step(_, carry):
        up, low = carry
        middle = [1.5 * eye - 0.5 * fdot(z, full(y)) for y, z in zip(up, low)]
        return (
            [fdot(y, full(m)) for y, m in zip(up, middle)],
            [fdot(m, full(z)) for z, m in zip(low, middle)],
        )

    upper, lower = lax.fori_loop(0, NS_STEPS - 2, step, (upper, lower))
    middle = [1.5 * eye - 0.5 * fdot(z, full(y)) for y, z in zip(upper, lower)]
    lower = [fdot(m, full(z)) for z, m in zip(lower, middle)]
    return [z * jnp.sqrt(ROWS / s) for z, s in zip(lower, scales)]


def triple(left, middle, right):
    return fdot(fdot(left, full(middle)), full(right))


def sided(value, side, wanted, axis, back):
    moved = pltpu.roll(value, back, axis)
    return jnp.where(jnp.full(value.shape, side, jnp.int32) == wanted, value, moved)


def next_gram(cross, gram_u, gram_v, side_u, side_v):
    shape = cross.shape
    lane, row = lanes_of(shape), rows_of(shape)
    upper = sided(sided(cross, side_u, 0, 0, 32), side_v, 1, 1, 32)
    corner_u = sided(sided(gram_u, side_u, 0, 0, 32), side_u, 0, 1, 96)
    corner_v = sided(sided(gram_v, side_v, 1, 0, 32), side_v, 1, 1, 32)
    flipped = jnp.concatenate([upper, upper], axis=0).T
    lower = jnp.where(lane < 64, flipped[:64], -flipped[64:])
    early = lax.rem(lane, 64) < 32
    return jnp.where(
        row < 32, jnp.where(early, corner_u, upper), jnp.where(early, lower, corner_v)
    )


def order_in(i):
    return lax.rem(2 + 3 * i + 3 * (i * (i - 1) // 2), 4)


def order_out(i):
    return lax.rem(3 * i + 3 * (i * (i - 1) // 2), 4)


def fused_kernel(
    assign, pairing, x_in, out, x_held, results, high0, low0, high1, low1, packed, from_core, relay,
    inbox, second_in, total, slices, from_z, mine_z, gathered, weights, near, roots_near, grams_near,
    near_in, x_sem, out_sem,
    core_send, core_recv, relay_send, relay_recv, inbox_send, inbox_recv, second_send, second_recv, zr_send,
    zr_recv, zg_send, zg_recv, wfull_send, wfull_recv, whalf_send, whalf_recv, wsecond_send,
    wsecond_recv, wcore_send, wcore_recv, near_send, near_recv,
):
    blk, row = lax.axis_index("blk"), lax.axis_index("row")
    y_lo, z, x = blk // (NZ * NX), lax.rem(blk // NX, NZ), lax.rem(blk, NX)
    y_hi, core = row // 2, lax.rem(row, 2)
    y = y_hi * 2 + y_lo
    half = UNITS // 2
    p, q = x + core * (y - x), y + core * (x - y)

    def device(yy, zz, xx, cc):
        return (lax.rem(yy, 2) * (NZ * NX) + zz * NX + xx, (yy // 2) * 2 + cc)

    def placed(pp, qq):
        return device(qq + core * (pp - qq), z, pp + core * (qq - pp), core)

    def beside(direction):
        return placed(lax.rem(p + 1 + 2 * direction, 4), q)

    def across(distance):
        return placed(p, lax.rem(q + distance, 4))

    partner = device(y, z, x, 1 - core)

    def owner(move):
        chunk = lax.rem(core * NXY + p * 4 + q + move, 2 * NXY)
        cc, pp, qq = chunk // NXY, lax.rem(chunk // 4, 4), lax.rem(chunk, 4)
        return device(qq + cc * (pp - qq), z, pp + cc * (qq - pp), cc)

    def ring_device(step):
        return device(y, lax.rem(z + step, NZ), x, core)

    def my_chunk(da, db):
        return (lax.rem(p + da, 4) * 4 + lax.rem(q + db, 4)) * CHUNK

    def other_chunk(da, db):
        return (lax.rem(q + da, 4) * 4 + lax.rem(p + db, 4)) * CHUNK

    def each(first, last, body):
        def run(step, carry):
            body(step)
            return carry

        lax.fori_loop(first, last, run, 0)

    def remote(src, dst, send, recv, to):
        return pltpu.make_async_remote_copy(
            src_ref=src, dst_ref=dst, send_sem=send, recv_sem=recv, device_id=to, device_id_type=MESH
        )

    barrier = pltpu.get_barrier_semaphore()

    def greet(to):
        pl.semaphore_signal(barrier, inc=1, device_id=to, device_id_type=MESH)

    greet(partner)
    for direction in range(2):
        greet(beside(direction))
    for distance in range(1, 4):
        greet(across(distance))
    for step in range(1, NZ):
        greet(ring_device(step))
    greet(owner(1))
    greet(owner(2 * NXY - 1))

    def x_copy(group):
        return pltpu.make_async_copy(
            x_in.at[:, pl.ds(group * 2 * STEP, 2 * STEP)], x_held.at[group], x_sem.at[group]
        )

    def load_group(group):
        x_copy(group).wait()
        flat = x_held.at[group].reshape(64 * 2 * STEP, 128)
        for k in range(STEP):
            real = flat[pl.ds(2 * k, 64, stride=2 * STEP), :]
            imag = flat[pl.ds(2 * k + 1, 64, stride=2 * STEP), :]
            flipped = jnp.concatenate([real, imag], axis=0).T
            keep((high0, low0), 4 * (group * STEP + k), 4, flipped)

    each(0, GROUPS, lambda group: x_copy(group).start())
    each(0, GROUPS, load_group)
    pl.semaphore_wait(barrier, 8 + NZ - 1)

    def reduced():
        source = (high0, low0)

        def core_copy(step):
            place = other_chunk(order_in(step // 4), order_in(lax.rem(step, 4)))
            return remote(
                packed.at[pl.ds((1 - core) * half + place, CHUNK)],
                from_core.at[pl.ds(place, CHUNK)],
                core_send.at[step], core_recv.at[step], partner,
            )

        def relay_copy(direction, slot, place):
            return remote(
                from_core.at[place + direction], relay.at[direction, slot],
                relay_send.at[direction, slot], relay_recv.at[direction, slot],
                beside(direction),
            )

        def inbox_copy(direction, slot, place):
            return remote(
                from_core.at[pl.ds(place, CHUNK)], inbox.at[direction, slot],
                inbox_send.at[direction, slot], inbox_recv.at[direction, slot],
                beside(direction),
            )

        def second_copy(ib, place):
            return remote(
                from_core.at[pl.ds(place, CHUNK)], second_in.at[ib],
                second_send.at[ib], second_recv.at[ib], across(order_in(ib)),
            )

        def gram_units(first):
            for u in range(CHUNK):
                d = first + u
                tops = []
                for h in range(2):
                    a, b = pair_places(assign, pairing, 0, d, h)
                    tops.append(gram_top(source, a, b, h == 1))
                    slots = slot_at(pairing[1, d], h)
                    around = [
                        pair_around(assign, pairing, *home_of(pairing, d, slot)) for slot in slots
                    ]
                    packed[d, pl.ds(64 + 64 * h, 64)] = cross_top(source, *around)
                packed[d, pl.ds(0, 64)] = pack(*tops)

        def compute(step):
            da, db = order_in(step // 4), order_in(lax.rem(step, 4))
            gram_units((1 - core) * half + other_chunk(da, db))
            core_copy(step).start()
            gram_units(core * half + my_chunk(da, db))

        def inbox_sum(slot):
            for direction in range(2):
                inbox_copy(direction, slot, 0).wait_recv()
            return inbox[0, slot] + inbox[1, slot]

        def ship(step):
            ia, ib = step // 4, lax.rem(step, 4)
            place = my_chunk(order_in(ia), order_in(ib))
            chunk = pl.ds(place, CHUNK)
            core_copy(step).wait_recv()
            from_core[chunk] += packed[pl.ds(core * half + place, CHUNK)]

            @pl.when(ia == 0)
            def _():
                for direction in range(2):
                    relay_copy(direction, ib, place).start()

            for direction in range(2):

                @pl.when(ia == 1 + direction)
                def _(direction=direction):
                    relay_copy(direction, ib, place).wait_recv()
                    from_core[place + direction] += relay[direction, ib]
                    inbox_copy(direction, ib, place).start()

            @pl.when(ia == 3)
            def _():
                from_core[chunk] += inbox_sum(ib)
                second_copy(ib, place).start()

        def advance(step):
            compute(step)
            ship(step - 1)

        compute(0)
        each(1, 16, advance)
        core_copy(15).wait_recv()
        place = my_chunk(0, 0)
        total[...] = (
            from_core[pl.ds(place, CHUNK)]
            + packed[pl.ds(core * half + place, CHUNK)]
            + inbox_sum(3)
        )
        for ib in range(3):
            second_copy(ib, 0).wait_recv()
            total[...] += second_in[ib]

        for k in range(NZ):
            slices[k] = total[:, k * SLICE : (k + 1) * SLICE, :]

        def zr_copy(step):
            return remote(
                slices.at[lax.rem(z + step, NZ)], from_z.at[step],
                zr_send.at[step], zr_recv.at[step], ring_device(step),
            )

        def zg_copy(step):
            return remote(
                mine_z, gathered.at[z], zg_send.at[step], zg_recv.at[step],
                ring_device(step),
            )

        far_first = (4, 3, 5, 2, 6, 1, 7)
        for step in far_first:
            zr_copy(step).start()
        acc = slices[z]
        for step in reversed(far_first):
            zr_copy(step).wait_recv()
            acc = acc + from_z[step]
        mine_z[...] = acc
        for step in far_first:
            zg_copy(step).start()
        gathered[z] = acc
        for step in reversed(far_first):
            zg_copy(step).wait_recv()

        def drain_core(step):
            core_copy(step).wait_send()

        def drain_plane(slot):
            for direction in range(2):
                relay_copy(direction, slot, 0).wait_send()
                inbox_copy(direction, slot, 0).wait_send()

        def drain_second(ib):
            second_copy(ib, 0).wait_send()

        def drain_z(step):
            zr_copy(step).wait_send()
            zg_copy(step).wait_send()

        def drain():
            each(0, 16, drain_core)
            each(0, 4, drain_plane)
            each(0, 3, drain_second)
            each(1, NZ, drain_z)

        return drain

    def handing(rnd, source):
        mine = core * half + my_chunk(0, 0)

        def wfull_copy(direction, slot, first):
            part = weights.at[rnd, pl.ds(first, CHUNK)]
            return remote(
                part, part, wfull_send.at[rnd, direction, slot], wfull_recv.at[rnd, direction, slot],
                beside(direction),
            )

        def whalf_copy(direction, slot, first):
            part = weights.at[rnd, first + direction]
            return remote(
                part, part, whalf_send.at[rnd, direction, slot], whalf_recv.at[rnd, direction, slot],
                beside(direction),
            )

        def wsecond_copy(ib, first):
            part = weights.at[rnd, pl.ds(first, CHUNK)]
            return remote(
                part, part, wsecond_send.at[rnd, ib], wsecond_recv.at[rnd, ib],
                across(4 - order_out(ib)),
            )

        def my_units(step):
            return core * half + my_chunk(order_out(step // 4), order_out(lax.rem(step, 4)))

        def other_units(step):
            return (1 - core) * half + other_chunk(order_out(step // 4), order_out(lax.rem(step, 4)))

        def wcore_copy(step):
            part = weights.at[rnd, pl.ds(my_units(step), CHUNK)]
            return remote(
                part, part, wcore_send.at[rnd, step], wcore_recv.at[rnd, step], partner
            )

        def out_copy(first, which):
            place = pl.ds(SLOTS * first, SLOTS * CHUNK)
            return pltpu.make_async_copy(results.at[place], out.at[place], out_sem.at[which])

        def apply_units(first, which):
            for u in range(CHUNK):
                d = first + u
                tops = unpack(weights[rnd, d])
                for h in range(2):
                    a, b = pair_places(assign, pairing, rnd, d, h)
                    new = applied(tops[h], source, a, b)
                    place = SLOTS * d + 2 * h
                    if rnd == 0:
                        keep((high1, low1), place, 2, new)
                    else:
                        results[pl.ds(place, 2)] = new.reshape(2, BLOCK, 128)
            if rnd == 1:
                out_copy(first, which).start()

        def apply_other(step):
            wcore_copy(step).wait_recv()
            apply_units(other_units(step), 16 + step)

        def take(step):
            ia, ib = step // 4, lax.rem(step, 4)
            first = my_units(step)

            @pl.when(ia == 0)
            def _():
                wsecond_copy(ib, first).wait_recv()
                for direction in range(2):
                    wfull_copy(direction, ib, first).start()

            @pl.when(ia == 1)
            def _():
                for direction in range(2):
                    whole = my_units(step + 4 * direction)
                    wfull_copy(direction, ib, whole).wait_recv()
                    whalf_copy(direction, ib, whole).start()

            @pl.when(ia == 3)
            def _():
                for direction in range(2):
                    whalf_copy(direction, ib, first).wait_recv()

            wcore_copy(step).start()
            apply_units(first, step)
            apply_other(step - 1)

        def begin():
            for ib in (3, 2, 1):
                wsecond_copy(ib, mine).start()
            for direction in range(2):
                wfull_copy(direction, 0, mine).start()
            wcore_copy(0).start()

        def finish():
            apply_units(mine, 0)
            each(1, 16, take)
            apply_other(15)

        def drain_core(step):
            wcore_copy(step).wait_send()
            if rnd == 1:
                out_copy(0, step).wait()
                out_copy(0, 16 + step).wait()

        def drain_plane(slot):
            for direction in range(2):
                wfull_copy(direction, slot, 0).wait_send()
                whalf_copy(direction, slot, 0).wait_send()

        def drain():
            each(0, 16, drain_core)
            each(0, 4, drain_plane)
            each(1, 4, lambda ib: wsecond_copy(ib, 0).wait_send())

        return begin, finish, drain

    drain_reduced = reduced()
    begin0, finish0, drain0 = handing(0, (high0, low0))
    begin1, finish1, drain1 = handing(1, (high1, low1))
    mine = core * half + my_chunk(0, 0)

    units = [gathered[:, u].reshape(DEPTH, 128) for u in range(CHUNK)]
    tops = []
    for unit in units:
        tops.extend(unpack(unit[:64]))
    roots = inverse_roots(tops)

    def packed_pair(values, u):
        return pack(values[2 * u], pltpu.roll(values[2 * u + 1], 64, 1))

    def near_copy(which):
        return remote(
            near.at[1 - which], near_in.at[which], near_send.at[which], near_recv.at[which],
            owner(1 if which == 0 else 2 * NXY - 1),
        )

    inner = [triple(w, g, w) for w, g in zip(roots, tops)]
    for u in range(CHUNK):
        near[u, 0] = packed_pair(roots, u)
        near[u, 1] = packed_pair(inner, u)
    for which in range(2):
        near_copy(which).start()
    for u in range(CHUNK):
        weights[0, mine + u] = near[u, 0]
        for h in range(2):
            roots_near[2 + 2 * u + h] = roots[2 * u + h]
            grams_near[2 + 2 * u + h] = inner[2 * u + h]
    begin0()
    for which in range(2):
        near_copy(which).wait_recv()
        for kind, table in enumerate((roots_near, grams_near)):
            for h, top in enumerate(unpack(near_in[which, kind])):
                table[6 * which + h] = top

    tops = []
    for u in range(CHUNK):
        for h in range(2):
            d = mine + u
            found = []
            for slot in slot_at(pairing[1, d], h):
                _, place = home_of(pairing, d, slot)
                index = 2 * (1 + u + turn_of(slot)) + place // 2
                found.append((index, lax.rem(place, 2)))
            (left, side_u), (right, side_v) = found
            cross = triple(
                roots_near[left], units[u][64 + 64 * h : 128 + 64 * h], roots_near[right]
            )
            tops.append(next_gram(cross, grams_near[left], grams_near[right], side_u, side_v))
    roots = inverse_roots(tops)
    for u in range(CHUNK):
        weights[1, mine + u] = packed_pair(roots, u)
    begin1()
    finish0()
    finish1()
    drain_reduced()
    drain0()
    drain1()
    for which in range(2):
        near_copy(which).wait_send()


def last_kernel(assign, pairing, source, out, places):
    @pl.when(pl.program_id(0) == 0)
    def _():
        def unit(d, carry):
            up = jnp.where(d == UNITS - 1, 0, d + 1)
            down = jnp.where(d == 0, UNITS - 1, d - 1)
            here, above, below = pairing[1, d], pairing[1, up], pairing[1, down]
            places[assign[SLOTS * d]] = SLOTS * d
            places[assign[SLOTS * d + 1]] = SLOTS * up + jnp.where(above == 0, 1, 2)
            places[assign[SLOTS * d + 2]] = SLOTS * down + jnp.where(
                below == 0, 2, jnp.where(below == 1, 1, 3)
            )
            places[assign[SLOTS * d + 3]] = SLOTS * d + jnp.where(here == 2, 1, 3)
            return carry

        lax.fori_loop(0, UNITS, unit, 0, unroll=4)

    flat = out.reshape(64 * 2 * STEP, 128)
    for k in range(STEP):
        ct = pl.program_id(0) * STEP + k
        parts = [source[places[4 * ct + j]] for j in range(4)]
        flipped = jnp.concatenate(parts, axis=0).T
        flat[pl.ds(2 * k, 64, stride=2 * STEP), :] = flipped[:64]
        flat[pl.ds(2 * k + 1, 64, stride=2 * STEP), :] = flipped[64:]


SMEM = pl.BlockSpec(memory_space=pltpu.SMEM)
VMEM = pl.BlockSpec(memory_space=pltpu.VMEM)
TABLE = (BLOCKS, BLOCK, 128)


def rounds(assignment, pairing, x):
    dma = pltpu.SemaphoreType.DMA
    chunks, plane, second, ring = dma((2, 16)), dma((2, 2, 4)), dma((2, 4)), dma((NZ,))
    part = pltpu.VMEM((BLOCKS, 2, BLOCK, 128), BF16)
    return pl.pallas_call(
        fused_kernel,
        out_shape=jax.ShapeDtypeStruct(TABLE, F32),
        in_specs=[SMEM, SMEM, pl.BlockSpec(memory_space=pl.ANY)],
        out_specs=pl.BlockSpec(memory_space=pl.ANY),
        scratch_shapes=[
            pltpu.VMEM((GROUPS, 64, 2 * STEP, 128), F32),
            pltpu.VMEM(TABLE, F32),
            part, part, part, part,
            pltpu.VMEM((UNITS, DEPTH, 128), F32),
            pltpu.VMEM((UNITS // 2, DEPTH, 128), F32),
            pltpu.VMEM((2, 4, DEPTH, 128), F32),
            pltpu.VMEM((2, 4, CHUNK, DEPTH, 128), F32),
            pltpu.VMEM((3, CHUNK, DEPTH, 128), F32),
            pltpu.VMEM((CHUNK, DEPTH, 128), F32),
            pltpu.VMEM((NZ, CHUNK, SLICE, 128), F32),
            pltpu.VMEM((NZ, CHUNK, SLICE, 128), F32),
            pltpu.VMEM((CHUNK, SLICE, 128), F32),
            pltpu.VMEM((NZ, CHUNK, SLICE, 128), F32),
            pltpu.VMEM((2, UNITS, 64, 128), F32),
            pltpu.VMEM((2, 2, 64, 128), F32),
            pltpu.VMEM((8, 64, 128), F32),
            pltpu.VMEM((8, 64, 128), F32),
            pltpu.VMEM((2, 2, 64, 128), F32),
            dma((GROUPS,)), dma((32,)),
            dma((16,)), dma((16,)), dma((2, 4)), dma((2, 4)), dma((2, 4)), dma((2, 4)),
            dma((4,)), dma((4,)), ring, ring, ring, ring,
            plane, plane, plane, plane, second, second, chunks, chunks, dma((2,)), dma((2,)),
        ],
        compiler_params=PARAMS(collective_id=0, has_side_effects=True),
        name="rounds",
    )(assignment, pairing, x)


def unturned(assignment, pairing, source):
    shape = (64, BLOCKS // 2, 128)
    return pl.pallas_call(
        last_kernel,
        out_shape=jax.ShapeDtypeStruct(shape, F32),
        grid=(BLOCKS // 4 // STEP,),
        in_specs=[SMEM, SMEM, VMEM],
        out_specs=pl.BlockSpec((64, 2 * STEP, 128), lambda i: (0, i, 0)),
        scratch_shapes=[pltpu.SMEM((BLOCKS,), jnp.int32)],
        compiler_params=PARAMS(),
        name="unturn",
    )(assignment, pairing, source)


def on_device(transmission, assignment, pairing):
    rows, _, cols = transmission.shape
    x = transmission.reshape(rows, 2, cols // 128, 128).transpose(0, 2, 1, 3).reshape(rows, -1, 128)
    turned_blocks = rounds(assignment, pairing, x)
    out = unturned(assignment, pairing, turned_blocks)
    out = out.reshape(rows, cols // 128, 2, 128).transpose(0, 2, 1, 3)
    return out.reshape(rows, 2, cols)


def solution(mesh):
    placed = (P(("blk", "row"), None, None), P(), P())
    return jax.shard_map(
        on_device,
        mesh=mesh,
        in_specs=placed,
        out_specs=P(("blk", "row"), None, None),
        check_vma=False,
    )
```

```python
import functools

import jax
import jax.numpy as jnp
from jax import lax
from jax.experimental import pallas as pl
from jax.experimental.pallas import tpu as pltpu
from jax.sharding import PartitionSpec as P

ROWS = 16384
BLOCK = 32
SLOTS = 4
NS_STEPS = 6
UNITS = 64
BLOCKS = 256
MESH = pl.DeviceIdType.MESH
F32 = jnp.float32
BF16 = jnp.bfloat16
NX, NY, NZ = 4, 4, 8
NXY = NX * NY
CHUNK = UNITS // 2 // NXY
DEPTH = 3 * 64
SLICES = (64 // NZ, 128 // NZ)
STEP = 8
GROUPS = BLOCKS // 4 // STEP
PARAMS = functools.partial(pltpu.CompilerParams, vmem_limit_bytes=60 * 1024 * 1024)


def position(pick, slot):
    if_two = jnp.where(slot == 0, 0, jnp.where(slot == 3, 1, slot + 1))
    if_one = jnp.where(slot == 1, 2, jnp.where(slot == 2, 1, slot))
    return jnp.where(pick == 0, slot, jnp.where(pick == 1, if_one, if_two))


def slot_at(pick, h):
    if h == 0:
        return 0, 1 + pick
    return jnp.where(pick == 0, 2, 1), jnp.where(pick == 2, 2, 3)


def turn_of(slot):
    return jnp.where(slot == 1, -1, jnp.where(slot == 2, 1, 0))


def home_of(pairing, d, slot):
    home = lax.rem(d + turn_of(slot) + UNITS, UNITS)
    return home, position(pairing[0, home], slot)


def pair_places(assign, pairing, rnd, d, h):
    slots = slot_at(pairing[rnd, d], h)
    if rnd == 0:
        return [assign[d * SLOTS + slot] for slot in slots]
    places = []
    for slot in slots:
        home, place = home_of(pairing, d, slot)
        places.append(home * SLOTS + place)
    return places


def pair_around(assign, pairing, home, place):
    pick = pairing[0, home]
    in_first = place < 2
    first = jnp.where(in_first, 0, jnp.where(pick == 0, 2, 1))
    second = jnp.where(in_first, 1 + pick, jnp.where(pick == 2, 2, 3))
    return assign[home * SLOTS + first], assign[home * SLOTS + second]


def lanes_of(shape):
    return lax.broadcasted_iota(jnp.int32, shape, 1)


def rows_of(shape):
    return lax.broadcasted_iota(jnp.int32, shape, 0)


def split(value):
    high = value.astype(BF16)
    return high, (value - high.astype(F32)).astype(BF16)


def turned(pair):
    rolled = pltpu.roll(pair, 64, 1)
    return jnp.where(lanes_of(pair.shape) < 64, rolled, -rolled)


def unpack(unit):
    lane, row = lanes_of(unit.shape), rows_of(unit.shape)
    left = lane < 64
    column = jnp.where(left, lane, lane - 64)
    flipped = jnp.concatenate([unit, unit], axis=0).T
    rolled = pltpu.roll(unit, 64, 1)
    tops = []
    for h in range(2):
        here = jnp.where(left, unit, rolled) if h == 0 else jnp.where(left, rolled, unit)
        there = flipped[64 * h : 64 * h + 64]
        real = jnp.where(row <= column, here, there)
        imag = jnp.where(row > column, here, jnp.where(row < column, -there, 0.0))
        tops.append(jnp.where(left, real, imag))
    return tops


def pack(first, second):
    lane, row = lanes_of(first.shape), rows_of(first.shape)
    left = lane < 64
    real = jnp.where(left, first, second)
    imag = pltpu.roll(jnp.where(left, second, first), 64, 1)
    return jnp.where(row <= jnp.where(left, lane, lane - 64), real, imag)


def nt_dot(a, b):
    return lax.dot_general(a, b, (((1,), (1,)), ((), ())), preferred_element_type=F32)


def parts_of(table, a, b, swapped=False):
    order = (1, 0) if swapped else (0, 1)
    return jnp.concatenate([table[k, half] for half in order for k in (a, b)], axis=0)


def gram_top(tables, a, b, swapped):
    high = parts_of(tables[0], a, b, swapped)
    low = parts_of(tables[1], a, b, swapped)
    pair = slice(64, 128) if swapped else slice(0, 64)
    lhs = jnp.concatenate([high[pair], low[pair]], axis=1)
    rhs = jnp.concatenate([high, high], axis=1)
    return nt_dot(lhs, rhs) + nt_dot(high[pair], low)


def cross_top(tables, left, right):
    lhigh = jnp.concatenate([tables[0][k, 0] for k in left], axis=0)
    llow = jnp.concatenate([tables[1][k, 0] for k in left], axis=0)
    high, low = parts_of(tables[0], *right), parts_of(tables[1], *right)
    lhs = jnp.concatenate([lhigh, llow], axis=1)
    rhs = jnp.concatenate([high, high], axis=1)
    return nt_dot(lhs, rhs) + nt_dot(lhigh, low)


def applied(top, tables, a, b):
    high, low = parts_of(tables[0], a, b), parts_of(tables[1], a, b)
    whigh, wlow = split(top)
    lhs = jnp.concatenate([whigh, wlow], axis=1)
    rhs = jnp.concatenate([high, high], axis=0)
    return jnp.dot(lhs, rhs, preferred_element_type=F32) + jnp.dot(
        whigh, low, preferred_element_type=F32
    )


def keep(tables, first, count, value):
    for index, whole in enumerate((value, turned(value))):
        for table, part in zip(tables, split(whole)):
            table[pl.ds(first, count), index] = part.reshape(count, BLOCK, 128)


def full(top):
    rolled = pltpu.roll(top, 64, 1)
    return jnp.concatenate([top, jnp.where(lanes_of(top.shape) < 64, -rolled, rolled)], axis=0)


def split3(value):
    first, second = split(value)
    rest = value - first.astype(F32) - second.astype(F32)
    return first, second, rest.astype(BF16)


def fdot(a, b):
    a1, a2, a3 = split3(a)
    b1, b2, b3 = split3(b)
    wide = jnp.concatenate([b1, b2], axis=1)
    main = jnp.dot(
        jnp.concatenate([a1, a2], axis=1),
        jnp.concatenate([wide, wide], axis=0),
        preferred_element_type=F32,
    )
    rest = jnp.dot(
        jnp.concatenate([a1, a3], axis=1),
        jnp.concatenate([b3, b1], axis=0),
        preferred_element_type=F32,
    )
    return main[:, :128] + (main[:, 128:] + rest)


def inverse_roots(tops):
    shape = tops[0].shape
    eye = jnp.where(lanes_of(shape) == rows_of(shape), 1.0, 0.0).astype(F32)
    scales = [jnp.sqrt(2.0 * jnp.sum(t * t, axis=(0, 1), keepdims=True)) for t in tops]
    upper = [t / s for t, s in zip(tops, scales)]
    lower = [1.5 * eye - 0.5 * u for u in upper]
    upper = [fdot(u, full(m)) for u, m in zip(upper, lower)]

    def step(_, carry):
        up, low = carry
        middle = [1.5 * eye - 0.5 * fdot(z, full(y)) for y, z in zip(up, low)]
        return (
            [fdot(y, full(m)) for y, m in zip(up, middle)],
            [fdot(m, full(z)) for z, m in zip(low, middle)],
        )

    upper, lower = lax.fori_loop(0, NS_STEPS - 2, step, (upper, lower))
    middle = [1.5 * eye - 0.5 * fdot(z, full(y)) for y, z in zip(upper, lower)]
    lower = [fdot(m, full(z)) for z, m in zip(lower, middle)]
    return [z * jnp.sqrt(ROWS / s) for z, s in zip(lower, scales)]


def triple(left, middle, right):
    return fdot(fdot(left, full(middle)), full(right))


def sided(value, side, wanted, axis, back):
    moved = pltpu.roll(value, back, axis)
    return jnp.where(jnp.full(value.shape, side, jnp.int32) == wanted, value, moved)


def next_gram(cross, gram_u, gram_v, side_u, side_v):
    shape = cross.shape
    lane, row = lanes_of(shape), rows_of(shape)
    upper = sided(sided(cross, side_u, 0, 0, 32), side_v, 1, 1, 32)
    corner_u = sided(sided(gram_u, side_u, 0, 0, 32), side_u, 0, 1, 96)
    corner_v = sided(sided(gram_v, side_v, 1, 0, 32), side_v, 1, 1, 32)
    flipped = jnp.concatenate([upper, upper], axis=0).T
    lower = jnp.where(lane < 64, flipped[:64], -flipped[64:])
    early = lax.rem(lane, 64) < 32
    return jnp.where(
        row < 32, jnp.where(early, corner_u, upper), jnp.where(early, lower, corner_v)
    )


def order_in(i):
    return lax.rem(2 + 3 * i + 3 * (i * (i - 1) // 2), 4)


def order_out(i):
    return lax.rem(3 * i + 3 * (i * (i - 1) // 2), 4)


def fused_kernel(
    assign, pairing, x_in, out, x_held, results, high0, low0, high1, low1, packed, from_core, relay,
    inbox, second_in, total, slices_0, from_z_0, mine_z_0, gathered_0, slices_1, from_z_1, mine_z_1,
    gathered_1, weights, near, roots_near, grams_near,
    near_in, x_sem, out_sem,
    core_send, core_recv, relay_send, relay_recv, inbox_send, inbox_recv, second_send, second_recv, zr_send,
    zr_recv, zg_send, zg_recv, wfull_send, wfull_recv, whalf_send, whalf_recv, wsecond_send,
    wsecond_recv, wcore_send, wcore_recv, near_send, near_recv,
):
    blk, row = lax.axis_index("blk"), lax.axis_index("row")
    y_lo, z, x = blk // (NZ * NX), lax.rem(blk // NX, NZ), lax.rem(blk, NX)
    y_hi, core = row // 2, lax.rem(row, 2)
    y = y_hi * 2 + y_lo
    half = UNITS // 2
    p, q = x + core * (y - x), y + core * (x - y)

    def device(yy, zz, xx, cc):
        return (lax.rem(yy, 2) * (NZ * NX) + zz * NX + xx, (yy // 2) * 2 + cc)

    def placed(pp, qq):
        return device(qq + core * (pp - qq), z, pp + core * (qq - pp), core)

    def beside(direction):
        return placed(lax.rem(p + 1 + 2 * direction, 4), q)

    def across(distance):
        return placed(p, lax.rem(q + distance, 4))

    partner = device(y, z, x, 1 - core)

    def owner(move):
        chunk = lax.rem(core * NXY + p * 4 + q + move, 2 * NXY)
        cc, pp, qq = chunk // NXY, lax.rem(chunk // 4, 4), lax.rem(chunk, 4)
        return device(qq + cc * (pp - qq), z, pp + cc * (qq - pp), cc)

    def ring_device(step):
        return device(y, lax.rem(z + step, NZ), x, core)

    def my_chunk(da, db):
        return (lax.rem(p + da, 4) * 4 + lax.rem(q + db, 4)) * CHUNK

    def other_chunk(da, db):
        return (lax.rem(q + da, 4) * 4 + lax.rem(p + db, 4)) * CHUNK

    def each(first, last, body):
        def run(step, carry):
            body(step)
            return carry

        lax.fori_loop(first, last, run, 0)

    def remote(src, dst, send, recv, to):
        return pltpu.make_async_remote_copy(
            src_ref=src, dst_ref=dst, send_sem=send, recv_sem=recv, device_id=to, device_id_type=MESH
        )

    barrier = pltpu.get_barrier_semaphore()

    def greet(to):
        pl.semaphore_signal(barrier, inc=1, device_id=to, device_id_type=MESH)

    greet(partner)
    for direction in range(2):
        greet(beside(direction))
    for distance in range(1, 4):
        greet(across(distance))
    for step in range(1, NZ):
        greet(ring_device(step))
    greet(owner(1))
    greet(owner(2 * NXY - 1))

    def x_copy(group):
        return pltpu.make_async_copy(
            x_in.at[:, pl.ds(group * 2 * STEP, 2 * STEP)], x_held.at[group], x_sem.at[group]
        )

    def load_group(group):
        x_copy(group).wait()
        flat = x_held.at[group].reshape(64 * 2 * STEP, 128)
        for k in range(STEP):
            real = flat[pl.ds(2 * k, 64, stride=2 * STEP), :]
            imag = flat[pl.ds(2 * k + 1, 64, stride=2 * STEP), :]
            flipped = jnp.concatenate([real, imag], axis=0).T
            keep((high0, low0), 4 * (group * STEP + k), 4, flipped)

    each(0, GROUPS, lambda group: x_copy(group).start())
    each(0, GROUPS, load_group)
    pl.semaphore_wait(barrier, 8 + NZ - 1)

    slices, from_z = (slices_0, slices_1), (from_z_0, from_z_1)
    mine_z, gathered = (mine_z_0, mine_z_1), (gathered_0, gathered_1)

    def reduced():
        source = (high0, low0)

        def core_copy(step):
            place = other_chunk(order_in(step // 4), order_in(lax.rem(step, 4)))
            return remote(
                packed.at[pl.ds((1 - core) * half + place, CHUNK)],
                from_core.at[pl.ds(place, CHUNK)],
                core_send.at[step], core_recv.at[step], partner,
            )

        def relay_copy(direction, slot, place):
            return remote(
                from_core.at[place + direction], relay.at[direction, slot],
                relay_send.at[direction, slot], relay_recv.at[direction, slot],
                beside(direction),
            )

        def inbox_copy(direction, slot, place):
            return remote(
                from_core.at[pl.ds(place, CHUNK)], inbox.at[direction, slot],
                inbox_send.at[direction, slot], inbox_recv.at[direction, slot],
                beside(direction),
            )

        def second_copy(ib, place):
            return remote(
                from_core.at[pl.ds(place, CHUNK)], second_in.at[ib],
                second_send.at[ib], second_recv.at[ib], across(order_in(ib)),
            )

        def gram_units(first):
            for u in range(CHUNK):
                d = first + u
                tops = []
                for h in range(2):
                    a, b = pair_places(assign, pairing, 0, d, h)
                    tops.append(gram_top(source, a, b, h == 1))
                    slots = slot_at(pairing[1, d], h)
                    around = [
                        pair_around(assign, pairing, *home_of(pairing, d, slot)) for slot in slots
                    ]
                    packed[d, pl.ds(64 + 64 * h, 64)] = cross_top(source, *around)
                packed[d, pl.ds(0, 64)] = pack(*tops)

        def compute(step):
            da, db = order_in(step // 4), order_in(lax.rem(step, 4))
            gram_units((1 - core) * half + other_chunk(da, db))
            core_copy(step).start()
            gram_units(core * half + my_chunk(da, db))

        def inbox_sum(slot):
            for direction in range(2):
                inbox_copy(direction, slot, 0).wait_recv()
            return inbox[0, slot] + inbox[1, slot]

        def ship(step):
            ia, ib = step // 4, lax.rem(step, 4)
            place = my_chunk(order_in(ia), order_in(ib))
            chunk = pl.ds(place, CHUNK)
            core_copy(step).wait_recv()
            from_core[chunk] += packed[pl.ds(core * half + place, CHUNK)]

            @pl.when(ia == 0)
            def _():
                for direction in range(2):
                    relay_copy(direction, ib, place).start()

            for direction in range(2):

                @pl.when(ia == 1 + direction)
                def _(direction=direction):
                    relay_copy(direction, ib, place).wait_recv()
                    from_core[place + direction] += relay[direction, ib]
                    inbox_copy(direction, ib, place).start()

            @pl.when(ia == 3)
            def _():
                from_core[chunk] += inbox_sum(ib)
                second_copy(ib, place).start()

        def advance(step):
            compute(step)
            ship(step - 1)

        compute(0)
        each(1, 16, advance)
        core_copy(15).wait_recv()
        place = my_chunk(0, 0)
        total[...] = (
            from_core[pl.ds(place, CHUNK)]
            + packed[pl.ds(core * half + place, CHUNK)]
            + inbox_sum(3)
        )
        for ib in range(3):
            second_copy(ib, 0).wait_recv()
            total[...] += second_in[ib]

        for part, size in enumerate(SLICES):
            for k in range(NZ):
                begin = 64 * part + k * size
                slices[part][k] = total[:, begin : begin + size, :]

        def zr_copy(part, step):
            return remote(
                slices[part].at[lax.rem(z + step, NZ)], from_z[part].at[step],
                zr_send.at[part, step], zr_recv.at[part, step], ring_device(step),
            )

        def zg_copy(part, step):
            return remote(
                mine_z[part], gathered[part].at[z], zg_send.at[part, step], zg_recv.at[part, step],
                ring_device(step),
            )

        far_first = (4, 3, 5, 2, 6, 1, 7)
        for part in range(2):
            for step in far_first:
                zr_copy(part, step).start()
        for part in range(2):
            acc = slices[part][z]
            for step in reversed(far_first):
                zr_copy(part, step).wait_recv()
                acc = acc + from_z[part][step]
            mine_z[part][...] = acc
            for step in far_first:
                zg_copy(part, step).start()
            gathered[part][z] = acc

        def units_of(part):
            for step in reversed(far_first):
                zg_copy(part, step).wait_recv()
            return [gathered[part][:, u].reshape(NZ * SLICES[part], 128) for u in range(CHUNK)]

        def drain_core(step):
            core_copy(step).wait_send()

        def drain_plane(slot):
            for direction in range(2):
                relay_copy(direction, slot, 0).wait_send()
                inbox_copy(direction, slot, 0).wait_send()

        def drain_second(ib):
            second_copy(ib, 0).wait_send()

        def drain_z(step):
            for part in range(2):
                zr_copy(part, step).wait_send()
                zg_copy(part, step).wait_send()

        def drain():
            each(0, 16, drain_core)
            each(0, 4, drain_plane)
            each(0, 3, drain_second)
            each(1, NZ, drain_z)

        return units_of, drain

    def handing(rnd, source):
        mine = core * half + my_chunk(0, 0)

        def wfull_copy(direction, slot, first):
            part = weights.at[rnd, pl.ds(first, CHUNK)]
            return remote(
                part, part, wfull_send.at[rnd, direction, slot], wfull_recv.at[rnd, direction, slot],
                beside(direction),
            )

        def whalf_copy(direction, slot, first):
            part = weights.at[rnd, first + direction]
            return remote(
                part, part, whalf_send.at[rnd, direction, slot], whalf_recv.at[rnd, direction, slot],
                beside(direction),
            )

        def wsecond_copy(ib, first):
            part = weights.at[rnd, pl.ds(first, CHUNK)]
            return remote(
                part, part, wsecond_send.at[rnd, ib], wsecond_recv.at[rnd, ib],
                across(4 - order_out(ib)),
            )

        def my_units(step):
            return core * half + my_chunk(order_out(step // 4), order_out(lax.rem(step, 4)))

        def other_units(step):
            return (1 - core) * half + other_chunk(order_out(step // 4), order_out(lax.rem(step, 4)))

        def wcore_copy(step):
            part = weights.at[rnd, pl.ds(my_units(step), CHUNK)]
            return remote(
                part, part, wcore_send.at[rnd, step], wcore_recv.at[rnd, step], partner
            )

        def out_copy(first, which):
            place = pl.ds(SLOTS * first, SLOTS * CHUNK)
            return pltpu.make_async_copy(results.at[place], out.at[place], out_sem.at[which])

        def apply_units(first, which):
            for u in range(CHUNK):
                d = first + u
                tops = unpack(weights[rnd, d])
                for h in range(2):
                    a, b = pair_places(assign, pairing, rnd, d, h)
                    new = applied(tops[h], source, a, b)
                    place = SLOTS * d + 2 * h
                    if rnd == 0:
                        keep((high1, low1), place, 2, new)
                    else:
                        results[pl.ds(place, 2)] = new.reshape(2, BLOCK, 128)
            if rnd == 1:
                out_copy(first, which).start()

        def forward(step):
            ia, ib = step // 4, lax.rem(step, 4)
            first = my_units(step)

            @pl.when(ia == 0)
            def _():
                wsecond_copy(ib, first).wait_recv()
                for direction in range(2):
                    wfull_copy(direction, ib, first).start()

            @pl.when(ia == 1)
            def _():
                for direction in range(2):
                    whole = my_units(step + 4 * direction)
                    wfull_copy(direction, ib, whole).wait_recv()
                    whalf_copy(direction, ib, whole).start()

            @pl.when(ia == 3)
            def _():
                for direction in range(2):
                    whalf_copy(direction, ib, first).wait_recv()

            wcore_copy(step).start()

        def use(step):
            apply_units(my_units(step), step)

        def use_other(step):
            wcore_copy(step).wait_recv()
            apply_units(other_units(step), 16 + step)

        def begin():
            for ib in (3, 2, 1):
                wsecond_copy(ib, mine).start()
            for direction in range(2):
                wfull_copy(direction, 0, mine).start()
            wcore_copy(0).start()

        def drain_core(step):
            wcore_copy(step).wait_send()
            if rnd == 1:
                out_copy(0, step).wait()
                out_copy(0, 16 + step).wait()

        def drain_plane(slot):
            for direction in range(2):
                wfull_copy(direction, slot, 0).wait_send()
                whalf_copy(direction, slot, 0).wait_send()

        def drain():
            each(0, 16, drain_core)
            each(0, 4, drain_plane)
            each(1, 4, lambda ib: wsecond_copy(ib, 0).wait_send())

        return begin, forward, use, use_other, drain

    units_of, drain_reduced = reduced()
    begin0, forward0, use0, use_other0, drain0 = handing(0, (high0, low0))
    begin1, forward1, use1, use_other1, drain1 = handing(1, (high1, low1))
    mine = core * half + my_chunk(0, 0)

    tops = []
    for unit in units_of(0):
        tops.extend(unpack(unit))
    roots = inverse_roots(tops)

    def packed_pair(values, u):
        return pack(values[2 * u], pltpu.roll(values[2 * u + 1], 64, 1))

    def near_copy(which):
        return remote(
            near.at[1 - which], near_in.at[which], near_send.at[which], near_recv.at[which],
            owner(1 if which == 0 else 2 * NXY - 1),
        )

    inner = [triple(w, g, w) for w, g in zip(roots, tops)]
    for u in range(CHUNK):
        near[u, 0] = packed_pair(roots, u)
        near[u, 1] = packed_pair(inner, u)
    for which in range(2):
        near_copy(which).start()
    for u in range(CHUNK):
        weights[0, mine + u] = near[u, 0]
        for h in range(2):
            roots_near[2 + 2 * u + h] = roots[2 * u + h]
            grams_near[2 + 2 * u + h] = inner[2 * u + h]
    begin0()
    use0(0)

    def take0(step):
        forward0(step)
        use0(step)
        use_other0(step - 1)

    each(1, 4, take0)
    crosses = units_of(1)
    for which in range(2):
        near_copy(which).wait_recv()
        for kind, table in enumerate((roots_near, grams_near)):
            for h, top in enumerate(unpack(near_in[which, kind])):
                table[6 * which + h] = top

    tops = []
    for u in range(CHUNK):
        for h in range(2):
            d = mine + u
            found = []
            for slot in slot_at(pairing[1, d], h):
                _, place = home_of(pairing, d, slot)
                index = 2 * (1 + u + turn_of(slot)) + place // 2
                found.append((index, lax.rem(place, 2)))
            (left, side_u), (right, side_v) = found
            cross = triple(
                roots_near[left], crosses[u][64 * h : 64 * h + 64], roots_near[right]
            )
            tops.append(next_gram(cross, grams_near[left], grams_near[right], side_u, side_v))
    roots = inverse_roots(tops)
    for u in range(CHUNK):
        weights[1, mine + u] = packed_pair(roots, u)
    begin1()
    each(4, 12, take0)
    each(1, 4, forward1)
    each(12, 16, take0)
    use_other0(15)
    use1(0)

    def take1(step):
        use1(step)
        use_other1(step - 1)

    def forward_and_take1(step):
        forward1(step)
        take1(step)

    each(1, 4, take1)
    each(4, 8, forward1)
    each(4, 8, take1)
    each(8, 16, forward_and_take1)
    use_other1(15)
    drain_reduced()
    drain0()
    drain1()
    for which in range(2):
        near_copy(which).wait_send()


def last_kernel(assign, pairing, source, out, places):
    @pl.when(pl.program_id(0) == 0)
    def _():
        def unit(d, carry):
            up = jnp.where(d == UNITS - 1, 0, d + 1)
            down = jnp.where(d == 0, UNITS - 1, d - 1)
            here, above, below = pairing[1, d], pairing[1, up], pairing[1, down]
            places[assign[SLOTS * d]] = SLOTS * d
            places[assign[SLOTS * d + 1]] = SLOTS * up + jnp.where(above == 0, 1, 2)
            places[assign[SLOTS * d + 2]] = SLOTS * down + jnp.where(
                below == 0, 2, jnp.where(below == 1, 1, 3)
            )
            places[assign[SLOTS * d + 3]] = SLOTS * d + jnp.where(here == 2, 1, 3)
            return carry

        lax.fori_loop(0, UNITS, unit, 0, unroll=4)

    flat = out.reshape(64 * 2 * STEP, 128)
    for k in range(STEP):
        ct = pl.program_id(0) * STEP + k
        parts = [source[places[4 * ct + j]] for j in range(4)]
        flipped = jnp.concatenate(parts, axis=0).T
        flat[pl.ds(2 * k, 64, stride=2 * STEP), :] = flipped[:64]
        flat[pl.ds(2 * k + 1, 64, stride=2 * STEP), :] = flipped[64:]


SMEM = pl.BlockSpec(memory_space=pltpu.SMEM)
VMEM = pl.BlockSpec(memory_space=pltpu.VMEM)
TABLE = (BLOCKS, BLOCK, 128)


def rounds(assignment, pairing, x):
    dma = pltpu.SemaphoreType.DMA
    chunks, plane, second, ring = dma((2, 16)), dma((2, 2, 4)), dma((2, 4)), dma((2, NZ))
    part = pltpu.VMEM((BLOCKS, 2, BLOCK, 128), BF16)
    return pl.pallas_call(
        fused_kernel,
        out_shape=jax.ShapeDtypeStruct(TABLE, F32),
        in_specs=[SMEM, SMEM, pl.BlockSpec(memory_space=pl.ANY)],
        out_specs=pl.BlockSpec(memory_space=pl.ANY),
        scratch_shapes=[
            pltpu.VMEM((GROUPS, 64, 2 * STEP, 128), F32),
            pltpu.VMEM(TABLE, F32),
            part, part, part, part,
            pltpu.VMEM((UNITS, DEPTH, 128), F32),
            pltpu.VMEM((UNITS // 2, DEPTH, 128), F32),
            pltpu.VMEM((2, 4, DEPTH, 128), F32),
            pltpu.VMEM((2, 4, CHUNK, DEPTH, 128), F32),
            pltpu.VMEM((3, CHUNK, DEPTH, 128), F32),
            pltpu.VMEM((CHUNK, DEPTH, 128), F32),
            pltpu.VMEM((NZ, CHUNK, SLICES[0], 128), F32),
            pltpu.VMEM((NZ, CHUNK, SLICES[0], 128), F32),
            pltpu.VMEM((CHUNK, SLICES[0], 128), F32),
            pltpu.VMEM((NZ, CHUNK, SLICES[0], 128), F32),
            pltpu.VMEM((NZ, CHUNK, SLICES[1], 128), F32),
            pltpu.VMEM((NZ, CHUNK, SLICES[1], 128), F32),
            pltpu.VMEM((CHUNK, SLICES[1], 128), F32),
            pltpu.VMEM((NZ, CHUNK, SLICES[1], 128), F32),
            pltpu.VMEM((2, UNITS, 64, 128), F32),
            pltpu.VMEM((2, 2, 64, 128), F32),
            pltpu.VMEM((8, 64, 128), F32),
            pltpu.VMEM((8, 64, 128), F32),
            pltpu.VMEM((2, 2, 64, 128), F32),
            dma((GROUPS,)), dma((32,)),
            dma((16,)), dma((16,)), dma((2, 4)), dma((2, 4)), dma((2, 4)), dma((2, 4)),
            dma((4,)), dma((4,)), ring, ring, ring, ring,
            plane, plane, plane, plane, second, second, chunks, chunks, dma((2,)), dma((2,)),
        ],
        compiler_params=PARAMS(collective_id=0, has_side_effects=True),
        name="rounds",
    )(assignment, pairing, x)


def unturned(assignment, pairing, source):
    shape = (64, BLOCKS // 2, 128)
    return pl.pallas_call(
        last_kernel,
        out_shape=jax.ShapeDtypeStruct(shape, F32),
        grid=(BLOCKS // 4 // STEP,),
        in_specs=[SMEM, SMEM, VMEM],
        out_specs=pl.BlockSpec((64, 2 * STEP, 128), lambda i: (0, i, 0)),
        scratch_shapes=[pltpu.SMEM((BLOCKS,), jnp.int32)],
        compiler_params=PARAMS(),
        name="unturn",
    )(assignment, pairing, source)


def on_device(transmission, assignment, pairing):
    rows, _, cols = transmission.shape
    x = transmission.reshape(rows, 2, cols // 128, 128).transpose(0, 2, 1, 3).reshape(rows, -1, 128)
    turned_blocks = rounds(assignment, pairing, x)
    out = unturned(assignment, pairing, turned_blocks)
    out = out.reshape(rows, cols // 128, 2, 128).transpose(0, 2, 1, 3)
    return out.reshape(rows, 2, cols)


def solution(mesh):
    placed = (P(("blk", "row"), None, None), P(), P())
    return jax.shard_map(
        on_device,
        mesh=mesh,
        in_specs=placed,
        out_specs=P(("blk", "row"), None, None),
        check_vma=False,
    )
```

```python
import functools

import jax
import jax.numpy as jnp
from jax import lax
from jax.experimental import pallas as pl
from jax.experimental.pallas import tpu as pltpu
from jax.sharding import PartitionSpec as P

ROWS = 16384
BLOCK = 32
SLOTS = 4
NS_STEPS = 6
UNITS = 64
BLOCKS = 256
MESH = pl.DeviceIdType.MESH
F32 = jnp.float32
BF16 = jnp.bfloat16
NX, NY, NZ = 4, 4, 8
NXY = NX * NY
CHUNK = UNITS // 2 // NXY
DEPTHS = (64, 128)
SLICES = (64 // NZ, 128 // NZ)
STEP = 8
GROUPS = BLOCKS // 4 // STEP
PARAMS = functools.partial(pltpu.CompilerParams, vmem_limit_bytes=60 * 1024 * 1024)


def position(pick, slot):
    if_two = jnp.where(slot == 0, 0, jnp.where(slot == 3, 1, slot + 1))
    if_one = jnp.where(slot == 1, 2, jnp.where(slot == 2, 1, slot))
    return jnp.where(pick == 0, slot, jnp.where(pick == 1, if_one, if_two))


def slot_at(pick, h):
    if h == 0:
        return 0, 1 + pick
    return jnp.where(pick == 0, 2, 1), jnp.where(pick == 2, 2, 3)


def turn_of(slot):
    return jnp.where(slot == 1, -1, jnp.where(slot == 2, 1, 0))


def home_of(pairing, d, slot):
    home = lax.rem(d + turn_of(slot) + UNITS, UNITS)
    return home, position(pairing[0, home], slot)


def pair_places(assign, pairing, rnd, d, h):
    slots = slot_at(pairing[rnd, d], h)
    if rnd == 0:
        return [assign[d * SLOTS + slot] for slot in slots]
    places = []
    for slot in slots:
        home, place = home_of(pairing, d, slot)
        places.append(home * SLOTS + place)
    return places


def pair_around(assign, pairing, home, place):
    pick = pairing[0, home]
    in_first = place < 2
    first = jnp.where(in_first, 0, jnp.where(pick == 0, 2, 1))
    second = jnp.where(in_first, 1 + pick, jnp.where(pick == 2, 2, 3))
    return assign[home * SLOTS + first], assign[home * SLOTS + second]


def lanes_of(shape):
    return lax.broadcasted_iota(jnp.int32, shape, 1)


def rows_of(shape):
    return lax.broadcasted_iota(jnp.int32, shape, 0)


def split(value):
    high = value.astype(BF16)
    return high, (value - high.astype(F32)).astype(BF16)


def turned(pair):
    rolled = pltpu.roll(pair, 64, 1)
    return jnp.where(lanes_of(pair.shape) < 64, rolled, -rolled)


def unpack(unit):
    lane, row = lanes_of(unit.shape), rows_of(unit.shape)
    left = lane < 64
    column = jnp.where(left, lane, lane - 64)
    flipped = jnp.concatenate([unit, unit], axis=0).T
    rolled = pltpu.roll(unit, 64, 1)
    tops = []
    for h in range(2):
        here = jnp.where(left, unit, rolled) if h == 0 else jnp.where(left, rolled, unit)
        there = flipped[64 * h : 64 * h + 64]
        real = jnp.where(row <= column, here, there)
        imag = jnp.where(row > column, here, jnp.where(row < column, -there, 0.0))
        tops.append(jnp.where(left, real, imag))
    return tops


def pack(first, second):
    lane, row = lanes_of(first.shape), rows_of(first.shape)
    left = lane < 64
    real = jnp.where(left, first, second)
    imag = pltpu.roll(jnp.where(left, second, first), 64, 1)
    return jnp.where(row <= jnp.where(left, lane, lane - 64), real, imag)


def nt_dot(a, b):
    return lax.dot_general(a, b, (((1,), (1,)), ((), ())), preferred_element_type=F32)


def parts_of(table, a, b, swapped=False):
    order = (1, 0) if swapped else (0, 1)
    return jnp.concatenate([table[k, half] for half in order for k in (a, b)], axis=0)


def gram_top(tables, a, b, swapped):
    high = parts_of(tables[0], a, b, swapped)
    low = parts_of(tables[1], a, b, swapped)
    pair = slice(64, 128) if swapped else slice(0, 64)
    lhs = jnp.concatenate([high[pair], low[pair]], axis=1)
    rhs = jnp.concatenate([high, high], axis=1)
    return nt_dot(lhs, rhs) + nt_dot(high[pair], low)


def cross_top(tables, left, right):
    lhigh = jnp.concatenate([tables[0][k, 0] for k in left], axis=0)
    llow = jnp.concatenate([tables[1][k, 0] for k in left], axis=0)
    high, low = parts_of(tables[0], *right), parts_of(tables[1], *right)
    lhs = jnp.concatenate([lhigh, llow], axis=1)
    rhs = jnp.concatenate([high, high], axis=1)
    return nt_dot(lhs, rhs) + nt_dot(lhigh, low)


def applied(top, tables, a, b):
    high, low = parts_of(tables[0], a, b), parts_of(tables[1], a, b)
    whigh, wlow = split(top)
    lhs = jnp.concatenate([whigh, wlow], axis=1)
    rhs = jnp.concatenate([high, high], axis=0)
    return jnp.dot(lhs, rhs, preferred_element_type=F32) + jnp.dot(
        whigh, low, preferred_element_type=F32
    )


def keep(tables, first, count, value):
    for index, whole in enumerate((value, turned(value))):
        for table, part in zip(tables, split(whole)):
            table[pl.ds(first, count), index] = part.reshape(count, BLOCK, 128)


def full(top):
    rolled = pltpu.roll(top, 64, 1)
    return jnp.concatenate([top, jnp.where(lanes_of(top.shape) < 64, -rolled, rolled)], axis=0)


def split3(value):
    first, second = split(value)
    rest = value - first.astype(F32) - second.astype(F32)
    return first, second, rest.astype(BF16)


def fdot(a, b):
    a1, a2, a3 = split3(a)
    b1, b2, b3 = split3(b)
    wide = jnp.concatenate([b1, b2], axis=1)
    main = jnp.dot(
        jnp.concatenate([a1, a2], axis=1),
        jnp.concatenate([wide, wide], axis=0),
        preferred_element_type=F32,
    )
    rest = jnp.dot(
        jnp.concatenate([a1, a3], axis=1),
        jnp.concatenate([b3, b1], axis=0),
        preferred_element_type=F32,
    )
    return main[:, :128] + (main[:, 128:] + rest)


def inverse_roots(tops):
    shape = tops[0].shape
    eye = jnp.where(lanes_of(shape) == rows_of(shape), 1.0, 0.0).astype(F32)
    scales = [jnp.sqrt(2.0 * jnp.sum(t * t, axis=(0, 1), keepdims=True)) for t in tops]
    upper = [t / s for t, s in zip(tops, scales)]
    lower = [1.5 * eye - 0.5 * u for u in upper]
    upper = [fdot(u, full(m)) for u, m in zip(upper, lower)]

    def step(_, carry):
        up, low = carry
        middle = [1.5 * eye - 0.5 * fdot(z, full(y)) for y, z in zip(up, low)]
        return (
            [fdot(y, full(m)) for y, m in zip(up, middle)],
            [fdot(m, full(z)) for z, m in zip(low, middle)],
        )

    upper, lower = lax.fori_loop(0, NS_STEPS - 2, step, (upper, lower))
    middle = [1.5 * eye - 0.5 * fdot(z, full(y)) for y, z in zip(upper, lower)]
    lower = [fdot(m, full(z)) for z, m in zip(lower, middle)]
    return [z * jnp.sqrt(ROWS / s) for z, s in zip(lower, scales)]


def triple(left, middle, right):
    return fdot(fdot(left, full(middle)), full(right))


def sided(value, side, wanted, axis, back):
    moved = pltpu.roll(value, back, axis)
    return jnp.where(jnp.full(value.shape, side, jnp.int32) == wanted, value, moved)


def next_gram(cross, gram_u, gram_v, side_u, side_v):
    shape = cross.shape
    lane, row = lanes_of(shape), rows_of(shape)
    upper = sided(sided(cross, side_u, 0, 0, 32), side_v, 1, 1, 32)
    corner_u = sided(sided(gram_u, side_u, 0, 0, 32), side_u, 0, 1, 96)
    corner_v = sided(sided(gram_v, side_v, 1, 0, 32), side_v, 1, 1, 32)
    flipped = jnp.concatenate([upper, upper], axis=0).T
    lower = jnp.where(lane < 64, flipped[:64], -flipped[64:])
    early = lax.rem(lane, 64) < 32
    return jnp.where(
        row < 32, jnp.where(early, corner_u, upper), jnp.where(early, lower, corner_v)
    )


def order_in(i):
    return lax.rem(2 + 3 * i + 3 * (i * (i - 1) // 2), 4)


def order_out(i):
    return lax.rem(3 * i + 3 * (i * (i - 1) // 2), 4)


def fused_kernel(
    assign, pairing, x_in, out, x_held, results, high0, low0, high1, low1,
    packed_0, from_core_0, relay_0, inbox_0, second_in_0, total_0, slices_0, from_z_0, mine_z_0, gathered_0,
    packed_1, from_core_1, relay_1, inbox_1, second_in_1, total_1, slices_1, from_z_1, mine_z_1, gathered_1,
    weights, near, roots_near, grams_near,
    near_in, x_sem, out_sem,
    core_send, core_recv, relay_send, relay_recv, inbox_send, inbox_recv, second_send, second_recv, zr_send,
    zr_recv, zg_send, zg_recv, wfull_send, wfull_recv, whalf_send, whalf_recv, wsecond_send,
    wsecond_recv, wcore_send, wcore_recv, near_send, near_recv,
):
    blk, row = lax.axis_index("blk"), lax.axis_index("row")
    y_lo, z, x = blk // (NZ * NX), lax.rem(blk // NX, NZ), lax.rem(blk, NX)
    y_hi, core = row // 2, lax.rem(row, 2)
    y = y_hi * 2 + y_lo
    half = UNITS // 2
    p, q = x + core * (y - x), y + core * (x - y)

    def device(yy, zz, xx, cc):
        return (lax.rem(yy, 2) * (NZ * NX) + zz * NX + xx, (yy // 2) * 2 + cc)

    def placed(pp, qq):
        return device(qq + core * (pp - qq), z, pp + core * (qq - pp), core)

    def beside(direction):
        return placed(lax.rem(p + 1 + 2 * direction, 4), q)

    def across(distance):
        return placed(p, lax.rem(q + distance, 4))

    partner = device(y, z, x, 1 - core)

    def owner(move):
        chunk = lax.rem(core * NXY + p * 4 + q + move, 2 * NXY)
        cc, pp, qq = chunk // NXY, lax.rem(chunk // 4, 4), lax.rem(chunk, 4)
        return device(qq + cc * (pp - qq), z, pp + cc * (qq - pp), cc)

    def ring_device(step):
        return device(y, lax.rem(z + step, NZ), x, core)

    def my_chunk(da, db):
        return (lax.rem(p + da, 4) * 4 + lax.rem(q + db, 4)) * CHUNK

    def other_chunk(da, db):
        return (lax.rem(q + da, 4) * 4 + lax.rem(p + db, 4)) * CHUNK

    def each(first, last, body):
        def run(step, carry):
            body(step)
            return carry

        lax.fori_loop(first, last, run, 0)

    def remote(src, dst, send, recv, to):
        return pltpu.make_async_remote_copy(
            src_ref=src, dst_ref=dst, send_sem=send, recv_sem=recv, device_id=to, device_id_type=MESH
        )

    barrier = pltpu.get_barrier_semaphore()

    def greet(to):
        pl.semaphore_signal(barrier, inc=1, device_id=to, device_id_type=MESH)

    greet(partner)
    for direction in range(2):
        greet(beside(direction))
    for distance in range(1, 4):
        greet(across(distance))
    for step in range(1, NZ):
        greet(ring_device(step))
    greet(owner(1))
    greet(owner(2 * NXY - 1))

    def x_copy(group):
        return pltpu.make_async_copy(
            x_in.at[:, pl.ds(group * 2 * STEP, 2 * STEP)], x_held.at[group], x_sem.at[group]
        )

    def load_group(group):
        x_copy(group).wait()
        flat = x_held.at[group].reshape(64 * 2 * STEP, 128)
        for k in range(STEP):
            real = flat[pl.ds(2 * k, 64, stride=2 * STEP), :]
            imag = flat[pl.ds(2 * k + 1, 64, stride=2 * STEP), :]
            flipped = jnp.concatenate([real, imag], axis=0).T
            keep((high0, low0), 4 * (group * STEP + k), 4, flipped)

    each(0, GROUPS, lambda group: x_copy(group).start())
    each(0, GROUPS, load_group)
    pl.semaphore_wait(barrier, 8 + NZ - 1)

    packed, from_core = (packed_0, packed_1), (from_core_0, from_core_1)
    relay, inbox = (relay_0, relay_1), (inbox_0, inbox_1)
    second_in, total = (second_in_0, second_in_1), (total_0, total_1)
    slices, from_z = (slices_0, slices_1), (from_z_0, from_z_1)
    mine_z, gathered = (mine_z_0, mine_z_1), (gathered_0, gathered_1)

    def reduction(part):
        source = (high0, low0)

        def core_copy(step):
            place = other_chunk(order_in(step // 4), order_in(lax.rem(step, 4)))
            return remote(
                packed[part].at[pl.ds((1 - core) * half + place, CHUNK)],
                from_core[part].at[pl.ds(place, CHUNK)],
                core_send.at[part, step], core_recv.at[part, step], partner,
            )

        def relay_copy(direction, slot, place):
            return remote(
                from_core[part].at[place + direction], relay[part].at[direction, slot],
                relay_send.at[part, direction, slot], relay_recv.at[part, direction, slot],
                beside(direction),
            )

        def inbox_copy(direction, slot, place):
            return remote(
                from_core[part].at[pl.ds(place, CHUNK)], inbox[part].at[direction, slot],
                inbox_send.at[part, direction, slot], inbox_recv.at[part, direction, slot],
                beside(direction),
            )

        def second_copy(ib, place):
            return remote(
                from_core[part].at[pl.ds(place, CHUNK)], second_in[part].at[ib],
                second_send.at[part, ib], second_recv.at[part, ib], across(order_in(ib)),
            )

        def gram_units(first):
            for u in range(CHUNK):
                d = first + u
                tops = []
                for h in range(2):
                    if part == 0:
                        a, b = pair_places(assign, pairing, 0, d, h)
                        tops.append(gram_top(source, a, b, h == 1))
                        continue
                    around = [
                        pair_around(assign, pairing, *home_of(pairing, d, slot))
                        for slot in slot_at(pairing[1, d], h)
                    ]
                    packed[part][d, pl.ds(64 * h, 64)] = cross_top(source, *around)
                if part == 0:
                    packed[part][d] = pack(*tops)

        def compute(step):
            da, db = order_in(step // 4), order_in(lax.rem(step, 4))
            gram_units((1 - core) * half + other_chunk(da, db))
            core_copy(step).start()
            gram_units(core * half + my_chunk(da, db))

        def inbox_sum(slot):
            for direction in range(2):
                inbox_copy(direction, slot, 0).wait_recv()
            return inbox[part][0, slot] + inbox[part][1, slot]

        def ship(step):
            ia, ib = step // 4, lax.rem(step, 4)
            place = my_chunk(order_in(ia), order_in(ib))
            chunk = pl.ds(place, CHUNK)
            core_copy(step).wait_recv()
            from_core[part][chunk] += packed[part][pl.ds(core * half + place, CHUNK)]

            @pl.when(ia == 0)
            def _():
                for direction in range(2):
                    relay_copy(direction, ib, place).start()

            for direction in range(2):

                @pl.when(ia == 1 + direction)
                def _(direction=direction):
                    relay_copy(direction, ib, place).wait_recv()
                    from_core[part][place + direction] += relay[part][direction, ib]
                    inbox_copy(direction, ib, place).start()

            @pl.when(ia == 3)
            def _():
                from_core[part][chunk] += inbox_sum(ib)
                second_copy(ib, place).start()

        def advance(step):
            compute(step)
            ship(step - 1)

        def close():
            core_copy(15).wait_recv()
            place = my_chunk(0, 0)
            total[part][...] = (
                from_core[part][pl.ds(place, CHUNK)]
                + packed[part][pl.ds(core * half + place, CHUNK)]
                + inbox_sum(3)
            )
            for ib in range(3):
                second_copy(ib, 0).wait_recv()
                total[part][...] += second_in[part][ib]
            size = SLICES[part]
            for k in range(NZ):
                slices[part][k] = total[part][:, k * size : (k + 1) * size, :]
            for step in far_first:
                zr_copy(step).start()

        def zr_copy(step):
            return remote(
                slices[part].at[lax.rem(z + step, NZ)], from_z[part].at[step],
                zr_send.at[part, step], zr_recv.at[part, step], ring_device(step),
            )

        def zg_copy(step):
            return remote(
                mine_z[part], gathered[part].at[z], zg_send.at[part, step], zg_recv.at[part, step],
                ring_device(step),
            )

        far_first = (4, 3, 5, 2, 6, 1, 7)

        def settle():
            acc = slices[part][z]
            for step in reversed(far_first):
                zr_copy(step).wait_recv()
                acc = acc + from_z[part][step]
            mine_z[part][...] = acc
            for step in far_first:
                zg_copy(step).start()
            gathered[part][z] = acc

        def units():
            for step in reversed(far_first):
                zg_copy(step).wait_recv()
            return [gathered[part][:, u].reshape(DEPTHS[part], 128) for u in range(CHUNK)]

        def drain_core(step):
            core_copy(step).wait_send()

        def drain_plane(slot):
            for direction in range(2):
                relay_copy(direction, slot, 0).wait_send()
                inbox_copy(direction, slot, 0).wait_send()

        def drain_second(ib):
            second_copy(ib, 0).wait_send()

        def drain_z(step):
            zr_copy(step).wait_send()
            zg_copy(step).wait_send()

        def drain():
            each(0, 16, drain_core)
            each(0, 4, drain_plane)
            each(0, 3, drain_second)
            each(1, NZ, drain_z)

        return compute, advance, close, settle, units, drain

    def handing(rnd, source):
        mine = core * half + my_chunk(0, 0)

        def wfull_copy(direction, slot, first):
            part = weights.at[rnd, pl.ds(first, CHUNK)]
            return remote(
                part, part, wfull_send.at[rnd, direction, slot], wfull_recv.at[rnd, direction, slot],
                beside(direction),
            )

        def whalf_copy(direction, slot, first):
            part = weights.at[rnd, first + direction]
            return remote(
                part, part, whalf_send.at[rnd, direction, slot], whalf_recv.at[rnd, direction, slot],
                beside(direction),
            )

        def wsecond_copy(ib, first):
            part = weights.at[rnd, pl.ds(first, CHUNK)]
            return remote(
                part, part, wsecond_send.at[rnd, ib], wsecond_recv.at[rnd, ib],
                across(4 - order_out(ib)),
            )

        def my_units(step):
            return core * half + my_chunk(order_out(step // 4), order_out(lax.rem(step, 4)))

        def other_units(step):
            return (1 - core) * half + other_chunk(order_out(step // 4), order_out(lax.rem(step, 4)))

        def wcore_copy(step):
            part = weights.at[rnd, pl.ds(my_units(step), CHUNK)]
            return remote(
                part, part, wcore_send.at[rnd, step], wcore_recv.at[rnd, step], partner
            )

        def out_copy(first, which):
            place = pl.ds(SLOTS * first, SLOTS * CHUNK)
            return pltpu.make_async_copy(results.at[place], out.at[place], out_sem.at[which])

        def apply_units(first, which):
            for u in range(CHUNK):
                d = first + u
                tops = unpack(weights[rnd, d])
                for h in range(2):
                    a, b = pair_places(assign, pairing, rnd, d, h)
                    new = applied(tops[h], source, a, b)
                    place = SLOTS * d + 2 * h
                    if rnd == 0:
                        keep((high1, low1), place, 2, new)
                    else:
                        results[pl.ds(place, 2)] = new.reshape(2, BLOCK, 128)
            if rnd == 1:
                out_copy(first, which).start()

        def forward(step):
            ia, ib = step // 4, lax.rem(step, 4)
            first = my_units(step)

            @pl.when(ia == 0)
            def _():
                wsecond_copy(ib, first).wait_recv()
                for direction in range(2):
                    wfull_copy(direction, ib, first).start()

            @pl.when(ia == 1)
            def _():
                for direction in range(2):
                    whole = my_units(step + 4 * direction)
                    wfull_copy(direction, ib, whole).wait_recv()
                    whalf_copy(direction, ib, whole).start()

            @pl.when(ia == 3)
            def _():
                for direction in range(2):
                    whalf_copy(direction, ib, first).wait_recv()

            wcore_copy(step).start()

        def use(step):
            apply_units(my_units(step), step)

        def use_other(step):
            wcore_copy(step).wait_recv()
            apply_units(other_units(step), 16 + step)

        def begin():
            for ib in (1, 2, 3):
                wsecond_copy(ib, mine).start()
            for direction in range(2):
                wfull_copy(direction, 0, mine).start()
            wcore_copy(0).start()

        def drain_core(step):
            wcore_copy(step).wait_send()
            if rnd == 1:
                out_copy(0, step).wait()
                out_copy(0, 16 + step).wait()

        def drain_plane(slot):
            for direction in range(2):
                wfull_copy(direction, slot, 0).wait_send()
                whalf_copy(direction, slot, 0).wait_send()

        def drain():
            each(0, 16, drain_core)
            each(0, 4, drain_plane)
            each(1, 4, lambda ib: wsecond_copy(ib, 0).wait_send())

        return begin, forward, use, use_other, drain

    compute_g, advance_g, close_g, settle_g, units_g, drain_g = reduction(0)
    compute_c, advance_c, close_c, settle_c, units_c, drain_c = reduction(1)
    compute_g(0)
    each(1, 16, advance_g)
    compute_c(0)
    each(1, 9, advance_c)
    close_g()
    each(9, 16, advance_c)
    settle_g()
    close_c()
    begin0, forward0, use0, use_other0, drain0 = handing(0, (high0, low0))
    begin1, forward1, use1, use_other1, drain1 = handing(1, (high1, low1))
    mine = core * half + my_chunk(0, 0)

    tops = []
    for unit in units_g():
        tops.extend(unpack(unit))
    roots = inverse_roots(tops)

    def packed_pair(values, u):
        return pack(values[2 * u], pltpu.roll(values[2 * u + 1], 64, 1))

    def near_copy(which):
        return remote(
            near.at[1 - which], near_in.at[which], near_send.at[which], near_recv.at[which],
            owner(1 if which == 0 else 2 * NXY - 1),
        )

    inner = [triple(w, g, w) for w, g in zip(roots, tops)]
    for u in range(CHUNK):
        near[u, 0] = packed_pair(roots, u)
        near[u, 1] = packed_pair(inner, u)
    for which in range(2):
        near_copy(which).start()
    for u in range(CHUNK):
        weights[0, mine + u] = near[u, 0]
        for h in range(2):
            roots_near[2 + 2 * u + h] = roots[2 * u + h]
            grams_near[2 + 2 * u + h] = inner[2 * u + h]
    begin0()
    use0(0)

    def take0(step):
        forward0(step)
        use0(step)
        use_other0(step - 1)

    settle_c()
    each(1, 4, take0)
    for which in range(2):
        near_copy(which).wait_recv()
        for kind, table in enumerate((roots_near, grams_near)):
            for h, top in enumerate(unpack(near_in[which, kind])):
                table[6 * which + h] = top
    crosses = units_c()

    tops = []
    for u in range(CHUNK):
        for h in range(2):
            d = mine + u
            found = []
            for slot in slot_at(pairing[1, d], h):
                _, place = home_of(pairing, d, slot)
                index = 2 * (1 + u + turn_of(slot)) + place // 2
                found.append((index, lax.rem(place, 2)))
            (left, side_u), (right, side_v) = found
            cross = triple(
                roots_near[left], crosses[u][64 * h : 64 * h + 64], roots_near[right]
            )
            tops.append(next_gram(cross, grams_near[left], grams_near[right], side_u, side_v))
    each(4, 8, forward0)
    roots = inverse_roots(tops)
    for u in range(CHUNK):
        weights[1, mine + u] = packed_pair(roots, u)
    begin1()

    def late0(step):
        use0(step)
        use_other0(step - 1)

    each(4, 8, late0)
    each(8, 12, take0)
    each(1, 4, forward1)
    each(12, 16, take0)
    use_other0(15)
    use1(0)

    def take1(step):
        use1(step)
        use_other1(step - 1)

    def forward_and_take1(step):
        forward1(step)
        take1(step)

    each(1, 4, take1)
    each(4, 8, forward1)
    each(4, 8, take1)
    each(8, 16, forward_and_take1)
    use_other1(15)
    drain_g()
    drain_c()
    drain0()
    drain1()
    for which in range(2):
        near_copy(which).wait_send()


def last_kernel(assign, pairing, source, out, places):
    @pl.when(pl.program_id(0) == 0)
    def _():
        def unit(d, carry):
            up = jnp.where(d == UNITS - 1, 0, d + 1)
            down = jnp.where(d == 0, UNITS - 1, d - 1)
            here, above, below = pairing[1, d], pairing[1, up], pairing[1, down]
            places[assign[SLOTS * d]] = SLOTS * d
            places[assign[SLOTS * d + 1]] = SLOTS * up + jnp.where(above == 0, 1, 2)
            places[assign[SLOTS * d + 2]] = SLOTS * down + jnp.where(
                below == 0, 2, jnp.where(below == 1, 1, 3)
            )
            places[assign[SLOTS * d + 3]] = SLOTS * d + jnp.where(here == 2, 1, 3)
            return carry

        lax.fori_loop(0, UNITS, unit, 0, unroll=4)

    flat = out.reshape(64 * 2 * STEP, 128)
    for k in range(STEP):
        ct = pl.program_id(0) * STEP + k
        parts = [source[places[4 * ct + j]] for j in range(4)]
        flipped = jnp.concatenate(parts, axis=0).T
        flat[pl.ds(2 * k, 64, stride=2 * STEP), :] = flipped[:64]
        flat[pl.ds(2 * k + 1, 64, stride=2 * STEP), :] = flipped[64:]


SMEM = pl.BlockSpec(memory_space=pltpu.SMEM)
VMEM = pl.BlockSpec(memory_space=pltpu.VMEM)
TABLE = (BLOCKS, BLOCK, 128)


def rounds(assignment, pairing, x):
    dma = pltpu.SemaphoreType.DMA
    chunks, plane, second, ring = dma((2, 16)), dma((2, 2, 4)), dma((2, 4)), dma((2, NZ))
    part = pltpu.VMEM((BLOCKS, 2, BLOCK, 128), BF16)
    return pl.pallas_call(
        fused_kernel,
        out_shape=jax.ShapeDtypeStruct(TABLE, F32),
        in_specs=[SMEM, SMEM, pl.BlockSpec(memory_space=pl.ANY)],
        out_specs=pl.BlockSpec(memory_space=pl.ANY),
        scratch_shapes=[
            pltpu.VMEM((GROUPS, 64, 2 * STEP, 128), F32),
            pltpu.VMEM(TABLE, F32),
            part, part, part, part,
            pltpu.VMEM((UNITS, DEPTHS[0], 128), F32),
            pltpu.VMEM((UNITS // 2, DEPTHS[0], 128), F32),
            pltpu.VMEM((2, 4, DEPTHS[0], 128), F32),
            pltpu.VMEM((2, 4, CHUNK, DEPTHS[0], 128), F32),
            pltpu.VMEM((3, CHUNK, DEPTHS[0], 128), F32),
            pltpu.VMEM((CHUNK, DEPTHS[0], 128), F32),
            pltpu.VMEM((NZ, CHUNK, SLICES[0], 128), F32),
            pltpu.VMEM((NZ, CHUNK, SLICES[0], 128), F32),
            pltpu.VMEM((CHUNK, SLICES[0], 128), F32),
            pltpu.VMEM((NZ, CHUNK, SLICES[0], 128), F32),
            pltpu.VMEM((UNITS, DEPTHS[1], 128), F32),
            pltpu.VMEM((UNITS // 2, DEPTHS[1], 128), F32),
            pltpu.VMEM((2, 4, DEPTHS[1], 128), F32),
            pltpu.VMEM((2, 4, CHUNK, DEPTHS[1], 128), F32),
            pltpu.VMEM((3, CHUNK, DEPTHS[1], 128), F32),
            pltpu.VMEM((CHUNK, DEPTHS[1], 128), F32),
            pltpu.VMEM((NZ, CHUNK, SLICES[1], 128), F32),
            pltpu.VMEM((NZ, CHUNK, SLICES[1], 128), F32),
            pltpu.VMEM((CHUNK, SLICES[1], 128), F32),
            pltpu.VMEM((NZ, CHUNK, SLICES[1], 128), F32),
            pltpu.VMEM((2, UNITS, 64, 128), F32),
            pltpu.VMEM((2, 2, 64, 128), F32),
            pltpu.VMEM((8, 64, 128), F32),
            pltpu.VMEM((8, 64, 128), F32),
            pltpu.VMEM((2, 2, 64, 128), F32),
            dma((GROUPS,)), dma((32,)),
            chunks, chunks, plane, plane, plane, plane, second, second, ring, ring, ring, ring,
            plane, plane, plane, plane, second, second, chunks, chunks, dma((2,)), dma((2,)),
        ],
        compiler_params=PARAMS(collective_id=0, has_side_effects=True),
        name="rounds",
    )(assignment, pairing, x)


def unturned(assignment, pairing, source):
    shape = (64, BLOCKS // 2, 128)
    return pl.pallas_call(
        last_kernel,
        out_shape=jax.ShapeDtypeStruct(shape, F32),
        grid=(BLOCKS // 4 // STEP,),
        in_specs=[SMEM, SMEM, VMEM],
        out_specs=pl.BlockSpec((64, 2 * STEP, 128), lambda i: (0, i, 0)),
        scratch_shapes=[pltpu.SMEM((BLOCKS,), jnp.int32)],
        compiler_params=PARAMS(),
        name="unturn",
    )(assignment, pairing, source)


def on_device(transmission, assignment, pairing):
    rows, _, cols = transmission.shape
    x = transmission.reshape(rows, 2, cols // 128, 128).transpose(0, 2, 1, 3).reshape(rows, -1, 128)
    turned_blocks = rounds(assignment, pairing, x)
    out = unturned(assignment, pairing, turned_blocks)
    out = out.reshape(rows, cols // 128, 2, 128).transpose(0, 2, 1, 3)
    return out.reshape(rows, 2, cols)


def solution(mesh):
    placed = (P(("blk", "row"), None, None), P(), P())
    return jax.shard_map(
        on_device,
        mesh=mesh,
        in_specs=placed,
        out_specs=P(("blk", "row"), None, None),
        check_vma=False,
    )
```

```python
import functools

import jax
import jax.numpy as jnp
from jax import lax
from jax.experimental import pallas as pl
from jax.experimental.pallas import tpu as pltpu
from jax.sharding import PartitionSpec as P

ROWS = 16384
BLOCK = 32
SLOTS = 4
NS_STEPS = 6
UNITS = 64
BLOCKS = 256
MESH = pl.DeviceIdType.MESH
F32 = jnp.float32
BF16 = jnp.bfloat16
NX, NY, NZ = 4, 4, 8
NXY = NX * NY
CHUNK = UNITS // 2 // NXY
DEPTHS = (64, 128)
SLICES = (64 // NZ, 128 // NZ)
STEP = 8
GROUPS = BLOCKS // 4 // STEP
PARAMS = functools.partial(pltpu.CompilerParams, vmem_limit_bytes=60 * 1024 * 1024)


def position(pick, slot):
    if_two = jnp.where(slot == 0, 0, jnp.where(slot == 3, 1, slot + 1))
    if_one = jnp.where(slot == 1, 2, jnp.where(slot == 2, 1, slot))
    return jnp.where(pick == 0, slot, jnp.where(pick == 1, if_one, if_two))


def slot_at(pick, h):
    if h == 0:
        return 0, 1 + pick
    return jnp.where(pick == 0, 2, 1), jnp.where(pick == 2, 2, 3)


def turn_of(slot):
    return jnp.where(slot == 1, -1, jnp.where(slot == 2, 1, 0))


def home_of(pairing, d, slot):
    home = lax.rem(d + turn_of(slot) + UNITS, UNITS)
    return home, position(pairing[0, home], slot)


def pair_places(assign, pairing, rnd, d, h):
    slots = slot_at(pairing[rnd, d], h)
    if rnd == 0:
        return [assign[d * SLOTS + slot] for slot in slots]
    places = []
    for slot in slots:
        home, place = home_of(pairing, d, slot)
        places.append(home * SLOTS + place)
    return places


def pair_around(assign, pairing, home, place):
    pick = pairing[0, home]
    in_first = place < 2
    first = jnp.where(in_first, 0, jnp.where(pick == 0, 2, 1))
    second = jnp.where(in_first, 1 + pick, jnp.where(pick == 2, 2, 3))
    return assign[home * SLOTS + first], assign[home * SLOTS + second]


def lanes_of(shape):
    return lax.broadcasted_iota(jnp.int32, shape, 1)


def rows_of(shape):
    return lax.broadcasted_iota(jnp.int32, shape, 0)


def split(value):
    high = value.astype(BF16)
    return high, (value - high.astype(F32)).astype(BF16)


def turned(pair):
    rolled = pltpu.roll(pair, 64, 1)
    return jnp.where(lanes_of(pair.shape) < 64, rolled, -rolled)


def unpack(unit):
    lane, row = lanes_of(unit.shape), rows_of(unit.shape)
    left = lane < 64
    column = jnp.where(left, lane, lane - 64)
    flipped = jnp.concatenate([unit, unit], axis=0).T
    rolled = pltpu.roll(unit, 64, 1)
    tops = []
    for h in range(2):
        here = jnp.where(left, unit, rolled) if h == 0 else jnp.where(left, rolled, unit)
        there = flipped[64 * h : 64 * h + 64]
        real = jnp.where(row <= column, here, there)
        imag = jnp.where(row > column, here, jnp.where(row < column, -there, 0.0))
        tops.append(jnp.where(left, real, imag))
    return tops


def pack(first, second):
    lane, row = lanes_of(first.shape), rows_of(first.shape)
    left = lane < 64
    real = jnp.where(left, first, second)
    imag = pltpu.roll(jnp.where(left, second, first), 64, 1)
    return jnp.where(row <= jnp.where(left, lane, lane - 64), real, imag)


def nt_dot(a, b):
    return lax.dot_general(a, b, (((1,), (1,)), ((), ())), preferred_element_type=F32)


def parts_of(table, a, b, swapped=False):
    order = (1, 0) if swapped else (0, 1)
    return jnp.concatenate([table[k, half] for half in order for k in (a, b)], axis=0)


def gram_top(tables, a, b, swapped):
    high = parts_of(tables[0], a, b, swapped)
    low = parts_of(tables[1], a, b, swapped)
    pair = slice(64, 128) if swapped else slice(0, 64)
    lhs = jnp.concatenate([high[pair], low[pair]], axis=1)
    rhs = jnp.concatenate([high, high], axis=1)
    return nt_dot(lhs, rhs) + nt_dot(high[pair], low)


def cross_top(tables, left, right):
    lhigh = jnp.concatenate([tables[0][k, 0] for k in left], axis=0)
    llow = jnp.concatenate([tables[1][k, 0] for k in left], axis=0)
    high, low = parts_of(tables[0], *right), parts_of(tables[1], *right)
    lhs = jnp.concatenate([lhigh, llow], axis=1)
    rhs = jnp.concatenate([high, high], axis=1)
    return nt_dot(lhs, rhs) + nt_dot(lhigh, low)


def applied(top, tables, a, b):
    high, low = parts_of(tables[0], a, b), parts_of(tables[1], a, b)
    whigh, wlow = split(top)
    lhs = jnp.concatenate([whigh, wlow], axis=1)
    rhs = jnp.concatenate([high, high], axis=0)
    return jnp.dot(lhs, rhs, preferred_element_type=F32) + jnp.dot(
        whigh, low, preferred_element_type=F32
    )


def keep(tables, first, count, value):
    for index, whole in enumerate((value, turned(value))):
        for table, part in zip(tables, split(whole)):
            table[pl.ds(first, count), index] = part.reshape(count, BLOCK, 128)


def full(top):
    rolled = pltpu.roll(top, 64, 1)
    return jnp.concatenate([top, jnp.where(lanes_of(top.shape) < 64, -rolled, rolled)], axis=0)


def split3(value):
    first, second = split(value)
    rest = value - first.astype(F32) - second.astype(F32)
    return first, second, rest.astype(BF16)


def fdot(a, b):
    a1, a2, a3 = split3(a)
    b1, b2, b3 = split3(b)
    wide = jnp.concatenate([b1, b2], axis=1)
    main = jnp.dot(
        jnp.concatenate([a1, a2], axis=1),
        jnp.concatenate([wide, wide], axis=0),
        preferred_element_type=F32,
    )
    rest = jnp.dot(
        jnp.concatenate([a1, a3], axis=1),
        jnp.concatenate([b3, b1], axis=0),
        preferred_element_type=F32,
    )
    return main[:, :128] + (main[:, 128:] + rest)


def inverse_roots(tops):
    shape = tops[0].shape
    eye = jnp.where(lanes_of(shape) == rows_of(shape), 1.0, 0.0).astype(F32)
    scales = [jnp.sqrt(2.0 * jnp.sum(t * t, axis=(0, 1), keepdims=True)) for t in tops]
    upper = [t / s for t, s in zip(tops, scales)]
    lower = [1.5 * eye - 0.5 * u for u in upper]
    upper = [fdot(u, full(m)) for u, m in zip(upper, lower)]

    def step(_, carry):
        up, low = carry
        middle = [1.5 * eye - 0.5 * fdot(z, full(y)) for y, z in zip(up, low)]
        return (
            [fdot(y, full(m)) for y, m in zip(up, middle)],
            [fdot(m, full(z)) for z, m in zip(low, middle)],
        )

    upper, lower = lax.fori_loop(0, NS_STEPS - 2, step, (upper, lower))
    middle = [1.5 * eye - 0.5 * fdot(z, full(y)) for y, z in zip(upper, lower)]
    lower = [fdot(m, full(z)) for z, m in zip(lower, middle)]
    return [z * jnp.sqrt(ROWS / s) for z, s in zip(lower, scales)]


def triple(left, middle, right):
    return fdot(fdot(left, full(middle)), full(right))


def sided(value, side, wanted, axis, back):
    moved = pltpu.roll(value, back, axis)
    return jnp.where(jnp.full(value.shape, side, jnp.int32) == wanted, value, moved)


def next_gram(cross, gram_u, gram_v, side_u, side_v):
    shape = cross.shape
    lane, row = lanes_of(shape), rows_of(shape)
    upper = sided(sided(cross, side_u, 0, 0, 32), side_v, 1, 1, 32)
    corner_u = sided(sided(gram_u, side_u, 0, 0, 32), side_u, 0, 1, 96)
    corner_v = sided(sided(gram_v, side_v, 1, 0, 32), side_v, 1, 1, 32)
    flipped = jnp.concatenate([upper, upper], axis=0).T
    lower = jnp.where(lane < 64, flipped[:64], -flipped[64:])
    early = lax.rem(lane, 64) < 32
    return jnp.where(
        row < 32, jnp.where(early, corner_u, upper), jnp.where(early, lower, corner_v)
    )


def order_in(i):
    return lax.rem(2 + 3 * i + 3 * (i * (i - 1) // 2), 4)


def order_out(i):
    return lax.rem(3 * i + 3 * (i * (i - 1) // 2), 4)


def fused_kernel(
    assign, pairing, x_in, out, x_held, results, high0, low0, high1, low1,
    packed_0, from_core_0, relay_0, inbox_0, second_in_0, total_0, slices_0, from_z_0, mine_z_0, gathered_0,
    packed_1, from_core_1, relay_1, inbox_1, second_in_1, total_1, slices_1, from_z_1, mine_z_1, gathered_1,
    weights, near, roots_near, grams_near,
    near_in, x_sem, out_sem,
    core_send, core_recv, relay_send, relay_recv, inbox_send, inbox_recv, second_send, second_recv, zr_send,
    zr_recv, zg_send, zg_recv, wfull_send, wfull_recv, whalf_send, whalf_recv, wsecond_send,
    wsecond_recv, wcore_send, wcore_recv, near_send, near_recv,
):
    blk, row = lax.axis_index("blk"), lax.axis_index("row")
    y_lo, z, x = blk // (NZ * NX), lax.rem(blk // NX, NZ), lax.rem(blk, NX)
    y_hi, core = row // 2, lax.rem(row, 2)
    y = y_hi * 2 + y_lo
    half = UNITS // 2
    p, q = x + core * (y - x), y + core * (x - y)

    def device(yy, zz, xx, cc):
        return (lax.rem(yy, 2) * (NZ * NX) + zz * NX + xx, (yy // 2) * 2 + cc)

    def placed(pp, qq):
        return device(qq + core * (pp - qq), z, pp + core * (qq - pp), core)

    def beside(direction):
        return placed(lax.rem(p + 1 + 2 * direction, 4), q)

    def across(distance):
        return placed(p, lax.rem(q + distance, 4))

    partner = device(y, z, x, 1 - core)

    def owner(move):
        chunk = lax.rem(core * NXY + p * 4 + q + move, 2 * NXY)
        cc, pp, qq = chunk // NXY, lax.rem(chunk // 4, 4), lax.rem(chunk, 4)
        return device(qq + cc * (pp - qq), z, pp + cc * (qq - pp), cc)

    def ring_device(step):
        return device(y, lax.rem(z + step, NZ), x, core)

    def my_chunk(da, db):
        return (lax.rem(p + da, 4) * 4 + lax.rem(q + db, 4)) * CHUNK

    def other_chunk(da, db):
        return (lax.rem(q + da, 4) * 4 + lax.rem(p + db, 4)) * CHUNK

    def each(first, last, body):
        def run(step, carry):
            body(step)
            return carry

        lax.fori_loop(first, last, run, 0)

    def remote(src, dst, send, recv, to):
        return pltpu.make_async_remote_copy(
            src_ref=src, dst_ref=dst, send_sem=send, recv_sem=recv, device_id=to, device_id_type=MESH
        )

    barrier = pltpu.get_barrier_semaphore()

    def greet(to):
        pl.semaphore_signal(barrier, inc=1, device_id=to, device_id_type=MESH)

    greet(partner)
    for direction in range(2):
        greet(beside(direction))
    for distance in range(1, 4):
        greet(across(distance))
    for step in range(1, NZ):
        greet(ring_device(step))
    greet(owner(1))
    greet(owner(2 * NXY - 1))

    def x_copy(group):
        return pltpu.make_async_copy(
            x_in.at[:, pl.ds(group * 2 * STEP, 2 * STEP)], x_held.at[group], x_sem.at[group]
        )

    def load_group(group):
        x_copy(group).wait()
        flat = x_held.at[group].reshape(64 * 2 * STEP, 128)
        for k in range(STEP):
            real = flat[pl.ds(2 * k, 64, stride=2 * STEP), :]
            imag = flat[pl.ds(2 * k + 1, 64, stride=2 * STEP), :]
            flipped = jnp.concatenate([real, imag], axis=0).T
            keep((high0, low0), 4 * (group * STEP + k), 4, flipped)

    each(0, GROUPS, lambda group: x_copy(group).start())
    each(0, GROUPS, load_group)
    pl.semaphore_wait(barrier, 8 + NZ - 1)

    packed, from_core = (packed_0, packed_1), (from_core_0, from_core_1)
    relay, inbox = (relay_0, relay_1), (inbox_0, inbox_1)
    second_in, total = (second_in_0, second_in_1), (total_0, total_1)
    slices, from_z = (slices_0, slices_1), (from_z_0, from_z_1)
    mine_z, gathered = (mine_z_0, mine_z_1), (gathered_0, gathered_1)

    def reduction(part):
        source = (high0, low0)

        def core_copy(step):
            place = other_chunk(order_in(step // 4), order_in(lax.rem(step, 4)))
            return remote(
                packed[part].at[pl.ds((1 - core) * half + place, CHUNK)],
                from_core[part].at[pl.ds(place, CHUNK)],
                core_send.at[part, step], core_recv.at[part, step], partner,
            )

        def relay_copy(direction, slot, place):
            return remote(
                from_core[part].at[place + direction], relay[part].at[direction, slot],
                relay_send.at[part, direction, slot], relay_recv.at[part, direction, slot],
                beside(direction),
            )

        def inbox_copy(direction, slot, place):
            return remote(
                from_core[part].at[pl.ds(place, CHUNK)], inbox[part].at[direction, slot],
                inbox_send.at[part, direction, slot], inbox_recv.at[part, direction, slot],
                beside(direction),
            )

        def second_copy(ib, place):
            return remote(
                from_core[part].at[pl.ds(place, CHUNK)], second_in[part].at[ib],
                second_send.at[part, ib], second_recv.at[part, ib], across(order_in(ib)),
            )

        def gram_units(first):
            for u in range(CHUNK):
                d = first + u
                tops = []
                for h in range(2):
                    if part == 0:
                        a, b = pair_places(assign, pairing, 0, d, h)
                        tops.append(gram_top(source, a, b, h == 1))
                        continue
                    around = [
                        pair_around(assign, pairing, *home_of(pairing, d, slot))
                        for slot in slot_at(pairing[1, d], h)
                    ]
                    packed[part][d, pl.ds(64 * h, 64)] = cross_top(source, *around)
                if part == 0:
                    packed[part][d] = pack(*tops)

        def compute(step):
            da, db = order_in(step // 4), order_in(lax.rem(step, 4))
            gram_units((1 - core) * half + other_chunk(da, db))
            core_copy(step).start()
            gram_units(core * half + my_chunk(da, db))

        def inbox_sum(slot):
            for direction in range(2):
                inbox_copy(direction, slot, 0).wait_recv()
            return inbox[part][0, slot] + inbox[part][1, slot]

        def ship(step):
            ia, ib = step // 4, lax.rem(step, 4)
            place = my_chunk(order_in(ia), order_in(ib))
            chunk = pl.ds(place, CHUNK)
            core_copy(step).wait_recv()
            from_core[part][chunk] += packed[part][pl.ds(core * half + place, CHUNK)]

            @pl.when(ia == 0)
            def _():
                for direction in range(2):
                    relay_copy(direction, ib, place).start()

            for direction in range(2):

                @pl.when(ia == 1 + direction)
                def _(direction=direction):
                    relay_copy(direction, ib, place).wait_recv()
                    from_core[part][place + direction] += relay[part][direction, ib]
                    inbox_copy(direction, ib, place).start()

            @pl.when(ia == 3)
            def _():
                from_core[part][chunk] += inbox_sum(ib)
                second_copy(ib, place).start()

        lag = 3 - part

        def advance(step):
            compute(step)
            ship(step - lag)

        def close():
            core_copy(15).wait_recv()
            place = my_chunk(0, 0)
            total[part][...] = (
                from_core[part][pl.ds(place, CHUNK)]
                + packed[part][pl.ds(core * half + place, CHUNK)]
                + inbox_sum(3)
            )
            for ib in range(3):
                second_copy(ib, 0).wait_recv()
                total[part][...] += second_in[part][ib]
            size = SLICES[part]
            for k in range(NZ):
                slices[part][k] = total[part][:, k * size : (k + 1) * size, :]
            for step in far_first:
                zr_copy(step).start()

        def zr_copy(step):
            return remote(
                slices[part].at[lax.rem(z + step, NZ)], from_z[part].at[step],
                zr_send.at[part, step], zr_recv.at[part, step], ring_device(step),
            )

        def zg_copy(step):
            return remote(
                mine_z[part], gathered[part].at[z], zg_send.at[part, step], zg_recv.at[part, step],
                ring_device(step),
            )

        far_first = (4, 3, 5, 2, 6, 1, 7)

        def settle():
            acc = slices[part][z]
            for step in reversed(far_first):
                zr_copy(step).wait_recv()
                acc = acc + from_z[part][step]
            mine_z[part][...] = acc
            for step in far_first:
                zg_copy(step).start()
            gathered[part][z] = acc

        def units():
            for step in reversed(far_first):
                zg_copy(step).wait_recv()
            return [gathered[part][:, u].reshape(DEPTHS[part], 128) for u in range(CHUNK)]

        def drain_core(step):
            core_copy(step).wait_send()

        def drain_plane(slot):
            for direction in range(2):
                relay_copy(direction, slot, 0).wait_send()
                inbox_copy(direction, slot, 0).wait_send()

        def drain_second(ib):
            second_copy(ib, 0).wait_send()

        def drain_z(step):
            zr_copy(step).wait_send()
            zg_copy(step).wait_send()

        def drain():
            each(0, 16, drain_core)
            each(0, 4, drain_plane)
            each(0, 3, drain_second)
            each(1, NZ, drain_z)

        return compute, advance, ship, close, settle, units, drain

    def handing(rnd, source):
        mine = core * half + my_chunk(0, 0)

        def wfull_copy(direction, slot, first):
            part = weights.at[rnd, pl.ds(first, CHUNK)]
            return remote(
                part, part, wfull_send.at[rnd, direction, slot], wfull_recv.at[rnd, direction, slot],
                beside(direction),
            )

        def whalf_copy(direction, slot, first):
            part = weights.at[rnd, first + direction]
            return remote(
                part, part, whalf_send.at[rnd, direction, slot], whalf_recv.at[rnd, direction, slot],
                beside(direction),
            )

        def wsecond_copy(ib, first):
            part = weights.at[rnd, pl.ds(first, CHUNK)]
            return remote(
                part, part, wsecond_send.at[rnd, ib], wsecond_recv.at[rnd, ib],
                across(4 - order_out(ib)),
            )

        def my_units(step):
            return core * half + my_chunk(order_out(step // 4), order_out(lax.rem(step, 4)))

        def other_units(step):
            return (1 - core) * half + other_chunk(order_out(step // 4), order_out(lax.rem(step, 4)))

        def wcore_copy(step):
            part = weights.at[rnd, pl.ds(my_units(step), CHUNK)]
            return remote(
                part, part, wcore_send.at[rnd, step], wcore_recv.at[rnd, step], partner
            )

        def out_copy(first, which):
            place = pl.ds(SLOTS * first, SLOTS * CHUNK)
            return pltpu.make_async_copy(results.at[place], out.at[place], out_sem.at[which])

        def apply_units(first, which):
            for u in range(CHUNK):
                d = first + u
                tops = unpack(weights[rnd, d])
                for h in range(2):
                    a, b = pair_places(assign, pairing, rnd, d, h)
                    new = applied(tops[h], source, a, b)
                    place = SLOTS * d + 2 * h
                    if rnd == 0:
                        keep((high1, low1), place, 2, new)
                    else:
                        results[pl.ds(place, 2)] = new.reshape(2, BLOCK, 128)
            if rnd == 1:
                out_copy(first, which).start()

        def forward(step):
            ia, ib = step // 4, lax.rem(step, 4)
            first = my_units(step)

            @pl.when(ia == 0)
            def _():
                wsecond_copy(ib, first).wait_recv()
                for direction in range(2):
                    wfull_copy(direction, ib, first).start()

            @pl.when(ia == 1)
            def _():
                for direction in range(2):
                    whole = my_units(step + 4 * direction)
                    wfull_copy(direction, ib, whole).wait_recv()
                    whalf_copy(direction, ib, whole).start()

            @pl.when(ia == 3)
            def _():
                for direction in range(2):
                    whalf_copy(direction, ib, first).wait_recv()

            wcore_copy(step).start()

        def use(step):
            apply_units(my_units(step), step)

        def use_other(step):
            wcore_copy(step).wait_recv()
            apply_units(other_units(step), 16 + step)

        def begin():
            for ib in (1, 2, 3):
                wsecond_copy(ib, mine).start()
            for direction in range(2):
                wfull_copy(direction, 0, mine).start()
            wcore_copy(0).start()

        def drain_core(step):
            wcore_copy(step).wait_send()
            if rnd == 1:
                out_copy(0, step).wait()
                out_copy(0, 16 + step).wait()

        def drain_plane(slot):
            for direction in range(2):
                wfull_copy(direction, slot, 0).wait_send()
                whalf_copy(direction, slot, 0).wait_send()

        def drain():
            each(0, 16, drain_core)
            each(0, 4, drain_plane)
            each(1, 4, lambda ib: wsecond_copy(ib, 0).wait_send())

        return begin, forward, use, use_other, drain

    compute_g, advance_g, ship_g, close_g, settle_g, units_g, drain_g = reduction(0)
    compute_c, advance_c, ship_c, close_c, settle_c, units_c, drain_c = reduction(1)
    each(0, 3, compute_g)
    each(3, 16, advance_g)
    for step in range(2):
        compute_c(step)
        ship_g(13 + step)
    each(2, 10, advance_c)
    close_g()
    each(10, 16, advance_c)
    ship_c(14)
    settle_g()
    close_c()
    begin0, forward0, use0, use_other0, drain0 = handing(0, (high0, low0))
    begin1, forward1, use1, use_other1, drain1 = handing(1, (high1, low1))
    mine = core * half + my_chunk(0, 0)

    tops = []
    for unit in units_g():
        tops.extend(unpack(unit))
    roots = inverse_roots(tops)

    def packed_pair(values, u):
        return pack(values[2 * u], pltpu.roll(values[2 * u + 1], 64, 1))

    def near_copy(which):
        return remote(
            near.at[1 - which], near_in.at[which], near_send.at[which], near_recv.at[which],
            owner(1 if which == 0 else 2 * NXY - 1),
        )

    inner = [triple(w, g, w) for w, g in zip(roots, tops)]
    for u in range(CHUNK):
        near[u, 0] = packed_pair(roots, u)
        near[u, 1] = packed_pair(inner, u)
    for which in range(2):
        near_copy(which).start()
    for u in range(CHUNK):
        weights[0, mine + u] = near[u, 0]
        for h in range(2):
            roots_near[2 + 2 * u + h] = roots[2 * u + h]
            grams_near[2 + 2 * u + h] = inner[2 * u + h]
    begin0()
    use0(0)

    def take0(step):
        forward0(step)
        use0(step)

    settle_c()
    each(1, 4, take0)
    for which in range(2):
        near_copy(which).wait_recv()
        for kind, table in enumerate((roots_near, grams_near)):
            for h, top in enumerate(unpack(near_in[which, kind])):
                table[6 * which + h] = top
    crosses = units_c()

    tops = []
    for u in range(CHUNK):
        for h in range(2):
            d = mine + u
            found = []
            for slot in slot_at(pairing[1, d], h):
                _, place = home_of(pairing, d, slot)
                index = 2 * (1 + u + turn_of(slot)) + place // 2
                found.append((index, lax.rem(place, 2)))
            (left, side_u), (right, side_v) = found
            cross = triple(
                roots_near[left], crosses[u][64 * h : 64 * h + 64], roots_near[right]
            )
            tops.append(next_gram(cross, grams_near[left], grams_near[right], side_u, side_v))
    each(4, 8, forward0)
    roots = inverse_roots(tops)
    for u in range(CHUNK):
        weights[1, mine + u] = packed_pair(roots, u)
    begin1()

    def late0(step):
        use0(step)
        use_other0(step - 4)

    def late1(step):
        use1(step)
        use_other1(step - 4)

    each(8, 16, forward0)
    each(4, 12, late0)
    each(1, 4, forward1)
    each(12, 16, late0)
    each(12, 16, use_other0)
    each(0, 4, use1)
    each(0, 4, use_other1)
    each(4, 12, forward1)
    each(4, 8, use1)
    each(8, 12, late1)
    each(12, 16, forward1)
    each(12, 16, late1)
    each(12, 16, use_other1)
    drain_g()
    drain_c()
    drain0()
    drain1()
    for which in range(2):
        near_copy(which).wait_send()


def last_kernel(assign, pairing, source, out, places):
    @pl.when(pl.program_id(0) == 0)
    def _():
        def unit(d, carry):
            up = jnp.where(d == UNITS - 1, 0, d + 1)
            down = jnp.where(d == 0, UNITS - 1, d - 1)
            here, above, below = pairing[1, d], pairing[1, up], pairing[1, down]
            places[assign[SLOTS * d]] = SLOTS * d
            places[assign[SLOTS * d + 1]] = SLOTS * up + jnp.where(above == 0, 1, 2)
            places[assign[SLOTS * d + 2]] = SLOTS * down + jnp.where(
                below == 0, 2, jnp.where(below == 1, 1, 3)
            )
            places[assign[SLOTS * d + 3]] = SLOTS * d + jnp.where(here == 2, 1, 3)
            return carry

        lax.fori_loop(0, UNITS, unit, 0, unroll=4)

    flat = out.reshape(64 * 2 * STEP, 128)
    for k in range(STEP):
        ct = pl.program_id(0) * STEP + k
        parts = [source[places[4 * ct + j]] for j in range(4)]
        flipped = jnp.concatenate(parts, axis=0).T
        flat[pl.ds(2 * k, 64, stride=2 * STEP), :] = flipped[:64]
        flat[pl.ds(2 * k + 1, 64, stride=2 * STEP), :] = flipped[64:]


SMEM = pl.BlockSpec(memory_space=pltpu.SMEM)
VMEM = pl.BlockSpec(memory_space=pltpu.VMEM)
TABLE = (BLOCKS, BLOCK, 128)


def rounds(assignment, pairing, x):
    dma = pltpu.SemaphoreType.DMA
    chunks, plane, second, ring = dma((2, 16)), dma((2, 2, 4)), dma((2, 4)), dma((2, NZ))
    part = pltpu.VMEM((BLOCKS, 2, BLOCK, 128), BF16)
    return pl.pallas_call(
        fused_kernel,
        out_shape=jax.ShapeDtypeStruct(TABLE, F32),
        in_specs=[SMEM, SMEM, pl.BlockSpec(memory_space=pl.ANY)],
        out_specs=pl.BlockSpec(memory_space=pl.ANY),
        scratch_shapes=[
            pltpu.VMEM((GROUPS, 64, 2 * STEP, 128), F32),
            pltpu.VMEM(TABLE, F32),
            part, part, part, part,
            pltpu.VMEM((UNITS, DEPTHS[0], 128), F32),
            pltpu.VMEM((UNITS // 2, DEPTHS[0], 128), F32),
            pltpu.VMEM((2, 4, DEPTHS[0], 128), F32),
            pltpu.VMEM((2, 4, CHUNK, DEPTHS[0], 128), F32),
            pltpu.VMEM((3, CHUNK, DEPTHS[0], 128), F32),
            pltpu.VMEM((CHUNK, DEPTHS[0], 128), F32),
            pltpu.VMEM((NZ, CHUNK, SLICES[0], 128), F32),
            pltpu.VMEM((NZ, CHUNK, SLICES[0], 128), F32),
            pltpu.VMEM((CHUNK, SLICES[0], 128), F32),
            pltpu.VMEM((NZ, CHUNK, SLICES[0], 128), F32),
            pltpu.VMEM((UNITS, DEPTHS[1], 128), F32),
            pltpu.VMEM((UNITS // 2, DEPTHS[1], 128), F32),
            pltpu.VMEM((2, 4, DEPTHS[1], 128), F32),
            pltpu.VMEM((2, 4, CHUNK, DEPTHS[1], 128), F32),
            pltpu.VMEM((3, CHUNK, DEPTHS[1], 128), F32),
            pltpu.VMEM((CHUNK, DEPTHS[1], 128), F32),
            pltpu.VMEM((NZ, CHUNK, SLICES[1], 128), F32),
            pltpu.VMEM((NZ, CHUNK, SLICES[1], 128), F32),
            pltpu.VMEM((CHUNK, SLICES[1], 128), F32),
            pltpu.VMEM((NZ, CHUNK, SLICES[1], 128), F32),
            pltpu.VMEM((2, UNITS, 64, 128), F32),
            pltpu.VMEM((2, 2, 64, 128), F32),
            pltpu.VMEM((8, 64, 128), F32),
            pltpu.VMEM((8, 64, 128), F32),
            pltpu.VMEM((2, 2, 64, 128), F32),
            dma((GROUPS,)), dma((32,)),
            chunks, chunks, plane, plane, plane, plane, second, second, ring, ring, ring, ring,
            plane, plane, plane, plane, second, second, chunks, chunks, dma((2,)), dma((2,)),
        ],
        compiler_params=PARAMS(collective_id=0, has_side_effects=True),
        name="rounds",
    )(assignment, pairing, x)


def unturned(assignment, pairing, source):
    shape = (64, BLOCKS // 2, 128)
    return pl.pallas_call(
        last_kernel,
        out_shape=jax.ShapeDtypeStruct(shape, F32),
        grid=(BLOCKS // 4 // STEP,),
        in_specs=[SMEM, SMEM, VMEM],
        out_specs=pl.BlockSpec((64, 2 * STEP, 128), lambda i: (0, i, 0)),
        scratch_shapes=[pltpu.SMEM((BLOCKS,), jnp.int32)],
        compiler_params=PARAMS(),
        name="unturn",
    )(assignment, pairing, source)


def on_device(transmission, assignment, pairing):
    rows, _, cols = transmission.shape
    x = transmission.reshape(rows, 2, cols // 128, 128).transpose(0, 2, 1, 3).reshape(rows, -1, 128)
    turned_blocks = rounds(assignment, pairing, x)
    out = unturned(assignment, pairing, turned_blocks)
    out = out.reshape(rows, cols // 128, 2, 128).transpose(0, 2, 1, 3)
    return out.reshape(rows, 2, cols)


def solution(mesh):
    placed = (P(("blk", "row"), None, None), P(), P())
    return jax.shard_map(
        on_device,
        mesh=mesh,
        in_specs=placed,
        out_specs=P(("blk", "row"), None, None),
        check_vma=False,
    )
```

```python
import functools

import jax
import jax.numpy as jnp
from jax import lax
from jax.experimental import pallas as pl
from jax.experimental.pallas import tpu as pltpu
from jax.sharding import PartitionSpec as P

ROWS = 16384
BLOCK = 32
SLOTS = 4
NS_STEPS = 6
UNITS = 64
BLOCKS = 256
MESH = pl.DeviceIdType.MESH
F32 = jnp.float32
BF16 = jnp.bfloat16
NX, NY, NZ = 4, 4, 8
NXY = NX * NY
CHUNK = UNITS // 2 // NXY
DEPTH = 3 * 64
SLICES = (64 // NZ, 128 // NZ)
STEP = 8
GROUPS = BLOCKS // 4 // STEP
PARAMS = functools.partial(pltpu.CompilerParams, vmem_limit_bytes=60 * 1024 * 1024)


def position(pick, slot):
    if_two = jnp.where(slot == 0, 0, jnp.where(slot == 3, 1, slot + 1))
    if_one = jnp.where(slot == 1, 2, jnp.where(slot == 2, 1, slot))
    return jnp.where(pick == 0, slot, jnp.where(pick == 1, if_one, if_two))


def slot_at(pick, h):
    if h == 0:
        return 0, 1 + pick
    return jnp.where(pick == 0, 2, 1), jnp.where(pick == 2, 2, 3)


def turn_of(slot):
    return jnp.where(slot == 1, -1, jnp.where(slot == 2, 1, 0))


def home_of(pairing, d, slot):
    home = lax.rem(d + turn_of(slot) + UNITS, UNITS)
    return home, position(pairing[0, home], slot)


def pair_places(assign, pairing, rnd, d, h):
    slots = slot_at(pairing[rnd, d], h)
    if rnd == 0:
        return [assign[d * SLOTS + slot] for slot in slots]
    places = []
    for slot in slots:
        home, place = home_of(pairing, d, slot)
        places.append(home * SLOTS + place)
    return places


def pair_around(assign, pairing, home, place):
    pick = pairing[0, home]
    in_first = place < 2
    first = jnp.where(in_first, 0, jnp.where(pick == 0, 2, 1))
    second = jnp.where(in_first, 1 + pick, jnp.where(pick == 2, 2, 3))
    return assign[home * SLOTS + first], assign[home * SLOTS + second]


def lanes_of(shape):
    return lax.broadcasted_iota(jnp.int32, shape, 1)


def rows_of(shape):
    return lax.broadcasted_iota(jnp.int32, shape, 0)


def split(value):
    high = value.astype(BF16)
    return high, (value - high.astype(F32)).astype(BF16)


def turned(pair):
    rolled = pltpu.roll(pair, 64, 1)
    return jnp.where(lanes_of(pair.shape) < 64, rolled, -rolled)


def unpack(unit):
    lane, row = lanes_of(unit.shape), rows_of(unit.shape)
    left = lane < 64
    column = jnp.where(left, lane, lane - 64)
    flipped = jnp.concatenate([unit, unit], axis=0).T
    rolled = pltpu.roll(unit, 64, 1)
    tops = []
    for h in range(2):
        here = jnp.where(left, unit, rolled) if h == 0 else jnp.where(left, rolled, unit)
        there = flipped[64 * h : 64 * h + 64]
        real = jnp.where(row <= column, here, there)
        imag = jnp.where(row > column, here, jnp.where(row < column, -there, 0.0))
        tops.append(jnp.where(left, real, imag))
    return tops


def pack(first, second):
    lane, row = lanes_of(first.shape), rows_of(first.shape)
    left = lane < 64
    real = jnp.where(left, first, second)
    imag = pltpu.roll(jnp.where(left, second, first), 64, 1)
    return jnp.where(row <= jnp.where(left, lane, lane - 64), real, imag)


def nt_dot(a, b):
    return lax.dot_general(a, b, (((1,), (1,)), ((), ())), preferred_element_type=F32)


def parts_of(table, a, b, swapped=False):
    order = (1, 0) if swapped else (0, 1)
    return jnp.concatenate([table[k, half] for half in order for k in (a, b)], axis=0)


def gram_top(tables, a, b, swapped):
    high = parts_of(tables[0], a, b, swapped)
    low = parts_of(tables[1], a, b, swapped)
    pair = slice(64, 128) if swapped else slice(0, 64)
    lhs = jnp.concatenate([high[pair], low[pair]], axis=1)
    rhs = jnp.concatenate([high, high], axis=1)
    return nt_dot(lhs, rhs) + nt_dot(high[pair], low)


def cross_top(tables, left, right):
    lhigh = jnp.concatenate([tables[0][k, 0] for k in left], axis=0)
    llow = jnp.concatenate([tables[1][k, 0] for k in left], axis=0)
    high, low = parts_of(tables[0], *right), parts_of(tables[1], *right)
    lhs = jnp.concatenate([lhigh, llow], axis=1)
    rhs = jnp.concatenate([high, high], axis=1)
    return nt_dot(lhs, rhs) + nt_dot(lhigh, low)


def applied(top, tables, a, b):
    high, low = parts_of(tables[0], a, b), parts_of(tables[1], a, b)
    whigh, wlow = split(top)
    lhs = jnp.concatenate([whigh, wlow], axis=1)
    rhs = jnp.concatenate([high, high], axis=0)
    return jnp.dot(lhs, rhs, preferred_element_type=F32) + jnp.dot(
        whigh, low, preferred_element_type=F32
    )


def keep(tables, first, count, value):
    for index, whole in enumerate((value, turned(value))):
        for table, part in zip(tables, split(whole)):
            table[pl.ds(first, count), index] = part.reshape(count, BLOCK, 128)


def full(top):
    rolled = pltpu.roll(top, 64, 1)
    return jnp.concatenate([top, jnp.where(lanes_of(top.shape) < 64, -rolled, rolled)], axis=0)


def split3(value):
    first, second = split(value)
    rest = value - first.astype(F32) - second.astype(F32)
    return first, second, rest.astype(BF16)


def fdot(a, b):
    a1, a2, a3 = split3(a)
    b1, b2, b3 = split3(b)
    wide = jnp.concatenate([b1, b2], axis=1)
    main = jnp.dot(
        jnp.concatenate([a1, a2], axis=1),
        jnp.concatenate([wide, wide], axis=0),
        preferred_element_type=F32,
    )
    rest = jnp.dot(
        jnp.concatenate([a1, a3], axis=1),
        jnp.concatenate([b3, b1], axis=0),
        preferred_element_type=F32,
    )
    return main[:, :128] + (main[:, 128:] + rest)


def inverse_roots(tops):
    shape = tops[0].shape
    eye = jnp.where(lanes_of(shape) == rows_of(shape), 1.0, 0.0).astype(F32)
    scales = [jnp.sqrt(2.0 * jnp.sum(t * t, axis=(0, 1), keepdims=True)) for t in tops]
    upper = [t / s for t, s in zip(tops, scales)]
    lower = [1.5 * eye - 0.5 * u for u in upper]
    upper = [fdot(u, full(m)) for u, m in zip(upper, lower)]

    def step(_, carry):
        up, low = carry
        middle = [1.5 * eye - 0.5 * fdot(z, full(y)) for y, z in zip(up, low)]
        return (
            [fdot(y, full(m)) for y, m in zip(up, middle)],
            [fdot(m, full(z)) for z, m in zip(low, middle)],
        )

    upper, lower = lax.fori_loop(0, NS_STEPS - 2, step, (upper, lower))
    middle = [1.5 * eye - 0.5 * fdot(z, full(y)) for y, z in zip(upper, lower)]
    lower = [fdot(m, full(z)) for z, m in zip(lower, middle)]
    return [z * jnp.sqrt(ROWS / s) for z, s in zip(lower, scales)]


def triple(left, middle, right):
    return fdot(fdot(left, full(middle)), full(right))


def sided(value, side, wanted, axis, back):
    moved = pltpu.roll(value, back, axis)
    return jnp.where(jnp.full(value.shape, side, jnp.int32) == wanted, value, moved)


def next_gram(cross, gram_u, gram_v, side_u, side_v):
    shape = cross.shape
    lane, row = lanes_of(shape), rows_of(shape)
    upper = sided(sided(cross, side_u, 0, 0, 32), side_v, 1, 1, 32)
    corner_u = sided(sided(gram_u, side_u, 0, 0, 32), side_u, 0, 1, 96)
    corner_v = sided(sided(gram_v, side_v, 1, 0, 32), side_v, 1, 1, 32)
    flipped = jnp.concatenate([upper, upper], axis=0).T
    lower = jnp.where(lane < 64, flipped[:64], -flipped[64:])
    early = lax.rem(lane, 64) < 32
    return jnp.where(
        row < 32, jnp.where(early, corner_u, upper), jnp.where(early, lower, corner_v)
    )


def order_in(i):
    return lax.rem(2 + 3 * i + 3 * (i * (i - 1) // 2), 4)


def order_out(i):
    return lax.rem(3 * i + 3 * (i * (i - 1) // 2), 4)


def fused_kernel(
    assign, pairing, x_in, out, x_held, results, high0, low0, high1, low1, packed, from_core, relay,
    inbox, second_in, total, slices_0, from_z_0, mine_z_0, gathered_0, slices_1, from_z_1, mine_z_1,
    gathered_1, weights, near, roots_near, grams_near,
    near_in, x_sem, out_sem,
    core_send, core_recv, relay_send, relay_recv, inbox_send, inbox_recv, second_send, second_recv, zr_send,
    zr_recv, zg_send, zg_recv, wfull_send, wfull_recv, whalf_send, whalf_recv, wsecond_send,
    wsecond_recv, wcore_send, wcore_recv, near_send, near_recv,
):
    blk, row = lax.axis_index("blk"), lax.axis_index("row")
    y_lo, z, x = blk // (NZ * NX), lax.rem(blk // NX, NZ), lax.rem(blk, NX)
    y_hi, core = row // 2, lax.rem(row, 2)
    y = y_hi * 2 + y_lo
    half = UNITS // 2
    p, q = x + core * (y - x), y + core * (x - y)

    def device(yy, zz, xx, cc):
        return (lax.rem(yy, 2) * (NZ * NX) + zz * NX + xx, (yy // 2) * 2 + cc)

    def placed(pp, qq):
        return device(qq + core * (pp - qq), z, pp + core * (qq - pp), core)

    def beside(direction):
        return placed(lax.rem(p + 1 + 2 * direction, 4), q)

    def across(distance):
        return placed(p, lax.rem(q + distance, 4))

    partner = device(y, z, x, 1 - core)

    def owner(move):
        chunk = lax.rem(core * NXY + p * 4 + q + move, 2 * NXY)
        cc, pp, qq = chunk // NXY, lax.rem(chunk // 4, 4), lax.rem(chunk, 4)
        return device(qq + cc * (pp - qq), z, pp + cc * (qq - pp), cc)

    def ring_device(step):
        return device(y, lax.rem(z + step, NZ), x, core)

    def my_chunk(da, db):
        return (lax.rem(p + da, 4) * 4 + lax.rem(q + db, 4)) * CHUNK

    def other_chunk(da, db):
        return (lax.rem(q + da, 4) * 4 + lax.rem(p + db, 4)) * CHUNK

    def each(first, last, body):
        def run(step, carry):
            body(step)
            return carry

        lax.fori_loop(first, last, run, 0)

    def remote(src, dst, send, recv, to):
        return pltpu.make_async_remote_copy(
            src_ref=src, dst_ref=dst, send_sem=send, recv_sem=recv, device_id=to, device_id_type=MESH
        )

    barrier = pltpu.get_barrier_semaphore()

    def greet(to):
        pl.semaphore_signal(barrier, inc=1, device_id=to, device_id_type=MESH)

    greet(partner)
    for direction in range(2):
        greet(beside(direction))
    for distance in range(1, 4):
        greet(across(distance))
    for step in range(1, NZ):
        greet(ring_device(step))
    greet(owner(1))
    greet(owner(2 * NXY - 1))

    def x_copy(group):
        return pltpu.make_async_copy(
            x_in.at[:, pl.ds(group * 2 * STEP, 2 * STEP)], x_held.at[group], x_sem.at[group]
        )

    def load_group(group):
        x_copy(group).wait()
        flat = x_held.at[group].reshape(64 * 2 * STEP, 128)
        for k in range(STEP):
            real = flat[pl.ds(2 * k, 64, stride=2 * STEP), :]
            imag = flat[pl.ds(2 * k + 1, 64, stride=2 * STEP), :]
            flipped = jnp.concatenate([real, imag], axis=0).T
            keep((high0, low0), 4 * (group * STEP + k), 4, flipped)

    each(0, GROUPS, lambda group: x_copy(group).start())
    each(0, GROUPS, load_group)
    pl.semaphore_wait(barrier, 8 + NZ - 1)

    slices, from_z = (slices_0, slices_1), (from_z_0, from_z_1)
    mine_z, gathered = (mine_z_0, mine_z_1), (gathered_0, gathered_1)

    def reduced():
        source = (high0, low0)

        def core_copy(step):
            place = other_chunk(order_in(step // 4), order_in(lax.rem(step, 4)))
            return remote(
                packed.at[pl.ds((1 - core) * half + place, CHUNK)],
                from_core.at[pl.ds(place, CHUNK)],
                core_send.at[step], core_recv.at[step], partner,
            )

        def relay_copy(direction, slot, place):
            return remote(
                from_core.at[place + direction], relay.at[direction, slot],
                relay_send.at[direction, slot], relay_recv.at[direction, slot],
                beside(direction),
            )

        def inbox_copy(direction, slot, place):
            return remote(
                from_core.at[pl.ds(place, CHUNK)], inbox.at[direction, slot],
                inbox_send.at[direction, slot], inbox_recv.at[direction, slot],
                beside(direction),
            )

        def second_copy(ib, place):
            return remote(
                from_core.at[pl.ds(place, CHUNK)], second_in.at[ib],
                second_send.at[ib], second_recv.at[ib], across(order_in(ib)),
            )

        def gram_units(first):
            for u in range(CHUNK):
                d = first + u
                tops = []
                for h in range(2):
                    a, b = pair_places(assign, pairing, 0, d, h)
                    tops.append(gram_top(source, a, b, h == 1))
                    slots = slot_at(pairing[1, d], h)
                    around = [
                        pair_around(assign, pairing, *home_of(pairing, d, slot)) for slot in slots
                    ]
                    packed[d, pl.ds(64 + 64 * h, 64)] = cross_top(source, *around)
                packed[d, pl.ds(0, 64)] = pack(*tops)

        def compute(step):
            da, db = order_in(step // 4), order_in(lax.rem(step, 4))
            gram_units((1 - core) * half + other_chunk(da, db))
            core_copy(step).start()
            gram_units(core * half + my_chunk(da, db))

        def inbox_sum(slot):
            for direction in range(2):
                inbox_copy(direction, slot, 0).wait_recv()
            return inbox[0, slot] + inbox[1, slot]

        def ship(step):
            ia, ib = step // 4, lax.rem(step, 4)
            place = my_chunk(order_in(ia), order_in(ib))
            chunk = pl.ds(place, CHUNK)
            core_copy(step).wait_recv()
            from_core[chunk] += packed[pl.ds(core * half + place, CHUNK)]

            @pl.when(ia == 0)
            def _():
                for direction in range(2):
                    relay_copy(direction, ib, place).start()

            for direction in range(2):

                @pl.when(ia == 1 + direction)
                def _(direction=direction):
                    relay_copy(direction, ib, place).wait_recv()
                    from_core[place + direction] += relay[direction, ib]
                    inbox_copy(direction, ib, place).start()

            @pl.when(ia == 3)
            def _():
                from_core[chunk] += inbox_sum(ib)
                second_copy(ib, place).start()

        def advance(step):
            compute(step)
            ship(step - 1)

        compute(0)
        each(1, 16, advance)
        core_copy(15).wait_recv()
        place = my_chunk(0, 0)
        total[...] = (
            from_core[pl.ds(place, CHUNK)]
            + packed[pl.ds(core * half + place, CHUNK)]
            + inbox_sum(3)
        )
        for ib in range(3):
            second_copy(ib, 0).wait_recv()
            total[...] += second_in[ib]

        for part, size in enumerate(SLICES):
            for k in range(NZ):
                begin = 64 * part + k * size
                slices[part][k] = total[:, begin : begin + size, :]

        def zr_copy(part, step):
            return remote(
                slices[part].at[lax.rem(z + step, NZ)], from_z[part].at[step],
                zr_send.at[part, step], zr_recv.at[part, step], ring_device(step),
            )

        def zg_copy(part, step):
            return remote(
                mine_z[part], gathered[part].at[z], zg_send.at[part, step], zg_recv.at[part, step],
                ring_device(step),
            )

        far_first = (4, 3, 5, 2, 6, 1, 7)
        for part in range(2):
            for step in far_first:
                zr_copy(part, step).start()
        for part in range(2):
            acc = slices[part][z]
            for step in reversed(far_first):
                zr_copy(part, step).wait_recv()
                acc = acc + from_z[part][step]
            mine_z[part][...] = acc
            for step in far_first:
                zg_copy(part, step).start()
            gathered[part][z] = acc

        def units_of(part):
            for step in reversed(far_first):
                zg_copy(part, step).wait_recv()
            return [gathered[part][:, u].reshape(NZ * SLICES[part], 128) for u in range(CHUNK)]

        def drain_core(step):
            core_copy(step).wait_send()

        def drain_plane(slot):
            for direction in range(2):
                relay_copy(direction, slot, 0).wait_send()
                inbox_copy(direction, slot, 0).wait_send()

        def drain_second(ib):
            second_copy(ib, 0).wait_send()

        def drain_z(step):
            for part in range(2):
                zr_copy(part, step).wait_send()
                zg_copy(part, step).wait_send()

        def drain():
            each(0, 16, drain_core)
            each(0, 4, drain_plane)
            each(0, 3, drain_second)
            each(1, NZ, drain_z)

        return units_of, drain

    def handing(rnd, source):
        mine = core * half + my_chunk(0, 0)

        def wfull_copy(direction, slot, first):
            part = weights.at[rnd, pl.ds(first, CHUNK)]
            return remote(
                part, part, wfull_send.at[rnd, direction, slot], wfull_recv.at[rnd, direction, slot],
                beside(direction),
            )

        def whalf_copy(direction, slot, first):
            part = weights.at[rnd, first + direction]
            return remote(
                part, part, whalf_send.at[rnd, direction, slot], whalf_recv.at[rnd, direction, slot],
                beside(direction),
            )

        def wsecond_copy(ib, first):
            part = weights.at[rnd, pl.ds(first, CHUNK)]
            return remote(
                part, part, wsecond_send.at[rnd, ib], wsecond_recv.at[rnd, ib],
                across(4 - order_out(ib)),
            )

        def my_units(step):
            return core * half + my_chunk(order_out(step // 4), order_out(lax.rem(step, 4)))

        def other_units(step):
            return (1 - core) * half + other_chunk(order_out(step // 4), order_out(lax.rem(step, 4)))

        def wcore_copy(step):
            part = weights.at[rnd, pl.ds(my_units(step), CHUNK)]
            return remote(
                part, part, wcore_send.at[rnd, step], wcore_recv.at[rnd, step], partner
            )

        def out_copy(first, which):
            place = pl.ds(SLOTS * first, SLOTS * CHUNK)
            return pltpu.make_async_copy(results.at[place], out.at[place], out_sem.at[which])

        def apply_units(first, which):
            for u in range(CHUNK):
                d = first + u
                tops = unpack(weights[rnd, d])
                for h in range(2):
                    a, b = pair_places(assign, pairing, rnd, d, h)
                    new = applied(tops[h], source, a, b)
                    place = SLOTS * d + 2 * h
                    if rnd == 0:
                        keep((high1, low1), place, 2, new)
                    else:
                        results[pl.ds(place, 2)] = new.reshape(2, BLOCK, 128)
            if rnd == 1:
                out_copy(first, which).start()

        def forward(step):
            ia, ib = step // 4, lax.rem(step, 4)
            first = my_units(step)

            @pl.when(ia == 0)
            def _():
                wsecond_copy(ib, first).wait_recv()
                for direction in range(2):
                    wfull_copy(direction, ib, first).start()

            @pl.when(ia == 1)
            def _():
                for direction in range(2):
                    whole = my_units(step + 4 * direction)
                    wfull_copy(direction, ib, whole).wait_recv()
                    whalf_copy(direction, ib, whole).start()

            @pl.when(ia == 3)
            def _():
                for direction in range(2):
                    whalf_copy(direction, ib, first).wait_recv()

            wcore_copy(step).start()

        def use(step):
            apply_units(my_units(step), step)

        def use_other(step):
            wcore_copy(step).wait_recv()
            apply_units(other_units(step), 16 + step)

        def begin():
            for ib in (1, 2, 3):
                wsecond_copy(ib, mine).start()
            for direction in range(2):
                wfull_copy(direction, 0, mine).start()
            wcore_copy(0).start()

        def drain_core(step):
            wcore_copy(step).wait_send()
            if rnd == 1:
                out_copy(0, step).wait()
                out_copy(0, 16 + step).wait()

        def drain_plane(slot):
            for direction in range(2):
                wfull_copy(direction, slot, 0).wait_send()
                whalf_copy(direction, slot, 0).wait_send()

        def drain():
            each(0, 16, drain_core)
            each(0, 4, drain_plane)
            each(1, 4, lambda ib: wsecond_copy(ib, 0).wait_send())

        return begin, forward, use, use_other, drain

    units_of, drain_reduced = reduced()
    begin0, forward0, use0, use_other0, drain0 = handing(0, (high0, low0))
    begin1, forward1, use1, use_other1, drain1 = handing(1, (high1, low1))
    mine = core * half + my_chunk(0, 0)

    tops = []
    for unit in units_of(0):
        tops.extend(unpack(unit))
    roots = inverse_roots(tops)

    def packed_pair(values, u):
        return pack(values[2 * u], pltpu.roll(values[2 * u + 1], 64, 1))

    def near_copy(which):
        return remote(
            near.at[1 - which], near_in.at[which], near_send.at[which], near_recv.at[which],
            owner(1 if which == 0 else 2 * NXY - 1),
        )

    inner = [triple(w, g, w) for w, g in zip(roots, tops)]
    for u in range(CHUNK):
        near[u, 0] = packed_pair(roots, u)
        near[u, 1] = packed_pair(inner, u)
    for which in range(2):
        near_copy(which).start()
    for u in range(CHUNK):
        weights[0, mine + u] = near[u, 0]
        for h in range(2):
            roots_near[2 + 2 * u + h] = roots[2 * u + h]
            grams_near[2 + 2 * u + h] = inner[2 * u + h]
    begin0()
    use0(0)

    def take0(step):
        forward0(step)
        use0(step)
        use_other0(step - 1)

    each(1, 4, take0)
    crosses = units_of(1)
    for which in range(2):
        near_copy(which).wait_recv()
        for kind, table in enumerate((roots_near, grams_near)):
            for h, top in enumerate(unpack(near_in[which, kind])):
                table[6 * which + h] = top

    tops = []
    for u in range(CHUNK):
        for h in range(2):
            d = mine + u
            found = []
            for slot in slot_at(pairing[1, d], h):
                _, place = home_of(pairing, d, slot)
                index = 2 * (1 + u + turn_of(slot)) + place // 2
                found.append((index, lax.rem(place, 2)))
            (left, side_u), (right, side_v) = found
            cross = triple(
                roots_near[left], crosses[u][64 * h : 64 * h + 64], roots_near[right]
            )
            tops.append(next_gram(cross, grams_near[left], grams_near[right], side_u, side_v))
    roots = inverse_roots(tops)
    for u in range(CHUNK):
        weights[1, mine + u] = packed_pair(roots, u)
    begin1()
    each(4, 12, take0)
    each(1, 4, forward1)
    each(12, 16, take0)
    use_other0(15)
    use1(0)

    def take1(step):
        use1(step)
        use_other1(step - 1)

    def forward_and_take1(step):
        forward1(step)
        take1(step)

    each(1, 4, take1)
    each(4, 8, forward1)
    each(4, 8, take1)
    each(8, 16, forward_and_take1)
    use_other1(15)
    drain_reduced()
    drain0()
    drain1()
    for which in range(2):
        near_copy(which).wait_send()


def last_kernel(assign, pairing, blocks, out, places, source, sem):
    @pl.when(pl.program_id(0) == 0)
    def _():
        copy = pltpu.make_async_copy(blocks, source, sem)
        copy.start()

        def unit(d, carry):
            up = jnp.where(d == UNITS - 1, 0, d + 1)
            down = jnp.where(d == 0, UNITS - 1, d - 1)
            here, above, below = pairing[1, d], pairing[1, up], pairing[1, down]
            places[assign[SLOTS * d]] = SLOTS * d
            places[assign[SLOTS * d + 1]] = SLOTS * up + jnp.where(above == 0, 1, 2)
            places[assign[SLOTS * d + 2]] = SLOTS * down + jnp.where(
                below == 0, 2, jnp.where(below == 1, 1, 3)
            )
            places[assign[SLOTS * d + 3]] = SLOTS * d + jnp.where(here == 2, 1, 3)
            return carry

        lax.fori_loop(0, UNITS, unit, 0, unroll=4)
        copy.wait()

    flat = out.reshape(64 * 2 * STEP, 128)
    for k in range(STEP):
        ct = pl.program_id(0) * STEP + k
        parts = [source[places[4 * ct + j]] for j in range(4)]
        flipped = jnp.concatenate(parts, axis=0).T
        flat[pl.ds(2 * k, 64, stride=2 * STEP), :] = flipped[:64]
        flat[pl.ds(2 * k + 1, 64, stride=2 * STEP), :] = flipped[64:]


SMEM = pl.BlockSpec(memory_space=pltpu.SMEM)
VMEM = pl.BlockSpec(memory_space=pltpu.VMEM)
TABLE = (BLOCKS, BLOCK, 128)


def rounds(assignment, pairing, x):
    dma = pltpu.SemaphoreType.DMA
    chunks, plane, second, ring = dma((2, 16)), dma((2, 2, 4)), dma((2, 4)), dma((2, NZ))
    part = pltpu.VMEM((BLOCKS, 2, BLOCK, 128), BF16)
    return pl.pallas_call(
        fused_kernel,
        out_shape=jax.ShapeDtypeStruct(TABLE, F32),
        in_specs=[SMEM, SMEM, pl.BlockSpec(memory_space=pl.ANY)],
        out_specs=pl.BlockSpec(memory_space=pl.ANY),
        scratch_shapes=[
            pltpu.VMEM((GROUPS, 64, 2 * STEP, 128), F32),
            pltpu.VMEM(TABLE, F32),
            part, part, part, part,
            pltpu.VMEM((UNITS, DEPTH, 128), F32),
            pltpu.VMEM((UNITS // 2, DEPTH, 128), F32),
            pltpu.VMEM((2, 4, DEPTH, 128), F32),
            pltpu.VMEM((2, 4, CHUNK, DEPTH, 128), F32),
            pltpu.VMEM((3, CHUNK, DEPTH, 128), F32),
            pltpu.VMEM((CHUNK, DEPTH, 128), F32),
            pltpu.VMEM((NZ, CHUNK, SLICES[0], 128), F32),
            pltpu.VMEM((NZ, CHUNK, SLICES[0], 128), F32),
            pltpu.VMEM((CHUNK, SLICES[0], 128), F32),
            pltpu.VMEM((NZ, CHUNK, SLICES[0], 128), F32),
            pltpu.VMEM((NZ, CHUNK, SLICES[1], 128), F32),
            pltpu.VMEM((NZ, CHUNK, SLICES[1], 128), F32),
            pltpu.VMEM((CHUNK, SLICES[1], 128), F32),
            pltpu.VMEM((NZ, CHUNK, SLICES[1], 128), F32),
            pltpu.VMEM((2, UNITS, 64, 128), F32),
            pltpu.VMEM((2, 2, 64, 128), F32),
            pltpu.VMEM((8, 64, 128), F32),
            pltpu.VMEM((8, 64, 128), F32),
            pltpu.VMEM((2, 2, 64, 128), F32),
            dma((GROUPS,)), dma((32,)),
            dma((16,)), dma((16,)), dma((2, 4)), dma((2, 4)), dma((2, 4)), dma((2, 4)),
            dma((4,)), dma((4,)), ring, ring, ring, ring,
            plane, plane, plane, plane, second, second, chunks, chunks, dma((2,)), dma((2,)),
        ],
        compiler_params=PARAMS(collective_id=0, has_side_effects=True),
        name="rounds",
    )(assignment, pairing, x)


def unturned(assignment, pairing, source):
    shape = (64, BLOCKS // 2, 128)
    return pl.pallas_call(
        last_kernel,
        out_shape=jax.ShapeDtypeStruct(shape, F32),
        grid=(BLOCKS // 4 // STEP,),
        in_specs=[SMEM, SMEM, pl.BlockSpec(memory_space=pl.ANY)],
        out_specs=pl.BlockSpec((64, 2 * STEP, 128), lambda i: (0, i, 0)),
        scratch_shapes=[
            pltpu.SMEM((BLOCKS,), jnp.int32), pltpu.VMEM(TABLE, F32), pltpu.SemaphoreType.DMA
        ],
        compiler_params=PARAMS(),
        name="unturn",
    )(assignment, pairing, source)


def on_device(transmission, assignment, pairing):
    rows, _, cols = transmission.shape
    x = transmission.reshape(rows, 2, cols // 128, 128).transpose(0, 2, 1, 3).reshape(rows, -1, 128)
    turned_blocks = rounds(assignment, pairing, x)
    out = unturned(assignment, pairing, turned_blocks)
    out = out.reshape(rows, cols // 128, 2, 128).transpose(0, 2, 1, 3)
    return out.reshape(rows, 2, cols)


def solution(mesh):
    placed = (P(("blk", "row"), None, None), P(), P())
    return jax.shard_map(
        on_device,
        mesh=mesh,
        in_specs=placed,
        out_specs=P(("blk", "row"), None, None),
        check_vma=False,
    )
```

```python
import functools

import jax
import jax.numpy as jnp
from jax import lax
from jax.experimental import pallas as pl
from jax.experimental.pallas import tpu as pltpu
from jax.sharding import PartitionSpec as P

ROWS = 16384
BLOCK = 32
SLOTS = 4
NS_STEPS = 6
UNITS = 64
BLOCKS = 256
MESH = pl.DeviceIdType.MESH
F32 = jnp.float32
BF16 = jnp.bfloat16
NX, NY, NZ = 4, 4, 8
NXY = NX * NY
CHUNK = UNITS // 2 // NXY
DEPTH = 3 * 64
SLICES = (64 // NZ, 128 // NZ)
STEP = 8
GROUPS = BLOCKS // 4 // STEP
PARAMS = functools.partial(pltpu.CompilerParams, vmem_limit_bytes=60 * 1024 * 1024)


def position(pick, slot):
    if_two = jnp.where(slot == 0, 0, jnp.where(slot == 3, 1, slot + 1))
    if_one = jnp.where(slot == 1, 2, jnp.where(slot == 2, 1, slot))
    return jnp.where(pick == 0, slot, jnp.where(pick == 1, if_one, if_two))


def slot_at(pick, h):
    if h == 0:
        return 0, 1 + pick
    return jnp.where(pick == 0, 2, 1), jnp.where(pick == 2, 2, 3)


def turn_of(slot):
    return jnp.where(slot == 1, -1, jnp.where(slot == 2, 1, 0))


def home_of(pairing, d, slot):
    home = lax.rem(d + turn_of(slot) + UNITS, UNITS)
    return home, position(pairing[0, home], slot)


def pair_places(assign, pairing, rnd, d, h):
    slots = slot_at(pairing[rnd, d], h)
    if rnd == 0:
        return [assign[d * SLOTS + slot] for slot in slots]
    places = []
    for slot in slots:
        home, place = home_of(pairing, d, slot)
        places.append(home * SLOTS + place)
    return places


def pair_around(assign, pairing, home, place):
    pick = pairing[0, home]
    in_first = place < 2
    first = jnp.where(in_first, 0, jnp.where(pick == 0, 2, 1))
    second = jnp.where(in_first, 1 + pick, jnp.where(pick == 2, 2, 3))
    return assign[home * SLOTS + first], assign[home * SLOTS + second]


def lanes_of(shape):
    return lax.broadcasted_iota(jnp.int32, shape, 1)


def rows_of(shape):
    return lax.broadcasted_iota(jnp.int32, shape, 0)


def split(value):
    high = value.astype(BF16)
    return high, (value - high.astype(F32)).astype(BF16)


def turned(pair):
    rolled = pltpu.roll(pair, 64, 1)
    return jnp.where(lanes_of(pair.shape) < 64, rolled, -rolled)


def unpack(unit):
    lane, row = lanes_of(unit.shape), rows_of(unit.shape)
    left = lane < 64
    column = jnp.where(left, lane, lane - 64)
    flipped = jnp.concatenate([unit, unit], axis=0).T
    rolled = pltpu.roll(unit, 64, 1)
    tops = []
    for h in range(2):
        here = jnp.where(left, unit, rolled) if h == 0 else jnp.where(left, rolled, unit)
        there = flipped[64 * h : 64 * h + 64]
        real = jnp.where(row <= column, here, there)
        imag = jnp.where(row > column, here, jnp.where(row < column, -there, 0.0))
        tops.append(jnp.where(left, real, imag))
    return tops


def pack(first, second):
    lane, row = lanes_of(first.shape), rows_of(first.shape)
    left = lane < 64
    real = jnp.where(left, first, second)
    imag = pltpu.roll(jnp.where(left, second, first), 64, 1)
    return jnp.where(row <= jnp.where(left, lane, lane - 64), real, imag)


def nt_dot(a, b):
    return lax.dot_general(a, b, (((1,), (1,)), ((), ())), preferred_element_type=F32)


def parts_of(table, a, b, swapped=False):
    order = (1, 0) if swapped else (0, 1)
    return jnp.concatenate([table[k, half] for half in order for k in (a, b)], axis=0)


def gram_top(tables, a, b, swapped):
    high = parts_of(tables[0], a, b, swapped)
    low = parts_of(tables[1], a, b, swapped)
    pair = slice(64, 128) if swapped else slice(0, 64)
    lhs = jnp.concatenate([high[pair], low[pair]], axis=1)
    rhs = jnp.concatenate([high, high], axis=1)
    return nt_dot(lhs, rhs) + nt_dot(high[pair], low)


def cross_top(tables, left, right):
    lhigh = jnp.concatenate([tables[0][k, 0] for k in left], axis=0)
    llow = jnp.concatenate([tables[1][k, 0] for k in left], axis=0)
    high, low = parts_of(tables[0], *right), parts_of(tables[1], *right)
    lhs = jnp.concatenate([lhigh, llow], axis=1)
    rhs = jnp.concatenate([high, high], axis=1)
    return nt_dot(lhs, rhs) + nt_dot(lhigh, low)


def applied(top, tables, a, b):
    high, low = parts_of(tables[0], a, b), parts_of(tables[1], a, b)
    whigh, wlow = split(top)
    lhs = jnp.concatenate([whigh, wlow], axis=1)
    rhs = jnp.concatenate([high, high], axis=0)
    return jnp.dot(lhs, rhs, preferred_element_type=F32) + jnp.dot(
        whigh, low, preferred_element_type=F32
    )


def keep(tables, first, count, value):
    for index, whole in enumerate((value, turned(value))):
        for table, part in zip(tables, split(whole)):
            table[pl.ds(first, count), index] = part.reshape(count, BLOCK, 128)


def full(top):
    rolled = pltpu.roll(top, 64, 1)
    return jnp.concatenate([top, jnp.where(lanes_of(top.shape) < 64, -rolled, rolled)], axis=0)


def split3(value):
    first, second = split(value)
    rest = value - first.astype(F32) - second.astype(F32)
    return first, second, rest.astype(BF16)


def fdot(a, b):
    a1, a2, a3 = split3(a)
    b1, b2, b3 = split3(b)
    wide = jnp.concatenate([b1, b2], axis=1)
    main = jnp.dot(
        jnp.concatenate([a1, a2], axis=1),
        jnp.concatenate([wide, wide], axis=0),
        preferred_element_type=F32,
    )
    rest = jnp.dot(
        jnp.concatenate([a1, a3], axis=1),
        jnp.concatenate([b3, b1], axis=0),
        preferred_element_type=F32,
    )
    return main[:, :128] + (main[:, 128:] + rest)


def inverse_roots(tops):
    shape = tops[0].shape
    eye = jnp.where(lanes_of(shape) == rows_of(shape), 1.0, 0.0).astype(F32)
    scales = [jnp.sqrt(2.0 * jnp.sum(t * t, axis=(0, 1), keepdims=True)) for t in tops]
    upper = [t / s for t, s in zip(tops, scales)]
    lower = [1.5 * eye - 0.5 * u for u in upper]
    upper = [fdot(u, full(m)) for u, m in zip(upper, lower)]

    def step(_, carry):
        up, low = carry
        middle = [1.5 * eye - 0.5 * fdot(z, full(y)) for y, z in zip(up, low)]
        return (
            [fdot(y, full(m)) for y, m in zip(up, middle)],
            [fdot(m, full(z)) for z, m in zip(low, middle)],
        )

    upper, lower = lax.fori_loop(0, NS_STEPS - 2, step, (upper, lower))
    middle = [1.5 * eye - 0.5 * fdot(z, full(y)) for y, z in zip(upper, lower)]
    lower = [fdot(m, full(z)) for z, m in zip(lower, middle)]
    return [z * jnp.sqrt(ROWS / s) for z, s in zip(lower, scales)]


def triple(left, middle, right):
    return fdot(fdot(left, full(middle)), full(right))


def sided(value, side, wanted, axis, back):
    moved = pltpu.roll(value, back, axis)
    return jnp.where(jnp.full(value.shape, side, jnp.int32) == wanted, value, moved)


def next_gram(cross, gram_u, gram_v, side_u, side_v):
    shape = cross.shape
    lane, row = lanes_of(shape), rows_of(shape)
    upper = sided(sided(cross, side_u, 0, 0, 32), side_v, 1, 1, 32)
    corner_u = sided(sided(gram_u, side_u, 0, 0, 32), side_u, 0, 1, 96)
    corner_v = sided(sided(gram_v, side_v, 1, 0, 32), side_v, 1, 1, 32)
    flipped = jnp.concatenate([upper, upper], axis=0).T
    lower = jnp.where(lane < 64, flipped[:64], -flipped[64:])
    early = lax.rem(lane, 64) < 32
    return jnp.where(
        row < 32, jnp.where(early, corner_u, upper), jnp.where(early, lower, corner_v)
    )


def order_in(i):
    return lax.rem(2 + 3 * i + 3 * (i * (i - 1) // 2), 4)


def order_out(i):
    return lax.rem(3 * i + 3 * (i * (i - 1) // 2), 4)


def fused_kernel(
    assign, pairing, x_in, out, x_held, results, high0, low0, high1, low1, packed, from_core, relay,
    inbox, second_in, total, slices_0, from_z_0, mine_z_0, gathered_0, slices_1, from_z_1, mine_z_1,
    gathered_1, weights, near, roots_near, grams_near,
    near_in, x_sem, out_sem,
    core_send, core_recv, relay_send, relay_recv, inbox_send, inbox_recv, second_send, second_recv, zr_send,
    zr_recv, zg_send, zg_recv, wfull_send, wfull_recv, whalf_send, whalf_recv, wsecond_send,
    wsecond_recv, wcore_send, wcore_recv, near_send, near_recv,
):
    blk, row = lax.axis_index("blk"), lax.axis_index("row")
    y_lo, z, x = blk // (NZ * NX), lax.rem(blk // NX, NZ), lax.rem(blk, NX)
    y_hi, core = row // 2, lax.rem(row, 2)
    y = y_hi * 2 + y_lo
    half = UNITS // 2
    p, q = x + core * (y - x), y + core * (x - y)

    def device(yy, zz, xx, cc):
        return (lax.rem(yy, 2) * (NZ * NX) + zz * NX + xx, (yy // 2) * 2 + cc)

    def placed(pp, qq):
        return device(qq + core * (pp - qq), z, pp + core * (qq - pp), core)

    def beside(direction):
        return placed(lax.rem(p + 1 + 2 * direction, 4), q)

    def across(distance):
        return placed(p, lax.rem(q + distance, 4))

    partner = device(y, z, x, 1 - core)

    def owner(move):
        chunk = lax.rem(core * NXY + p * 4 + q + move, 2 * NXY)
        cc, pp, qq = chunk // NXY, lax.rem(chunk // 4, 4), lax.rem(chunk, 4)
        return device(qq + cc * (pp - qq), z, pp + cc * (qq - pp), cc)

    def ring_device(step):
        return device(y, lax.rem(z + step, NZ), x, core)

    def my_chunk(da, db):
        return (lax.rem(p + da, 4) * 4 + lax.rem(q + db, 4)) * CHUNK

    def other_chunk(da, db):
        return (lax.rem(q + da, 4) * 4 + lax.rem(p + db, 4)) * CHUNK

    def each(first, last, body):
        def run(step, carry):
            body(step)
            return carry

        lax.fori_loop(first, last, run, 0)

    def remote(src, dst, send, recv, to):
        return pltpu.make_async_remote_copy(
            src_ref=src, dst_ref=dst, send_sem=send, recv_sem=recv, device_id=to, device_id_type=MESH
        )

    barrier = pltpu.get_barrier_semaphore()

    def greet(to):
        pl.semaphore_signal(barrier, inc=1, device_id=to, device_id_type=MESH)

    greet(partner)
    for direction in range(2):
        greet(beside(direction))
    for distance in range(1, 4):
        greet(across(distance))
    for step in range(1, NZ):
        greet(ring_device(step))
    greet(owner(1))
    greet(owner(2 * NXY - 1))

    def x_copy(group):
        return pltpu.make_async_copy(
            x_in.at[:, pl.ds(group * 2 * STEP, 2 * STEP)], x_held.at[group], x_sem.at[group]
        )

    def load_group(group):
        x_copy(group).wait()
        flat = x_held.at[group].reshape(64 * 2 * STEP, 128)
        for k in range(STEP):
            real = flat[pl.ds(2 * k, 64, stride=2 * STEP), :]
            imag = flat[pl.ds(2 * k + 1, 64, stride=2 * STEP), :]
            flipped = jnp.concatenate([real, imag], axis=0).T
            keep((high0, low0), 4 * (group * STEP + k), 4, flipped)

    each(0, GROUPS, lambda group: x_copy(group).start())
    each(0, GROUPS, load_group)
    pl.semaphore_wait(barrier, 8 + NZ - 1)

    slices, from_z = (slices_0, slices_1), (from_z_0, from_z_1)
    mine_z, gathered = (mine_z_0, mine_z_1), (gathered_0, gathered_1)

    def reduced():
        source = (high0, low0)

        def core_copy(step):
            place = other_chunk(order_in(step // 4), order_in(lax.rem(step, 4)))
            return remote(
                packed.at[pl.ds((1 - core) * half + place, CHUNK)],
                from_core.at[pl.ds(place, CHUNK)],
                core_send.at[step], core_recv.at[step], partner,
            )

        def relay_copy(direction, slot, place):
            return remote(
                from_core.at[place + direction], relay.at[direction, slot],
                relay_send.at[direction, slot], relay_recv.at[direction, slot],
                beside(direction),
            )

        def inbox_copy(direction, slot, place):
            return remote(
                from_core.at[pl.ds(place, CHUNK)], inbox.at[direction, slot],
                inbox_send.at[direction, slot], inbox_recv.at[direction, slot],
                beside(direction),
            )

        def second_copy(ib, place):
            return remote(
                from_core.at[pl.ds(place, CHUNK)], second_in.at[ib],
                second_send.at[ib], second_recv.at[ib], across(order_in(ib)),
            )

        def gram_units(first):
            for u in range(CHUNK):
                d = first + u
                tops = []
                for h in range(2):
                    a, b = pair_places(assign, pairing, 0, d, h)
                    tops.append(gram_top(source, a, b, h == 1))
                    slots = slot_at(pairing[1, d], h)
                    around = [
                        pair_around(assign, pairing, *home_of(pairing, d, slot)) for slot in slots
                    ]
                    packed[d, pl.ds(64 + 64 * h, 64)] = cross_top(source, *around)
                packed[d, pl.ds(0, 64)] = pack(*tops)

        def compute(step):
            da, db = order_in(step // 4), order_in(lax.rem(step, 4))
            gram_units((1 - core) * half + other_chunk(da, db))
            core_copy(step).start()
            gram_units(core * half + my_chunk(da, db))

        def inbox_sum(slot):
            for direction in range(2):
                inbox_copy(direction, slot, 0).wait_recv()
            return inbox[0, slot] + inbox[1, slot]

        def ship(step):
            ia, ib = step // 4, lax.rem(step, 4)
            place = my_chunk(order_in(ia), order_in(ib))
            chunk = pl.ds(place, CHUNK)
            core_copy(step).wait_recv()
            from_core[chunk] += packed[pl.ds(core * half + place, CHUNK)]

            @pl.when(ia == 0)
            def _():
                for direction in range(2):
                    relay_copy(direction, ib, place).start()

            for direction in range(2):

                @pl.when(ia == 1 + direction)
                def _(direction=direction):
                    relay_copy(direction, ib, place).wait_recv()
                    from_core[place + direction] += relay[direction, ib]
                    inbox_copy(direction, ib, place).start()

            @pl.when(ia == 3)
            def _():
                from_core[chunk] += inbox_sum(ib)
                second_copy(ib, place).start()

        def advance(step):
            compute(step)
            ship(step - 1)

        compute(0)
        each(1, 16, advance)
        core_copy(15).wait_recv()
        place = my_chunk(0, 0)
        total[...] = (
            from_core[pl.ds(place, CHUNK)]
            + packed[pl.ds(core * half + place, CHUNK)]
            + inbox_sum(3)
        )
        for ib in range(3):
            second_copy(ib, 0).wait_recv()
            total[...] += second_in[ib]

        for part, size in enumerate(SLICES):
            for k in range(NZ):
                begin = 64 * part + k * size
                slices[part][k] = total[:, begin : begin + size, :]

        def zr_copy(part, step):
            return remote(
                slices[part].at[lax.rem(z + step, NZ)], from_z[part].at[step],
                zr_send.at[part, step], zr_recv.at[part, step], ring_device(step),
            )

        def zg_copy(part, step):
            return remote(
                mine_z[part], gathered[part].at[z], zg_send.at[part, step], zg_recv.at[part, step],
                ring_device(step),
            )

        far_first = (4, 3, 5, 2, 6, 1, 7)
        for part in range(2):
            for step in far_first:
                zr_copy(part, step).start()
        for part in range(2):
            acc = slices[part][z]
            for step in reversed(far_first):
                zr_copy(part, step).wait_recv()
                acc = acc + from_z[part][step]
            mine_z[part][...] = acc
            for step in far_first:
                zg_copy(part, step).start()
            gathered[part][z] = acc

        def units_of(part):
            for step in reversed(far_first):
                zg_copy(part, step).wait_recv()
            return [gathered[part][:, u].reshape(NZ * SLICES[part], 128) for u in range(CHUNK)]

        def drain_core(step):
            core_copy(step).wait_send()

        def drain_plane(slot):
            for direction in range(2):
                relay_copy(direction, slot, 0).wait_send()
                inbox_copy(direction, slot, 0).wait_send()

        def drain_second(ib):
            second_copy(ib, 0).wait_send()

        def drain_z(step):
            for part in range(2):
                zr_copy(part, step).wait_send()
                zg_copy(part, step).wait_send()

        def drain():
            each(0, 16, drain_core)
            each(0, 4, drain_plane)
            each(0, 3, drain_second)
            each(1, NZ, drain_z)

        return units_of, drain

    def handing(rnd, source):
        mine = core * half + my_chunk(0, 0)

        def wfull_copy(direction, slot, first):
            part = weights.at[rnd, pl.ds(first, CHUNK)]
            return remote(
                part, part, wfull_send.at[rnd, direction, slot], wfull_recv.at[rnd, direction, slot],
                beside(direction),
            )

        def whalf_copy(direction, slot, first):
            part = weights.at[rnd, first + direction]
            return remote(
                part, part, whalf_send.at[rnd, direction, slot], whalf_recv.at[rnd, direction, slot],
                beside(direction),
            )

        def wsecond_copy(ib, first):
            part = weights.at[rnd, pl.ds(first, CHUNK)]
            return remote(
                part, part, wsecond_send.at[rnd, ib], wsecond_recv.at[rnd, ib],
                across(4 - order_out(ib)),
            )

        def my_units(step):
            return core * half + my_chunk(order_out(step // 4), order_out(lax.rem(step, 4)))

        def other_units(step):
            return (1 - core) * half + other_chunk(order_out(step // 4), order_out(lax.rem(step, 4)))

        def wcore_copy(step):
            part = weights.at[rnd, pl.ds(my_units(step), CHUNK)]
            return remote(
                part, part, wcore_send.at[rnd, step], wcore_recv.at[rnd, step], partner
            )

        def out_copy(first, which):
            place = pl.ds(SLOTS * first, SLOTS * CHUNK)
            return pltpu.make_async_copy(results.at[place], out.at[place], out_sem.at[which])

        def apply_units(first, which):
            for u in range(CHUNK):
                d = first + u
                tops = unpack(weights[rnd, d])
                for h in range(2):
                    a, b = pair_places(assign, pairing, rnd, d, h)
                    new = applied(tops[h], source, a, b)
                    place = SLOTS * d + 2 * h
                    if rnd == 0:
                        keep((high1, low1), place, 2, new)
                    else:
                        results[pl.ds(place, 2)] = new.reshape(2, BLOCK, 128)
            if rnd == 1:
                out_copy(first, which).start()

        def forward(step):
            ia, ib = step // 4, lax.rem(step, 4)
            first = my_units(step)

            @pl.when(ia == 0)
            def _():
                wsecond_copy(ib, first).wait_recv()
                for direction in range(2):
                    wfull_copy(direction, ib, first).start()

            @pl.when(ia == 1)
            def _():
                for direction in range(2):
                    whole = my_units(step + 4 * direction)
                    wfull_copy(direction, ib, whole).wait_recv()
                    whalf_copy(direction, ib, whole).start()

            @pl.when(ia == 3)
            def _():
                for direction in range(2):
                    whalf_copy(direction, ib, first).wait_recv()

            wcore_copy(step).start()

        def use(step):
            apply_units(my_units(step), step)

        def use_other(step):
            wcore_copy(step).wait_recv()
            apply_units(other_units(step), 16 + step)

        def begin():
            for ib in (1, 2, 3):
                wsecond_copy(ib, mine).start()
            for direction in range(2):
                wfull_copy(direction, 0, mine).start()
            wcore_copy(0).start()

        def drain_core(step):
            wcore_copy(step).wait_send()
            if rnd == 1:
                out_copy(0, step).wait()
                out_copy(0, 16 + step).wait()

        def drain_plane(slot):
            for direction in range(2):
                wfull_copy(direction, slot, 0).wait_send()
                whalf_copy(direction, slot, 0).wait_send()

        def drain():
            each(0, 16, drain_core)
            each(0, 4, drain_plane)
            each(1, 4, lambda ib: wsecond_copy(ib, 0).wait_send())

        return begin, forward, use, use_other, drain

    units_of, drain_reduced = reduced()
    begin0, forward0, use0, use_other0, drain0 = handing(0, (high0, low0))
    begin1, forward1, use1, use_other1, drain1 = handing(1, (high1, low1))
    mine = core * half + my_chunk(0, 0)

    tops = []
    for unit in units_of(0):
        tops.extend(unpack(unit))
    roots = inverse_roots(tops)

    def packed_pair(values, u):
        return pack(values[2 * u], pltpu.roll(values[2 * u + 1], 64, 1))

    def near_copy(which):
        return remote(
            near.at[1 - which], near_in.at[which], near_send.at[which], near_recv.at[which],
            owner(1 if which == 0 else 2 * NXY - 1),
        )

    inner = [triple(w, g, w) for w, g in zip(roots, tops)]
    for u in range(CHUNK):
        near[u, 0] = packed_pair(roots, u)
        near[u, 1] = packed_pair(inner, u)
    for which in range(2):
        near_copy(which).start()
    for u in range(CHUNK):
        weights[0, mine + u] = near[u, 0]
        for h in range(2):
            roots_near[2 + 2 * u + h] = roots[2 * u + h]
            grams_near[2 + 2 * u + h] = inner[2 * u + h]
    begin0()
    use0(0)

    def take0(step):
        forward0(step)
        use0(step)
        use_other0(step - 1)

    each(1, 4, take0)
    crosses = units_of(1)
    for which in range(2):
        near_copy(which).wait_recv()
        for kind, table in enumerate((roots_near, grams_near)):
            for h, top in enumerate(unpack(near_in[which, kind])):
                table[6 * which + h] = top

    tops = []
    for u in range(CHUNK):
        for h in range(2):
            d = mine + u
            found = []
            for slot in slot_at(pairing[1, d], h):
                _, place = home_of(pairing, d, slot)
                index = 2 * (1 + u + turn_of(slot)) + place // 2
                found.append((index, lax.rem(place, 2)))
            (left, side_u), (right, side_v) = found
            cross = triple(
                roots_near[left], crosses[u][64 * h : 64 * h + 64], roots_near[right]
            )
            tops.append(next_gram(cross, grams_near[left], grams_near[right], side_u, side_v))
    roots = inverse_roots(tops)
    for u in range(CHUNK):
        weights[1, mine + u] = packed_pair(roots, u)
    begin1()
    each(4, 12, take0)
    each(1, 4, forward1)
    each(12, 16, take0)
    use_other0(15)
    use1(0)

    def take1(step):
        use1(step)
        use_other1(step - 1)

    def forward_and_take1(step):
        forward1(step)
        take1(step)

    each(1, 4, take1)
    each(4, 8, forward1)
    each(4, 8, take1)
    each(8, 16, forward_and_take1)
    use_other1(15)
    drain_reduced()
    drain0()
    drain1()
    for which in range(2):
        near_copy(which).wait_send()


def last_kernel(assign, pairing, blocks, out, places, source, sem):
    @pl.when(pl.program_id(0) == 0)
    def _():
        copy = pltpu.make_async_copy(blocks, source, sem)
        copy.start()

        def unit(d, carry):
            up = jnp.where(d == UNITS - 1, 0, d + 1)
            down = jnp.where(d == 0, UNITS - 1, d - 1)
            here, above, below = pairing[1, d], pairing[1, up], pairing[1, down]
            places[assign[SLOTS * d]] = SLOTS * d
            places[assign[SLOTS * d + 1]] = SLOTS * up + jnp.where(above == 0, 1, 2)
            places[assign[SLOTS * d + 2]] = SLOTS * down + jnp.where(
                below == 0, 2, jnp.where(below == 1, 1, 3)
            )
            places[assign[SLOTS * d + 3]] = SLOTS * d + jnp.where(here == 2, 1, 3)
            return carry

        lax.fori_loop(0, UNITS, unit, 0, unroll=16)
        copy.wait()

    flat = out.reshape(64 * 2 * STEP, 128)
    for k in range(STEP):
        ct = pl.program_id(0) * STEP + k
        parts = [source[places[4 * ct + j]] for j in range(4)]
        flipped = jnp.concatenate(parts, axis=0).T
        flat[pl.ds(2 * k, 64, stride=2 * STEP), :] = flipped[:64]
        flat[pl.ds(2 * k + 1, 64, stride=2 * STEP), :] = flipped[64:]


SMEM = pl.BlockSpec(memory_space=pltpu.SMEM)
VMEM = pl.BlockSpec(memory_space=pltpu.VMEM)
TABLE = (BLOCKS, BLOCK, 128)


def rounds(assignment, pairing, x):
    dma = pltpu.SemaphoreType.DMA
    chunks, plane, second, ring = dma((2, 16)), dma((2, 2, 4)), dma((2, 4)), dma((2, NZ))
    part = pltpu.VMEM((BLOCKS, 2, BLOCK, 128), BF16)
    return pl.pallas_call(
        fused_kernel,
        out_shape=jax.ShapeDtypeStruct(TABLE, F32),
        in_specs=[SMEM, SMEM, pl.BlockSpec(memory_space=pl.ANY)],
        out_specs=pl.BlockSpec(memory_space=pl.ANY),
        scratch_shapes=[
            pltpu.VMEM((GROUPS, 64, 2 * STEP, 128), F32),
            pltpu.VMEM(TABLE, F32),
            part, part, part, part,
            pltpu.VMEM((UNITS, DEPTH, 128), F32),
            pltpu.VMEM((UNITS // 2, DEPTH, 128), F32),
            pltpu.VMEM((2, 4, DEPTH, 128), F32),
            pltpu.VMEM((2, 4, CHUNK, DEPTH, 128), F32),
            pltpu.VMEM((3, CHUNK, DEPTH, 128), F32),
            pltpu.VMEM((CHUNK, DEPTH, 128), F32),
            pltpu.VMEM((NZ, CHUNK, SLICES[0], 128), F32),
            pltpu.VMEM((NZ, CHUNK, SLICES[0], 128), F32),
            pltpu.VMEM((CHUNK, SLICES[0], 128), F32),
            pltpu.VMEM((NZ, CHUNK, SLICES[0], 128), F32),
            pltpu.VMEM((NZ, CHUNK, SLICES[1], 128), F32),
            pltpu.VMEM((NZ, CHUNK, SLICES[1], 128), F32),
            pltpu.VMEM((CHUNK, SLICES[1], 128), F32),
            pltpu.VMEM((NZ, CHUNK, SLICES[1], 128), F32),
            pltpu.VMEM((2, UNITS, 64, 128), F32),
            pltpu.VMEM((2, 2, 64, 128), F32),
            pltpu.VMEM((8, 64, 128), F32),
            pltpu.VMEM((8, 64, 128), F32),
            pltpu.VMEM((2, 2, 64, 128), F32),
            dma((GROUPS,)), dma((32,)),
            dma((16,)), dma((16,)), dma((2, 4)), dma((2, 4)), dma((2, 4)), dma((2, 4)),
            dma((4,)), dma((4,)), ring, ring, ring, ring,
            plane, plane, plane, plane, second, second, chunks, chunks, dma((2,)), dma((2,)),
        ],
        compiler_params=PARAMS(collective_id=0, has_side_effects=True),
        name="rounds",
    )(assignment, pairing, x)


def unturned(assignment, pairing, source):
    shape = (64, BLOCKS // 2, 128)
    return pl.pallas_call(
        last_kernel,
        out_shape=jax.ShapeDtypeStruct(shape, F32),
        grid=(BLOCKS // 4 // STEP,),
        in_specs=[SMEM, SMEM, pl.BlockSpec(memory_space=pl.ANY)],
        out_specs=pl.BlockSpec((64, 2 * STEP, 128), lambda i: (0, i, 0)),
        scratch_shapes=[
            pltpu.SMEM((BLOCKS,), jnp.int32), pltpu.VMEM(TABLE, F32), pltpu.SemaphoreType.DMA
        ],
        compiler_params=PARAMS(),
        name="unturn",
    )(assignment, pairing, source)


def on_device(transmission, assignment, pairing):
    rows, _, cols = transmission.shape
    x = transmission.reshape(rows, 2, cols // 128, 128).transpose(0, 2, 1, 3).reshape(rows, -1, 128)
    turned_blocks = rounds(assignment, pairing, x)
    out = unturned(assignment, pairing, turned_blocks)
    out = out.reshape(rows, cols // 128, 2, 128).transpose(0, 2, 1, 3)
    return out.reshape(rows, 2, cols)


def solution(mesh):
    placed = (P(("blk", "row"), None, None), P(), P())
    return jax.shard_map(
        on_device,
        mesh=mesh,
        in_specs=placed,
        out_specs=P(("blk", "row"), None, None),
        check_vma=False,
    )
```
